32 devices in a mesh: row: 4 (over z), col: 8 (over y, x, core).
Axes of the slice: x: 2, y: 2, z: 4, core: 2. Of those that a mesh axis runs over, the one named last changes fastest.
Arguments:
- initial_voltage: float32 [4, 16, 128, 128], P('row', 'col'), may hold values from -6 to 6
- inject: float32 [4, 16, 128, 128], P('row', 'col'), may hold values from -6 to 6
- conduct: float32 [4, 16, 128, 128], P('row', 'col'), as said below
- capacitance: float32 [4, 16, 128], P('row', 'col'), may hold values from 1 to 4
- track_gain: float32 [4, 16, 2, 32], P('row', 'col'), may hold values from 0.3 to 3
- driver_tile: int32 [4, 8, 64], P('row', 'col'), may hold values from 0 to 1
- sink_net: int32 [4, 8, 8, 8], P('row', 'col'), may hold values from 0 to 63
- sink_count: int32 [4, 8, 8], P('row', 'col'), may hold values from 0 to 8, as said below
- sink_tile: int32 [4, 8, 8, 8], P('row', 'col'), may hold values from 0 to 1
- sink_node: int32 [4, 8, 8, 8], P('row', 'col'), may hold values from 0 to 127
- sink_gain: float32 [4, 8, 8, 8], P('row', 'col'), may hold values from 0.5 to 2
Outputs:
- voltage: float32 [4, 16, 128, 128], P('row', 'col')
The draws below stay inside these ranges and needn't reach their ends.
Inputs may be any that keep to these rules, and one draw needn't show every extreme that they name: Slots k >= sink_count[d, s] are ignored; some receiving device takes all 8 slots from some source device in every draw. `conduct`: each tile's block is symmetric with non-positive entries off the diagonal and rows summing to zero.
All inputs are finite; a program needn't handle non-finite values.
Results may differ from the reference program's by a relative error of at most 0.0001.
Values sent between devices are 32-bit elements; how exact they have to be, the bound alone decides.
No kernel may reach another device: no remote copies, remote signals or barrier semaphores. Data moves between devices by JAX's collectives and lax.ppermute only.
A program may use at most 64 MiB of HBM per device.

```python
import math
import jax
import jax.numpy as jnp
from jax import lax

NODE = 128
EDGE = 32
PAT = 128
TR = 1
TC = 2
NETS = 64
SLOT = 8
ITERS = 3
STEPS = 1
TILES = 2
GR = 4
GC = 16
N_ROW = 4
N_COL = 8


def draw_conduct(key, part):
    key_base = jax.random.fold_in(key, 0)
    uniform_draw = jax.random.uniform(key_base, (GR, GC, NODE, NODE), jnp.float32)
    weights = 0.6 * uniform_draw ** 16
    weights = 0.5 * (weights + jnp.swapaxes(weights, -1, -2))
    identity = jnp.eye(NODE, dtype=jnp.float32)
    weights = weights * (1.0 - identity)
    degree = jnp.sum(weights, axis=-1)
    return degree[..., :, None] * identity - weights


def draw_sink_count(key, part):
    key_count, key_spot = jax.random.split(key)
    counts = jax.random.randint(key_count, (N_ROW, N_COL, N_COL), 0, SLOT + 1)
    position = jax.random.randint(key_spot, (), 0, N_ROW * N_COL * N_COL)
    flat_counts = counts.reshape(-1).at[position].set(SLOT)
    return flat_counts.reshape((N_ROW, N_COL, N_COL)).astype(jnp.int32)


def plant(entries, key, low, high):
    dims = entries.shape
    index_at = [jax.random.randint(jax.random.fold_in(key, axis), (), 0, dims[axis]) for axis in range(len(dims))]
    entries = entries.at[tuple(index_at)].set(low)
    longest = dims.index(max(dims))
    index_at[longest] = (index_at[longest] + 1) % dims[longest]
    return entries.at[tuple(index_at)].set(high)


def block_levels(rng, dims, cuts, smallest, high):
    level = 1.0
    for dim, shards_of in cuts:
        heights = jax.random.uniform(jax.random.fold_in(jax.random.fold_in(rng, 6), dim), (shards_of,), jnp.float32, smallest / len(cuts), high / len(cuts))
        level = level * jnp.repeat(jnp.exp(heights), dims[dim] // shards_of).reshape((-1,) + (1,) * (len(dims) - 1 - dim))
    return level


def centred(stream_key, shape, scale, limit, cuts=(), kind=jnp.bfloat16):
    factor_of = block_levels(stream_key, shape, cuts, -0.22, 0.18) if cuts else 1.0
    entries = jax.random.normal(stream_key, shape, jnp.float32) * scale * factor_of
    return jnp.minimum(jnp.maximum(entries, -limit), limit).astype(kind)


def setup_inputs(seed: int = 0) -> dict:
    keys = jax.random.split(jax.random.key(seed), 12)
    initial_voltage = centred(keys[0], (GR, GC, NODE, PAT), 1.0, 6.0, ((0, 4), (1, 8)), jnp.float32)
    inject = centred(keys[1], (GR, GC, NODE, PAT), 1.0, 6.0, ((0, 4), (1, 8)), jnp.float32)
    conduct = draw_conduct(jax.random.fold_in(keys[11], 71), 0)
    capacitance = jnp.clip(jnp.exp(math.log(4.0) - 1.3862944 * jax.random.uniform(keys[3], (GR, GC, NODE), jnp.float32) ** block_levels(keys[3], (GR, GC, NODE), ((0, 4), (1, 8)), -0.2, 0.2)), 1.0, 4.0)
    track_gain = jnp.clip(jnp.exp(math.log(3.0) - 2.3025851 * jax.random.uniform(keys[4], (GR, GC, 2, EDGE), jnp.float32) ** block_levels(keys[4], (GR, GC, 2, EDGE), ((0, 4), (1, 8)), -0.2, 0.2)), 0.3, 3.0)
    driver_tile = plant(jax.random.randint(keys[5], (N_ROW, N_COL, NETS), 0, TILES), jax.random.fold_in(keys[5], 1), 0, TILES - 1).astype(jnp.int32)
    sink_net = plant(jax.random.randint(keys[6], (N_ROW, N_COL, N_COL, SLOT), 0, NETS), jax.random.fold_in(keys[6], 1), 0, NETS - 1).astype(jnp.int32)
    sink_count = draw_sink_count(jax.random.fold_in(keys[11], 71), 0)
    sink_tile = plant(jax.random.randint(keys[8], (N_ROW, N_COL, N_COL, SLOT), 0, TILES), jax.random.fold_in(keys[8], 1), 0, TILES - 1).astype(jnp.int32)
    sink_node = plant(jax.random.randint(keys[9], (N_ROW, N_COL, N_COL, SLOT), 0, NODE), jax.random.fold_in(keys[9], 1), 0, NODE - 1).astype(jnp.int32)
    sink_gain = jnp.clip(jnp.exp(math.log(2.0) - 1.3862944 * jax.random.uniform(keys[10], (N_ROW, N_COL, N_COL, SLOT), jnp.float32) ** block_levels(keys[10], (N_ROW, N_COL, N_COL, SLOT), ((0, 4), (1, 8)), -0.2, 0.2)), 0.5, 2.0)
    return dict(initial_voltage=initial_voltage, inject=inject, conduct=conduct, capacitance=capacitance, track_gain=track_gain, driver_tile=driver_tile, sink_net=sink_net, sink_count=sink_count, sink_tile=sink_tile, sink_node=sink_node, sink_gain=sink_gain)


PRECISE = lax.Precision.HIGHEST

def tile_inverse(conduct, capacitance):
    node_count = conduct.shape[-1]
    identity = jnp.eye(node_count, dtype=jnp.float32)
    whole_block = conduct + capacitance[..., None] * identity
    flat_blocks = whole_block.reshape((-1, node_count, node_count))
    factors = jnp.linalg.cholesky(flat_blocks)
    inverse = jax.vmap(lambda factor: jax.scipy.linalg.cho_solve((factor, True), identity))(factors)
    return inverse.reshape(whole_block.shape)

def combine_tracks(inner_part, rim_cells, padded, track_pad):
    edge_count = rim_cells.shape[2]
    east_gain = track_pad[1:-1, 1:-1, 0][..., None]
    west_gain = track_pad[1:-1, :-2, 0][..., None]
    south_gain = track_pad[1:-1, 1:-1, 1][..., None]
    north_gain = track_pad[:-2, 1:-1, 1][..., None]
    track_flow = east_gain * (rim_cells - padded[1:-1, 2:]) + west_gain * (rim_cells - padded[1:-1, :-2])
    track_flow = track_flow + south_gain * (rim_cells - padded[2:, 1:-1]) + north_gain * (rim_cells - padded[:-2, 1:-1])
    return jnp.concatenate([inner_part[:, :, :edge_count] + track_flow, inner_part[:, :, edge_count:]], axis=2)

def apply_grid(voltage, conduct, capacitance, track_pad):
    edge_count = track_pad.shape[-1]
    inner_part = jnp.einsum('rcij,rcjp->rcip', conduct, voltage, precision=PRECISE) + capacitance[..., None] * voltage
    rim_cells = voltage[:, :, :edge_count, :]
    padded = jnp.pad(rim_cells, ((1, 1), (1, 1), (0, 0), (0, 0)))
    return combine_tracks(inner_part, rim_cells, padded, track_pad)

def precondition(inverse, residual):
    return jnp.einsum('rcij,rcjp->rcip', inverse, residual, precision=PRECISE)

def inner_sum(left_vec, right_vec):
    return jnp.sum(left_vec * right_vec, axis=(0, 1, 2))

def by_device(array):
    shaped = array.reshape((N_ROW, TR, N_COL, TC) + array.shape[2:])
    moved = jnp.moveaxis(shaped, 2, 1)
    return moved.reshape((N_ROW, N_COL, TR * TC) + array.shape[2:])

def from_device(array):
    shaped = array.reshape((N_ROW, N_COL, TR, TC) + array.shape[3:])
    moved = jnp.moveaxis(shaped, 1, 2)
    return moved.reshape((N_ROW * TR, N_COL * TC) + array.shape[3:])

def sink_injection(voltage, driver_tile, sink_net, sink_count, sink_tile, sink_node, sink_gain):
    node_count = voltage.shape[2]
    pattern_count = voltage.shape[3]
    device_volts = by_device(voltage).reshape((N_ROW, N_COL, TR * TC * node_count, pattern_count))
    net_count = driver_tile.shape[-1]
    driver_rows = driver_tile * node_count + jnp.arange(net_count, dtype=jnp.int32) % node_count
    driver = jnp.take_along_axis(device_volts, driver_rows[..., None], axis=2)
    row_ids = jnp.arange(N_ROW, dtype=jnp.int32)[:, None, None, None]
    col_ids = jnp.arange(N_COL, dtype=jnp.int32)[None, :, None, None]
    source_ids = jnp.arange(N_COL, dtype=jnp.int32)[None, None, :, None]
    values = driver[row_ids, source_ids, sink_net]
    slot_ids = jnp.arange(sink_net.shape[-1], dtype=jnp.int32)
    weight = jnp.where(slot_ids < sink_count[..., None], sink_gain, jnp.float32(0.0))
    target = sink_tile * node_count + sink_node
    injected = jnp.zeros(device_volts.shape, jnp.float32)
    injected = injected.at[row_ids, col_ids, target].add(values * weight[..., None])
    return from_device(injected.reshape((N_ROW, N_COL, TR * TC, node_count, pattern_count)))

def solve_step(right_side, initial, conduct, capacitance, track_pad, inverse):
    solution = initial
    residual = right_side - apply_grid(initial, conduct, capacitance, track_pad)
    precond = precondition(inverse, residual)
    direction = precond
    rz_now = inner_sum(residual, precond)
    for sweep_idx in range(ITERS):
        applied = apply_grid(direction, conduct, capacitance, track_pad)
        step_size = rz_now / inner_sum(direction, applied)
        solution = solution + step_size * direction
        residual = residual - step_size * applied
        precond = precondition(inverse, residual)
        rz_fresh = inner_sum(residual, precond)
        direction = precond + rz_fresh / rz_now * direction
        rz_now = rz_fresh
    return solution

def reference(initial_voltage, inject, conduct, capacitance, track_gain, driver_tile, sink_net, sink_count, sink_tile, sink_node, sink_gain):
    inverse = tile_inverse(conduct, capacitance)
    track_pad = jnp.pad(track_gain, ((1, 1), (1, 1), (0, 0), (0, 0)))
    voltage = initial_voltage
    for time_step in range(STEPS):
        injected = sink_injection(voltage, driver_tile, sink_net, sink_count, sink_tile, sink_node, sink_gain)
        right_side = capacitance[..., None] * voltage + inject + injected
        voltage = solve_step(right_side, voltage, conduct, capacitance, track_pad, inverse)
    return voltage
```

```python
import functools

import jax
import jax.numpy as jnp
from jax import lax
from jax.experimental import pallas as pl
from jax.experimental.pallas import tpu as pltpu
from jax.sharding import PartitionSpec as P

PRECISE = lax.Precision.HIGHEST
DOUBLINGS = 5
SMALL = 2.0**-13


def tile_kernel(conduct_ref, cap_ref, volt_ref, inject_ref, inverse_ref, rest_ref, sum_ref, power_ref):
    tiles, nodes = conduct_ref.shape[0], conduct_ref.shape[1]
    dot = functools.partial(
        jnp.dot, precision=PRECISE, preferred_element_type=jnp.float32
    )
    row = lax.broadcasted_iota(jnp.int32, (nodes, nodes), 0)
    col = lax.broadcasted_iota(jnp.int32, (nodes, nodes), 1)
    eye = jnp.where(row == col, 1.0, 0.0).astype(jnp.float32)
    sums, powers, scales = [], [], []
    for t in range(tiles):
        conduct = conduct_ref[t]
        diagonal = (conduct + cap_ref[t : t + 1, :]) * eye
        down = jnp.sum(diagonal, axis=1, keepdims=True)
        across = jnp.sum(diagonal, axis=0, keepdims=True)
        power = (conduct * eye - conduct) / down
        sums.append(eye + power)
        powers.append(dot(power, power))
        scales.append(1.0 / across)
        rest_ref[t] = inject_ref[t] - dot(conduct, volt_ref[t])

    def step(sums, powers):
        out_sums, out_powers, largest = [], [], jnp.float32(0.0)
        for total, power in zip(sums, powers):
            both = dot(jnp.concatenate([total, power], axis=0), power)
            out_sums.append(total + both[:nodes])
            out_powers.append(both[nodes:])
            largest = jnp.maximum(largest, jnp.max(jnp.sum(power, axis=1)))
        return out_sums, out_powers, largest

    for _ in range(DOUBLINGS):
        sums, powers, largest = step(sums, powers)
    for t in range(tiles):
        sum_ref[t], power_ref[t] = sums[t], powers[t]

    def again(carry):
        sums, powers, largest = step(
            [sum_ref[t] for t in range(tiles)], [power_ref[t] for t in range(tiles)]
        )
        for t in range(tiles):
            sum_ref[t], power_ref[t] = sums[t], powers[t]
        return largest, carry[1] + 1

    lax.while_loop(
        lambda carry: (carry[0] > SMALL) & (carry[1] < 40), again, (largest, jnp.int32(0))
    )
    for t in range(tiles):
        inverse_ref[t] = sum_ref[t] * scales[t]


def tile_inverse(conduct, capacitance, voltage, inject):
    block = jax.ShapeDtypeStruct(conduct.shape, jnp.float32)
    vmem = pl.BlockSpec(memory_space=pltpu.VMEM)
    return pl.pallas_call(
        tile_kernel,
        out_shape=(block, block),
        in_specs=[vmem] * 4,
        out_specs=(vmem, vmem),
        scratch_shapes=[pltpu.VMEM(conduct.shape, jnp.float32)] * 2,
    )(conduct, capacitance, voltage, inject)


def other(block, axis, count, distance):
    return lax.ppermute(block, axis, [(i, i ^ distance) for i in range(count)])


def xor_gather(block, axis, count):
    blocks, held = [block], 1
    while held < count:
        whole = jnp.concatenate(blocks, axis=0)
        reach = 2 if (count // held).bit_length() % 2 == 0 else 4
        blocks = [whole] + [other(whole, axis, count, held * k) for k in range(1, reach)]
        held *= reach
    return jnp.concatenate(blocks, axis=0)


def xor_sum(block, axis, count):
    held = 1
    while held < count:
        reach = 2 if (count // held).bit_length() % 2 == 0 else 4
        block = sum([other(block, axis, count, held * k) for k in range(1, reach)], block)
        held *= reach
    return block


def outer(block, axis, count):
    pairs = [(i, (i + 1) % count if i % 2 else (i - 1) % count) for i in range(count)]
    return lax.ppermute(block, axis, pairs)


def south_flow(rim, gain, not_last):
    below = jnp.roll(rim, -1, axis=0) * not_last
    return gain * (rim - below), rim - below


def net_flow(east, south, not_first):
    return east[:, 1:] - east[:, :-1] + south - jnp.roll(south, 1, axis=0) * not_first


def local(
    initial_voltage,
    inject,
    conduct,
    capacitance,
    track_gain,
    driver_tile,
    sink_net,
    sink_count,
    sink_tile,
    sink_node,
    sink_gain,
):
    rows, cols = lax.axis_size("row"), lax.axis_size("col")
    my_row, my_col = lax.axis_index("row"), lax.axis_index("col")
    odd = my_col % 2 == 1
    has_west = (my_col > 0).astype(jnp.float32)
    has_east = (my_col < cols - 1).astype(jnp.float32)
    has_far = (my_col < cols - 2).astype(jnp.float32)
    tiles, nodes, patterns = initial_voltage.shape[1:]
    edge = track_gain.shape[-1]
    nets = driver_tile.shape[-1]
    voltage = initial_voltage[0]
    rims = voltage[:, :edge]
    east_gain, south_gain = track_gain[0, :, 0, :, None], track_gain[0, :, 1, :, None]

    picked = driver_tile.reshape((nets, 1))
    node_of = voltage[:, :nets] if nets <= nodes else jnp.tile(voltage, (1, -(-nets // nodes), 1))[:, :nets]
    drivers = sum(jnp.where(picked == t, node_of[t], 0.0) for t in range(tiles))
    gathered = xor_gather(drivers, "col", cols)

    wide = jnp.broadcast_to(east_gain[-1], (edge, patterns))
    inner0 = other(jnp.concatenate([jnp.where(odd, rims[0], rims[1]), wide]), "col", cols, 1)
    outer0 = outer(jnp.concatenate([jnp.where(odd, rims[1], rims[0]), wide]), "col", cols)
    west0 = jnp.where(odd, inner0, outer0) * has_west
    east0 = jnp.where(odd, outer0, inner0) * has_east

    inverse, rest = tile_inverse(conduct[0], capacitance[0], voltage, inject[0])

    source = jnp.arange(cols, dtype=jnp.int32)[:, None] ^ my_col
    slots = sink_net.shape[-1]
    place = (source * nets + sink_net[0, 0]).reshape(-1)
    live = jnp.arange(slots, dtype=jnp.int32)[None] < sink_count[0, 0][:, None]
    weight = jnp.where(live, sink_gain[0, 0], 0.0).reshape((-1, 1))
    target = (sink_tile * nodes + sink_node).reshape(-1)
    take = (place[:, None] == jnp.arange(cols * nets, dtype=jnp.int32)).astype(jnp.float32)
    put = (target[:, None] == jnp.arange(tiles * nodes, dtype=jnp.int32)).astype(jnp.float32)
    take, put = lax.optimization_barrier((take, put * weight))
    spread_drivers = lax.dot_general(put, take, (((0,), (0,)), ((), ())), precision=PRECISE)
    injected = jnp.dot(spread_drivers, gathered, precision=PRECISE).reshape(voltage.shape)

    flow0 = jnp.stack(
        [
            west0[edge:] * (west0[:edge] - rims[0]),
            east_gain[0] * (rims[0] - rims[1]),
            east_gain[1] * (rims[1] - east0[:edge]),
        ]
    )
    residual = rest + injected
    residual = jnp.concatenate(
        [residual[:, :edge] - (flow0[1:] - flow0[:-1]), residual[:, edge:]], axis=1
    )
    precond = jnp.einsum("cij,cjp->cip", inverse, residual, precision=PRECISE)
    first = jnp.sum(precond * residual, axis=(0, 1))

    core = inverse[:, :edge, :edge]
    extras = jnp.concatenate(
        [core[0], core[1], east_gain[0], east_gain[1], south_gain[0], south_gain[1]], axis=1
    )
    extras = jnp.pad(extras, ((0, 0), (0, patterns - extras.shape[1])))
    message = jnp.concatenate(
        [
            precond[:, :edge].reshape((-1, patterns)),
            rims.reshape((-1, patterns)),
            extras,
            jnp.pad(first[None], ((0, 7), (0, 0))),
        ]
    )
    column = jnp.stack(
        [message]
        + [
            lax.ppermute(message, "row", [((i + k) % rows, i) for i in range(rows)])
            for k in range(1, rows)
        ]
    )
    true_row = (my_row + jnp.arange(rows, dtype=jnp.int32)) % rows
    not_first = (true_row > 0).astype(jnp.float32)[:, None, None, None]
    not_last = (true_row < rows - 1).astype(jnp.float32)[:, None, None, None]
    span = tiles * edge
    raw = column[:, :span].reshape((rows, tiles, edge, patterns))
    start = column[:, span : 2 * span].reshape((rows, tiles, edge, patterns))
    table = column[:, 2 * span : 2 * span + edge]
    first = jnp.sum(column[:, 2 * span + edge], axis=0)

    def unpack(table):
        cores = jnp.stack([table[:, :, :edge], table[:, :, edge : 2 * edge]], axis=1)
        gains = [table[:, :, 2 * edge + k : 2 * edge + k + 1] for k in range(4)]
        return cores, jnp.stack(gains[:2], axis=1), jnp.stack(gains[2:], axis=1)

    def spread(cores, flow):
        return jnp.einsum("rcij,rcjp->rcip", cores, flow, precision=PRECISE)

    cores, easts, souths = unpack(table)
    south0, _ = south_flow(start, souths, not_last)
    vertical = south0 - jnp.roll(south0, 1, axis=0) * not_first
    u0 = raw - spread(cores, vertical)
    first = first - jnp.sum(vertical * (raw + u0), axis=(0, 1, 2))
    precond = precond - jnp.einsum(
        "cij,cjp->cip", inverse[:, :, :edge], vertical[0], precision=PRECISE
    )

    message = jnp.concatenate([u0.reshape((rows, span, patterns)), table], axis=1)
    inner = other(message, "col", cols, 1)
    beyond = outer(message, "col", cols)
    far = lax.ppermute(u0[:, :1], "col", [((i + 2) % cols, i) for i in range(cols)]) * has_far
    west = jnp.where(odd, inner, beyond) * has_west
    east = jnp.where(odd, beyond, inner) * has_east

    def parts(block):
        return (block[:, :span].reshape((rows, tiles, edge, patterns)),) + unpack(block[:, span:])

    west_u, west_cores, west_easts, west_souths = parts(west)
    east_u, east_cores, east_easts, east_souths = parts(east)
    u0 = jnp.concatenate([west_u, u0, east_u, far], axis=1)
    cores = jnp.concatenate([west_cores[:, 1:], cores, east_cores], axis=1)
    easts = jnp.concatenate([west_easts, easts, east_easts], axis=1)
    souths = jnp.concatenate([west_souths[:, 1:], souths, east_souths], axis=1)

    south, _ = south_flow(u0[:, 1:-1], souths, not_last)
    t0 = net_flow(easts * (u0[:, :-1] - u0[:, 1:]), south, not_first)
    u1 = spread(cores, t0)
    south, _ = south_flow(u1[:, 1:-1], souths[:, 1:-1], not_last)
    t1 = net_flow(easts[:, 1:-1] * (u1[:, :-1] - u1[:, 1:]), south, not_first)
    u2 = spread(cores[:, 1:-1], t1)
    south, drop = south_flow(u2[:, :-1], souths[:, 1:3], not_last)
    ahead = u2[:, :-1] - u2[:, 1:]

    def total(left, right):
        return jnp.sum(left * right, axis=(0, 1, 2))

    own_t0, own_u1, own_t1 = t0[:, 1:3], u1[:, 1:3], t1[:, :2]
    moments = jnp.stack(
        [
            first,
            total(u0[:, 2:4], own_t0),
            total(own_u1, own_t0),
            total(own_u1, own_t1),
            total(u2[:, :2], own_t1),
            total(south, drop) + total(easts[:, 2:4] * ahead, ahead),
            jnp.zeros_like(first),
            jnp.zeros_like(first),
        ]
    )
    m = xor_sum(moments, "col", cols)

    a00, a01, a02 = m[0] + m[1], m[1] + m[2], m[2] + m[3]
    a12, a22 = m[3] + m[4], m[4] + m[5]
    l1, l2 = a01 / a00, a02 / a00
    d1 = a02 - l1 * a01
    e12 = a12 - l2 * a01
    l12 = e12 / d1
    d2 = a22 - l2 * a02 - l12 * e12
    y1 = m[1] - l1 * m[0]
    y2 = m[2] - l2 * m[0] - l12 * y1
    c2 = y2 / d2
    c1 = y1 / d1 - l12 * c2
    c0 = m[0] / a00 - l1 * c1 - l2 * c2
    mixed = c1 * t0[0, 1:3] + c2 * t1[0, :2]
    update = jnp.einsum("cij,cjp->cip", inverse[:, :, :edge], mixed, precision=PRECISE)
    return (voltage + c0 * precond + update)[None]


def solution(mesh):
    whole = P("row", "col", None, None)
    third = P("row", "col", None)
    placed = (whole, whole, whole, third, whole, third, whole, third, whole, whole, whole)
    return jax.shard_map(local, mesh=mesh, in_specs=placed, out_specs=whole, check_vma=False)
```

```python
import functools

import jax
import jax.numpy as jnp
from jax import lax
from jax.experimental import pallas as pl
from jax.experimental.pallas import tpu as pltpu
from jax.sharding import PartitionSpec as P

PRECISE = lax.Precision.HIGHEST
DOUBLINGS = 5
SMALL = 2.0**-13


def tile_kernel(conduct_ref, cap_ref, volt_ref, inject_ref, inverse_ref, rest_ref, sum_ref, power_ref):
    tiles, nodes = conduct_ref.shape[0], conduct_ref.shape[1]
    dot = functools.partial(
        jnp.dot, precision=PRECISE, preferred_element_type=jnp.float32
    )
    row = lax.broadcasted_iota(jnp.int32, (nodes, nodes), 0)
    col = lax.broadcasted_iota(jnp.int32, (nodes, nodes), 1)
    eye = jnp.where(row == col, 1.0, 0.0).astype(jnp.float32)
    sums, powers, scales = [], [], []
    for t in range(tiles):
        conduct = conduct_ref[t]
        diagonal = (conduct + cap_ref[t : t + 1, :]) * eye
        down = jnp.sum(diagonal, axis=1, keepdims=True)
        across = jnp.sum(diagonal, axis=0, keepdims=True)
        power = (conduct * eye - conduct) / down
        sums.append(eye + power)
        powers.append(dot(power, power))
        scales.append(1.0 / across)
        rest_ref[t] = inject_ref[t] - dot(conduct, volt_ref[t])

    def step(sums, powers):
        out_sums, out_powers, largest = [], [], jnp.float32(0.0)
        for total, power in zip(sums, powers):
            both = dot(jnp.concatenate([total, power], axis=0), power)
            out_sums.append(total + both[:nodes])
            out_powers.append(both[nodes:])
            largest = jnp.maximum(largest, jnp.max(jnp.sum(power, axis=1)))
        return out_sums, out_powers, largest

    for _ in range(DOUBLINGS):
        sums, powers, largest = step(sums, powers)
    for t in range(tiles):
        sum_ref[t], power_ref[t] = sums[t], powers[t]

    def again(carry):
        sums, powers, largest = step(
            [sum_ref[t] for t in range(tiles)], [power_ref[t] for t in range(tiles)]
        )
        for t in range(tiles):
            sum_ref[t], power_ref[t] = sums[t], powers[t]
        return largest, carry[1] + 1

    lax.while_loop(
        lambda carry: (carry[0] > SMALL) & (carry[1] < 40), again, (largest, jnp.int32(0))
    )
    for t in range(tiles):
        inverse_ref[t] = sum_ref[t] * scales[t]


def tile_inverse(conduct, capacitance, voltage, inject):
    block = jax.ShapeDtypeStruct(conduct.shape, jnp.float32)
    vmem = pl.BlockSpec(memory_space=pltpu.VMEM)
    return pl.pallas_call(
        tile_kernel,
        out_shape=(block, block),
        in_specs=[vmem] * 4,
        out_specs=(vmem, vmem),
        scratch_shapes=[pltpu.VMEM(conduct.shape, jnp.float32)] * 2,
    )(conduct, capacitance, voltage, inject)


def other(block, axis, count, distance):
    return lax.ppermute(block, axis, [(i, i ^ distance) for i in range(count)])


def xor_gather(block, axis, count, held):
    blocks = [block]
    while held < count:
        whole = jnp.concatenate(blocks, axis=0)
        reach = 2 if (count // held).bit_length() % 2 == 0 else 4
        blocks = [whole] + [other(whole, axis, count, held * k) for k in range(1, reach)]
        held *= reach
    return jnp.concatenate(blocks, axis=0)


def xor_sum(block, axis, count):
    held = 1
    while held < count:
        reach = 2 if (count // held).bit_length() % 2 == 0 else 4
        block = sum([other(block, axis, count, held * k) for k in range(1, reach)], block)
        held *= reach
    return block


def outer(block, axis, count):
    pairs = [(i, (i + 1) % count if i % 2 else (i - 1) % count) for i in range(count)]
    return lax.ppermute(block, axis, pairs)


def local(
    initial_voltage,
    inject,
    conduct,
    capacitance,
    track_gain,
    driver_tile,
    sink_net,
    sink_count,
    sink_tile,
    sink_node,
    sink_gain,
):
    rows, cols = lax.axis_size("row"), lax.axis_size("col")
    my_row, my_col = lax.axis_index("row"), lax.axis_index("col")
    odd = my_col % 2 == 1
    has_west = (my_col > 0).astype(jnp.float32)
    has_east = (my_col < cols - 1).astype(jnp.float32)
    has_far = (my_col < cols - 2).astype(jnp.float32)
    tiles, nodes, patterns = initial_voltage.shape[1:]
    edge = track_gain.shape[-1]
    nets = driver_tile.shape[-1]
    voltage = initial_voltage[0]

    picked = driver_tile.reshape((nets, 1))
    node_of = voltage[:, :nets] if nets <= nodes else jnp.tile(voltage, (1, -(-nets // nodes), 1))[:, :nets]
    drivers = sum(jnp.where(picked == t, node_of[t], 0.0) for t in range(tiles))
    paired = jnp.concatenate([drivers, other(drivers, "col", cols, 1)], axis=0)
    (
        paired,
        voltage,
        inject,
        conduct,
        capacitance,
        track_gain,
        sink_net,
        sink_count,
        sink_tile,
        sink_node,
        sink_gain,
    ) = lax.optimization_barrier(
        (
            paired,
            voltage,
            inject,
            conduct,
            capacitance,
            track_gain,
            sink_net,
            sink_count,
            sink_tile,
            sink_node,
            sink_gain,
        )
    )
    rims = voltage[:, :edge]
    east_gain, south_gain = track_gain[0, :, 0, :, None], track_gain[0, :, 1, :, None]
    gathered = xor_gather(paired, "col", cols, 2)

    wide = jnp.broadcast_to(east_gain[-1], (edge, patterns))
    inner0 = other(jnp.concatenate([jnp.where(odd, rims[0], rims[1]), wide]), "col", cols, 1)
    outer0 = outer(jnp.concatenate([jnp.where(odd, rims[1], rims[0]), wide]), "col", cols)
    west0 = jnp.where(odd, inner0, outer0) * has_west
    east0 = jnp.where(odd, outer0, inner0) * has_east

    inverse, rest = tile_inverse(conduct[0], capacitance[0], voltage, inject[0])

    source = jnp.arange(cols, dtype=jnp.int32)[:, None] ^ my_col
    slots = sink_net.shape[-1]
    place = (source * nets + sink_net[0, 0]).reshape(-1)
    live = jnp.arange(slots, dtype=jnp.int32)[None] < sink_count[0, 0][:, None]
    weight = jnp.where(live, sink_gain[0, 0], 0.0).reshape((-1, 1))
    target = (sink_tile * nodes + sink_node).reshape(-1)
    take = (place[:, None] == jnp.arange(cols * nets, dtype=jnp.int32)).astype(jnp.float32)
    put = (target[:, None] == jnp.arange(tiles * nodes, dtype=jnp.int32)).astype(jnp.float32)
    take, put = lax.optimization_barrier((take, put * weight))
    spread_drivers = lax.dot_general(put, take, (((0,), (0,)), ((), ())), precision=PRECISE)
    injected = jnp.dot(spread_drivers, gathered, precision=PRECISE).reshape(voltage.shape)

    flow0 = jnp.stack(
        [
            west0[edge:] * (west0[:edge] - rims[0]),
            east_gain[0] * (rims[0] - rims[1]),
            east_gain[1] * (rims[1] - east0[:edge]),
        ]
    )
    residual = rest + injected
    residual = jnp.concatenate(
        [residual[:, :edge] - (flow0[1:] - flow0[:-1]), residual[:, edge:]], axis=1
    )
    precond = jnp.einsum("cij,cjp->cip", inverse, residual, precision=PRECISE)
    first = jnp.sum(precond * residual, axis=(0, 1))

    core = inverse[:, :edge, :edge]
    extras = jnp.concatenate(
        [core[0], core[1], east_gain[0], east_gain[1], south_gain[0], south_gain[1]], axis=1
    )
    extras = jnp.pad(extras, ((0, 0), (0, patterns - extras.shape[1])))
    message = jnp.concatenate(
        [
            precond[:, :edge].reshape((-1, patterns)),
            rims.reshape((-1, patterns)),
            extras,
            jnp.pad(first[None], ((0, 7), (0, 0))),
        ]
    )
    column = [message] + [
        lax.ppermute(message, "row", [((i + k) % rows, i) for i in range(rows)])
        for k in range(1, rows)
    ]
    true_row = [(my_row + k) % rows for k in range(rows)]
    not_first = [(r > 0).astype(jnp.float32) for r in true_row]
    not_last = [(r < rows - 1).astype(jnp.float32) for r in true_row]
    span = tiles * edge

    def unpack(table):
        cores = jnp.stack([table[:, :edge], table[:, edge : 2 * edge]])
        gains = [table[:, 2 * edge + k : 2 * edge + k + 1] for k in range(4)]
        return cores, jnp.stack(gains[:2]), jnp.stack(gains[2:])

    def spread(cores, flow):
        return jnp.einsum("cij,cjp->cip", cores, flow, precision=PRECISE)

    def south_drops(rims):
        return [rims[k] - rims[(k + 1) % rows] * not_last[k] for k in range(rows)]

    def vertical(flows):
        return [flows[k] - flows[k - 1] * not_first[k] for k in range(rows)]

    raw = [block[:span].reshape((tiles, edge, patterns)) for block in column]
    start = [block[span : 2 * span].reshape((tiles, edge, patterns)) for block in column]
    table = [block[2 * span : 2 * span + edge] for block in column]
    first = sum(block[2 * span + edge] for block in column)
    cores, easts, souths = zip(*[unpack(t) for t in table])
    flow = vertical([g * d for g, d in zip(souths, south_drops(start))])
    u0 = [raw[k] - spread(cores[k], flow[k]) for k in range(rows)]
    first = first - sum(jnp.sum(flow[k] * (raw[k] + u0[k]), axis=(0, 1)) for k in range(rows))
    precond = precond - spread(inverse[:, :, :edge], flow[0])

    message = jnp.concatenate(
        [piece for k in range(rows) for piece in (u0[k].reshape((span, patterns)), table[k])]
    )
    inner = other(message, "col", cols, 1)
    beyond = outer(message, "col", cols)
    far = lax.ppermute(
        jnp.concatenate([u[0] for u in u0]), "col", [((i + 2) % cols, i) for i in range(cols)]
    )
    far = far * has_far
    west = jnp.where(odd, inner, beyond) * has_west
    east = jnp.where(odd, beyond, inner) * has_east
    stride = span + edge

    def parts(block, k):
        block = block[k * stride : (k + 1) * stride]
        return (block[:span].reshape((tiles, edge, patterns)),) + unpack(block[span:])

    wide_u0, wide_cores, wide_easts, wide_souths, mid_cores = [], [], [], [], []
    for k in range(rows):
        west_u, west_cores, west_easts, west_souths = parts(west, k)
        east_u, east_cores, east_easts, east_souths = parts(east, k)
        wide_u0.append(
            jnp.concatenate([west_u, u0[k], east_u, far[None, k * edge : (k + 1) * edge]])
        )
        wide_cores.append(jnp.concatenate([west_cores[1:], cores[k], east_cores]))
        mid_cores.append(jnp.concatenate([cores[k], east_cores[:1]]))
        wide_easts.append(jnp.concatenate([west_easts, easts[k], east_easts]))
        wide_souths.append(jnp.concatenate([west_souths[1:], souths[k], east_souths]))

    def net_flow(rims, easts, souths):
        across = [g * (u[:-1] - u[1:]) for g, u in zip(easts, rims)]
        down = vertical([g * d for g, d in zip(souths, south_drops([u[1:-1] for u in rims]))])
        return [a[1:] - a[:-1] + d for a, d in zip(across, down)]

    t0 = net_flow(wide_u0, wide_easts, wide_souths)
    u1 = [spread(c, t) for c, t in zip(wide_cores, t0)]
    t1 = net_flow(u1, [g[1:-1] for g in wide_easts], [g[1:-1] for g in wide_souths])
    u2 = [spread(c, t) for c, t in zip(mid_cores, t1)]
    drops = south_drops([u[:2] for u in u2])

    def total(left, right):
        return sum(jnp.sum(a * b, axis=(0, 1)) for a, b in zip(left, right))

    own_t0, own_u1, own_t1 = [t[1:3] for t in t0], [u[1:3] for u in u1], [t[:2] for t in t1]
    ahead = [u[:2] - u[1:] for u in u2]
    moments = jnp.stack(
        [
            first,
            total([u[2:4] for u in wide_u0], own_t0),
            total(own_u1, own_t0),
            total(own_u1, own_t1),
            total([u[:2] for u in u2], own_t1),
            total([g[1:3] * d for g, d in zip(wide_souths, drops)], drops)
            + total([g[2:4] * d for g, d in zip(wide_easts, ahead)], ahead),
            jnp.zeros_like(first),
            jnp.zeros_like(first),
        ]
    )
    m = xor_sum(moments, "col", cols)

    a00, a01, a02 = m[0] + m[1], m[1] + m[2], m[2] + m[3]
    a12, a22 = m[3] + m[4], m[4] + m[5]
    l1, l2 = a01 / a00, a02 / a00
    d1 = a02 - l1 * a01
    e12 = a12 - l2 * a01
    l12 = e12 / d1
    d2 = a22 - l2 * a02 - l12 * e12
    y1 = m[1] - l1 * m[0]
    y2 = m[2] - l2 * m[0] - l12 * y1
    c2 = y2 / d2
    c1 = y1 / d1 - l12 * c2
    c0 = m[0] / a00 - l1 * c1 - l2 * c2
    mixed = c1 * own_t0[0] + c2 * own_t1[0]
    update = jnp.einsum("cij,cjp->cip", inverse[:, :, :edge], mixed, precision=PRECISE)
    return (voltage + c0 * precond + update)[None]


def solution(mesh):
    whole = P("row", "col", None, None)
    third = P("row", "col", None)
    placed = (whole, whole, whole, third, whole, third, whole, third, whole, whole, whole)
    return jax.shard_map(local, mesh=mesh, in_specs=placed, out_specs=whole, check_vma=False)
```

```python
import functools

import jax
import jax.numpy as jnp
from jax import lax
from jax.experimental import pallas as pl
from jax.experimental.pallas import tpu as pltpu
from jax.sharding import PartitionSpec as P

DOUBLINGS = 5
SMALL = 2.0**-13
VMEM_BYTES = 16 * 1024 * 1024

dot = functools.partial(
    jnp.dot, precision=lax.Precision.HIGHEST, preferred_element_type=jnp.float32
)


def run(kernel, outs, *args, scratch=(), flops=0):
    vmem = pl.BlockSpec(memory_space=pltpu.VMEM)
    shapes = tuple(jax.ShapeDtypeStruct(shape, jnp.float32) for shape in outs)
    moved = sum(4 * a.size for a in args) + sum(4 * s.size for s in shapes)
    return pl.pallas_call(
        kernel,
        out_shape=shapes,
        in_specs=[vmem] * len(args),
        out_specs=(vmem,) * len(shapes),
        scratch_shapes=list(scratch),
        compiler_params=pltpu.CompilerParams(vmem_limit_bytes=VMEM_BYTES),
        cost_estimate=pl.CostEstimate(flops=flops, bytes_accessed=moved, transcendentals=0),
    )(*args)


def iota(shape, axis):
    return lax.broadcasted_iota(jnp.int32, shape, axis)


def to_column(row):
    count = row.shape[1]
    square = jnp.broadcast_to(row, (count, count))
    keep = iota((count, count), 0) == iota((count, count), 1)
    return jnp.sum(jnp.where(keep, square, 0.0), axis=1, keepdims=True)


def slot_column(table):
    sources, slots = table.shape
    spread = jnp.concatenate(
        [jnp.broadcast_to(table[s : s + 1], (slots, slots)) for s in range(sources)], axis=0
    )
    keep = iota(spread.shape, 0) % slots == iota(spread.shape, 1)
    return jnp.sum(jnp.where(keep, spread, 0.0), axis=1, keepdims=True)


def source_column(row, slots):
    sources = row.shape[1]
    spread = jnp.broadcast_to(row, (sources * slots, sources))
    keep = iota(spread.shape, 0) // slots == iota(spread.shape, 1)
    return jnp.sum(jnp.where(keep, spread, 0.0), axis=1, keepdims=True)


def start_kernel(nets, edge, volt_ref, driver_ref, gain_ref, out_ref):
    tiles, nodes, patterns = volt_ref.shape
    odd = lax.axis_index("col") % 2 == 1
    picked = to_column(driver_ref[...].astype(jnp.float32))
    drivers = jnp.zeros((nets, patterns), jnp.float32)
    for t in range(tiles):
        block = volt_ref[t]
        block = jnp.concatenate([block] * (-(-nets // nodes)), axis=0)[:nets]
        drivers = jnp.where(picked == t, block, drivers)
    low, high = volt_ref[0, :edge], volt_ref[tiles - 1, :edge]
    out_ref[:nets] = drivers
    out_ref[nets : nets + edge] = jnp.where(odd, low, high)
    out_ref[nets + edge : nets + 2 * edge] = jnp.where(odd, high, low)
    out_ref[nets + 2 * edge :] = jnp.zeros((8, patterns), jnp.float32)
    out_ref[nets + 2 * edge : nets + 2 * edge + 1, :edge] = gain_ref[tiles - 1, 0:1]


def pair_kernel(nets, edge, mine_ref, mate_ref, out_ref):
    out_ref[:nets] = mine_ref[:nets]
    out_ref[nets : 2 * nets] = mate_ref[:nets]
    out_ref[2 * nets :] = mate_ref[nets + edge :]


def tile_kernel(
    nets,
    edge,
    conduct_ref,
    cap_ref,
    volt_ref,
    inject_ref,
    gain_ref,
    net_ref,
    count_ref,
    tile_ref,
    node_ref,
    weight_ref,
    inverse_ref,
    rest_ref,
    table_ref,
    take_ref,
    put_ref,
    sum_ref,
    power_ref,
):
    tiles, nodes = conduct_ref.shape[0], conduct_ref.shape[1]
    eye = jnp.where(iota((nodes, nodes), 0) == iota((nodes, nodes), 1), 1.0, 0.0)
    sums, powers, scales = [], [], []
    for t in range(tiles):
        conduct = conduct_ref[t]
        diagonal = (conduct + cap_ref[t : t + 1, :]) * eye
        down = jnp.sum(diagonal, axis=1, keepdims=True)
        across = jnp.sum(diagonal, axis=0, keepdims=True)
        power = (conduct * eye - conduct) / down
        sums.append(eye + power)
        powers.append(dot(power, power))
        scales.append(1.0 / across)
        rest_ref[t] = inject_ref[t] - dot(conduct, volt_ref[t])

    def step(sums, powers):
        out_sums, out_powers, largest = [], [], jnp.float32(0.0)
        for total, power in zip(sums, powers):
            both = dot(jnp.concatenate([total, power], axis=0), power)
            out_sums.append(total + both[:nodes])
            out_powers.append(both[nodes:])
            largest = jnp.maximum(largest, jnp.max(jnp.sum(power, axis=1)))
        return out_sums, out_powers, largest

    for _ in range(DOUBLINGS):
        sums, powers, largest = step(sums, powers)
    for t in range(tiles):
        sum_ref[t], power_ref[t] = sums[t], powers[t]

    def again(carry):
        sums, powers, largest = step(
            [sum_ref[t] for t in range(tiles)], [power_ref[t] for t in range(tiles)]
        )
        for t in range(tiles):
            sum_ref[t], power_ref[t] = sums[t], powers[t]
        return largest, carry[1] + 1

    lax.while_loop(
        lambda carry: (carry[0] > SMALL) & (carry[1] < 40), again, (largest, jnp.int32(0))
    )
    lane = iota((edge, nodes), 1)
    table = jnp.zeros((edge, nodes), jnp.float32)
    for t in range(tiles):
        inverse = sum_ref[t] * scales[t]
        inverse_ref[t] = inverse
        corner = inverse[:edge] if t == 0 else pltpu.roll(inverse[:edge], t * edge, 1)
        table = jnp.where((lane >= t * edge) & (lane < (t + 1) * edge), corner, table)
        for side in range(2):
            gain = to_column(gain_ref[t, side : side + 1])
            table = jnp.where(lane == tiles * edge + side * tiles + t, gain, table)
    table_ref[...] = table

    sources, slots = net_ref.shape
    mine = lax.axis_index("col")
    block = iota((sources, slots), 0) ^ mine
    place = slot_column((block * nets + net_ref[...]).astype(jnp.float32))
    target = slot_column((tile_ref[...] * nodes + node_ref[...]).astype(jnp.float32))
    live = source_column(count_ref[...].astype(jnp.float32), slots)
    slot = (iota(live.shape, 0) % slots).astype(jnp.float32)
    weight = jnp.where(slot < live, slot_column(weight_ref[...]), 0.0)
    take_ref[...] = jnp.where(place == iota(take_ref.shape, 1).astype(jnp.float32), 1.0, 0.0)
    put_ref[...] = jnp.where(target == iota(put_ref.shape, 1).astype(jnp.float32), weight, 0.0)


def residual_kernel(
    nets,
    edge,
    cols,
    volt_ref,
    mate_ref,
    inverse_ref,
    rest_ref,
    table_ref,
    take_ref,
    put_ref,
    *refs,
):
    *group_refs, message_ref, precond_ref = refs
    tiles, nodes, patterns = volt_ref.shape
    mine = lax.axis_index("col")
    odd = mine % 2 == 1
    stride = 2 * nets + edge + 8
    blocks = [(ref, base) for ref in group_refs for base in range(0, ref.shape[0], stride)]
    values = sum(
        dot(take_ref[:, j * 2 * nets : (j + 1) * 2 * nets], ref[base : base + 2 * nets])
        for j, (ref, base) in enumerate(blocks)
    )
    injected = lax.dot_general(
        put_ref[...],
        values,
        (((0,), (0,)), ((), ())),
        precision=lax.Precision.HIGHEST,
        preferred_element_type=jnp.float32,
    )
    beyond = lax.rem(jnp.where(odd, mine + 1, mine + cols - 1), cols) ^ 1
    which = (mine ^ beyond) // 2
    outer = jnp.zeros((edge + 8, patterns), jnp.float32)
    for j, (ref, base) in enumerate(blocks):
        outer = jnp.where(which == j, ref[base + 2 * nets : base + stride], outer)
    inner = mate_ref[nets : nets + edge]
    inner_gain = mate_ref[nets + 2 * edge : nets + 2 * edge + 1]
    has_west = jnp.where(mine > 0, 1.0, 0.0)
    has_east = jnp.where(mine < cols - 1, 1.0, 0.0)
    west = jnp.where(odd, inner, outer[:edge]) * has_west
    east = jnp.where(odd, outer[:edge], inner) * has_east
    west_gain = to_column(jnp.where(odd, inner_gain, outer[edge : edge + 1])[:, :edge]) * has_west
    first_gain = tiles * edge
    gains = [west_gain] + [
        table_ref[:, first_gain + t : first_gain + t + 1] for t in range(tiles)
    ]
    rims = [west] + [volt_ref[t, :edge] for t in range(tiles)] + [east]
    flows = [gains[t] * (rims[t] - rims[t + 1]) for t in range(tiles + 1)]
    first = jnp.zeros((1, patterns), jnp.float32)
    for t in range(tiles):
        residual = rest_ref[t] + injected[t * nodes : (t + 1) * nodes]
        residual = jnp.concatenate(
            [residual[:edge] - (flows[t + 1] - flows[t]), residual[edge:]], axis=0
        )
        precond = dot(inverse_ref[t], residual)
        precond_ref[t] = precond
        first = first + jnp.sum(residual * precond, axis=0, keepdims=True)
        message_ref[t * edge : (t + 1) * edge] = precond[:edge]
        message_ref[(tiles + t) * edge : (tiles + t + 1) * edge] = volt_ref[t, :edge]
    message_ref[2 * tiles * edge : (2 * tiles + 1) * edge] = table_ref[...]
    message_ref[(2 * tiles + 1) * edge :] = jnp.broadcast_to(first, (8, patterns))


def corners(tables, tiles, edge):
    lane = iota((edge, tables.shape[1]), 1)
    parts = [
        jnp.where((lane >= t * edge) & (lane < (t + 1) * edge), tables, 0.0) for t in range(tiles)
    ]
    return jnp.concatenate(parts, axis=0)[:, : tiles * edge]


def row_masks(rows):
    place = lax.axis_index("row")
    index = [lax.rem(place + k, rows) for k in range(rows)]
    not_first = [jnp.where(i > 0, 1.0, 0.0) for i in index]
    not_last = [jnp.where(i < rows - 1, 1.0, 0.0) for i in index]
    return not_first, not_last


def rim_kernel(rows, tiles, edge, *refs):
    column_refs, (message_ref, far_ref, flow_ref, first_ref) = refs[:rows], refs[rows:]
    patterns = message_ref.shape[1]
    span, gain_lane = tiles * edge, tiles * edge + tiles
    not_first, not_last = row_masks(rows)
    start = [ref[span : 2 * span] for ref in column_refs]
    tables = [ref[2 * span : 2 * span + edge] for ref in column_refs]
    south = []
    for k in range(rows):
        gain = jnp.concatenate(
            [
                jnp.broadcast_to(tables[k][:, gain_lane + t : gain_lane + t + 1], (edge, patterns))
                for t in range(tiles)
            ],
            axis=0,
        )
        south.append(gain * (start[k] - start[(k + 1) % rows] * not_last[k]))
    first = sum(ref[2 * span + edge : 2 * span + edge + 1] for ref in column_refs)
    dropped = jnp.zeros((span, patterns), jnp.float32)
    stride = span + edge
    for k in range(rows):
        flow = south[k] - south[k - 1] * not_first[k]
        raw = column_refs[k][:span]
        rim = raw - dot(corners(tables[k], tiles, edge), flow)
        dropped = dropped + flow * (raw + rim)
        message_ref[k * stride : k * stride + span] = rim
        message_ref[k * stride + span : (k + 1) * stride] = tables[k]
        far_ref[k * edge : (k + 1) * edge] = rim[:edge]
        if k == 0:
            flow_ref[...] = flow
    first = first - jnp.sum(dropped, axis=0, keepdims=True)
    first_ref[...] = jnp.broadcast_to(first, first_ref.shape)


def moment_kernel(
    rows, cols, tiles, edge, own_ref, inner_ref, outer_ref, far_ref, first_ref, moment_ref, t0_ref, t1_ref
):
    patterns = own_ref.shape[1]
    mine = lax.axis_index("col")
    odd = mine % 2 == 1
    has_west = jnp.where(mine > 0, 1.0, 0.0)
    has_east = jnp.where(mine < cols - 1, 1.0, 0.0)
    has_far = jnp.where(mine < cols - 2, 1.0, 0.0)
    not_first, not_last = row_masks(rows)
    span = tiles * edge
    stride = span + edge
    easts, souths, u0, mats = [], [], [], []
    for k in range(rows):
        piece = slice(k * stride, (k + 1) * stride)
        own = own_ref[piece]
        west = jnp.where(odd, inner_ref[piece], outer_ref[piece]) * has_west
        east = jnp.where(odd, outer_ref[piece], inner_ref[piece]) * has_east
        far = far_ref[k * edge : (k + 1) * edge] * has_far
        u0.append(
            [block[t * edge : (t + 1) * edge] for block in (west, own, east) for t in range(tiles)]
            + [far]
        )
        tables = [block[span:] for block in (west, own, east)]

        def gain(table, lane):
            return jnp.broadcast_to(table[:, lane : lane + 1], (edge, patterns))

        easts.append([gain(table, span + t) for table in tables for t in range(tiles)])
        souths.append([gain(table, span + tiles + t) for table in tables for t in range(tiles)])
        mats.append([corners(table, tiles, edge) for table in tables])

    def net_flow(rims, low, high):
        flows = []
        for k in range(rows):
            below, above = (k + 1) % rows, k - 1
            row = []
            for c in range(low, high):
                flow = easts[k][c] * (rims[k][c] - rims[k][c + 1])
                flow = flow - easts[k][c - 1] * (rims[k][c - 1] - rims[k][c])
                flow = flow + souths[k][c] * (rims[k][c] - rims[below][c] * not_last[k])
                back = souths[above][c] * (rims[k][c] - rims[above][c])
                row.append(flow + back * not_first[k])
            flows.append([None] * low + row)
        return flows

    def spread(flows, devices, low, high):
        out = []
        for k in range(rows):
            row = []
            for d in devices:
                block = [
                    flows[k][c] if low <= c < high else jnp.zeros((edge, patterns), jnp.float32)
                    for c in range(d * tiles, (d + 1) * tiles)
                ]
                block = dot(mats[k][d], jnp.concatenate(block, axis=0))
                row += [block[t * edge : (t + 1) * edge] for t in range(tiles)]
            out.append([None] * (devices[0] * tiles) + row)
        return out

    t0 = net_flow(u0, tiles - 1, 3 * tiles)
    u1 = spread(t0, [0, 1, 2], tiles - 1, 3 * tiles)
    t1 = net_flow(u1, tiles, 2 * tiles + 1)
    u2 = spread(t1, [1, 2], tiles, 2 * tiles + 1)
    zero = jnp.zeros((edge, patterns), jnp.float32)
    sums = [zero] * 5
    for k in range(rows):
        for c in range(tiles, 2 * tiles):
            ahead = u2[k][c] - u2[k][c + 1]
            drop = u2[k][c] - u2[(k + 1) % rows][c] * not_last[k]
            parts = (
                u0[k][c] * t0[k][c],
                u1[k][c] * t0[k][c],
                u1[k][c] * t1[k][c],
                u2[k][c] * t1[k][c],
                easts[k][c] * ahead * ahead + souths[k][c] * drop * drop,
            )
            sums = [total + part for total, part in zip(sums, parts)]
    moment_ref[0:1] = first_ref[0:1]
    for i, total in enumerate(sums):
        moment_ref[i + 1 : i + 2] = jnp.sum(total, axis=0, keepdims=True)
    moment_ref[6:8] = jnp.zeros((2, patterns), jnp.float32)
    t0_ref[...] = jnp.concatenate(t0[0][tiles : 2 * tiles], axis=0)
    t1_ref[...] = jnp.concatenate(t1[0][tiles : 2 * tiles], axis=0)


def final_kernel(edge, volt_ref, precond_ref, inverse_ref, flow_ref, t0_ref, t1_ref, *refs):
    *sum_refs, out_ref = refs
    tiles = volt_ref.shape[0]
    sums = sum(ref[...] for ref in sum_refs)
    m = [sums[i : i + 1] for i in range(6)]
    a00, a01, a02 = m[0] + m[1], m[1] + m[2], m[2] + m[3]
    a12, a22 = m[3] + m[4], m[4] + m[5]
    l1, l2 = a01 / a00, a02 / a00
    d1 = a02 - l1 * a01
    e12 = a12 - l2 * a01
    l12 = e12 / d1
    d2 = a22 - l2 * a02 - l12 * e12
    y1 = m[1] - l1 * m[0]
    y2 = m[2] - l2 * m[0] - l12 * y1
    c2 = y2 / d2
    c1 = y1 / d1 - l12 * c2
    c0 = m[0] / a00 - l1 * c1 - l2 * c2
    mixed = c1 * t0_ref[...] + c2 * t1_ref[...] - c0 * flow_ref[...]
    for t in range(tiles):
        update = dot(inverse_ref[t, :, :edge], mixed[t * edge : (t + 1) * edge])
        out_ref[t] = volt_ref[t] + c0 * precond_ref[t] + update


def other(block, axis, count, distance):
    return lax.ppermute(block, axis, [(i, i ^ distance) for i in range(count)])


def stages(count, held):
    while held < count:
        reach = 2 if (count // held).bit_length() % 2 == 0 else 4
        yield [held * k for k in range(1, reach)]
        held *= reach


def outer_swap(block, axis, count):
    pairs = [(i, (i + 1) % count if i % 2 else (i - 1) % count) for i in range(count)]
    return lax.ppermute(block, axis, pairs)


def local(
    initial_voltage,
    inject,
    conduct,
    capacitance,
    track_gain,
    driver_tile,
    sink_net,
    sink_count,
    sink_tile,
    sink_node,
    sink_gain,
):
    rows, cols = lax.axis_size("row"), lax.axis_size("col")
    tiles, nodes, patterns = initial_voltage.shape[1:]
    edge, nets = track_gain.shape[-1], driver_tile.shape[-1]
    slots = cols * sink_net.shape[-1]
    voltage = initial_voltage[0]
    field = (tiles, nodes, patterns)
    span = tiles * edge

    mine = run(
        functools.partial(start_kernel, nets, edge),
        [(nets + 2 * edge + 8, patterns)],
        voltage,
        driver_tile[0],
        track_gain[0],
    )[0]
    mate = other(mine, "col", cols, 1)
    pair = run(
        functools.partial(pair_kernel, nets, edge), [(2 * nets + edge + 8, patterns)], mine, mate
    )[0]
    pair, conduct = lax.optimization_barrier((pair, conduct))
    groups = [pair]
    for distances in stages(cols, 2):
        whole = groups[0] if len(groups) == 1 else jnp.concatenate(groups)
        groups = [whole] + [other(whole, "col", cols, d) for d in distances]

    inverse, rest, table, take, put = run(
        functools.partial(tile_kernel, nets, edge),
        [field, field, (edge, patterns), (slots, cols * nets), (slots, tiles * nodes)],
        conduct[0],
        capacitance[0],
        voltage,
        inject[0],
        track_gain[0],
        sink_net[0, 0],
        sink_count[0],
        sink_tile[0, 0],
        sink_node[0, 0],
        sink_gain[0, 0],
        scratch=[pltpu.VMEM(field, jnp.float32)] * 2,
        flops=16 * 2 * tiles * nodes**3 * 6,
    )

    message, precond = run(
        functools.partial(residual_kernel, nets, edge, cols),
        [(2 * span + edge + 8, patterns), field],
        voltage,
        mate,
        inverse,
        rest,
        table,
        take,
        put,
        *groups,
    )

    column = [message] + [
        lax.ppermute(message, "row", [((i + k) % rows, i) for i in range(rows)])
        for k in range(1, rows)
    ]
    message, far, flow, first = run(
        functools.partial(rim_kernel, rows, tiles, edge),
        [(rows * (span + edge), patterns), (rows * edge, patterns), (span, patterns), (8, patterns)],
        *column,
    )

    inner = other(message, "col", cols, 1)
    beyond = outer_swap(message, "col", cols)
    far = lax.ppermute(far, "col", [((i + 2) % cols, i) for i in range(cols)])
    moments, t0, t1 = run(
        functools.partial(moment_kernel, rows, cols, tiles, edge),
        [(8, patterns), (span, patterns), (span, patterns)],
        message,
        inner,
        beyond,
        far,
        first,
    )

    sums = [moments]
    for distances in stages(cols, 1):
        moments = sum(sums[1:], sums[0])
        sums = [moments] + [other(moments, "col", cols, d) for d in distances]
    return run(
        functools.partial(final_kernel, edge),
        [field],
        voltage,
        precond,
        inverse,
        flow,
        t0,
        t1,
        *sums,
    )[0][None]


def solution(mesh):
    whole = P("row", "col", None, None)
    third = P("row", "col", None)
    placed = (whole, whole, whole, third, whole, third, whole, third, whole, whole, whole)
    return jax.shard_map(local, mesh=mesh, in_specs=placed, out_specs=whole, check_vma=False)
```

```python
import functools

import jax
import jax.numpy as jnp
from jax import lax
from jax.experimental import pallas as pl
from jax.experimental.pallas import tpu as pltpu
from jax.sharding import PartitionSpec as P

DOUBLINGS = 5
SMALL = 2.0**-13
VMEM_BYTES = 16 * 1024 * 1024

dot = functools.partial(
    jnp.dot, precision=lax.Precision.HIGHEST, preferred_element_type=jnp.float32
)


def split(block):
    high = block.astype(jnp.bfloat16)
    return high, (block - high.astype(jnp.float32)).astype(jnp.bfloat16)


def narrow(left, right):
    return jnp.dot(left, right, preferred_element_type=jnp.float32)


def dot3(left, right):
    (left_high, left_low), (right_high, right_low) = split(left), split(right)
    return narrow(left_high, right_high) + (
        narrow(left_high, right_low) + narrow(left_low, right_high)
    )


def select(onehot, block):
    high = block.astype(jnp.bfloat16)
    rest = block - high.astype(jnp.float32)
    middle, low = split(rest)
    return narrow(onehot, high) + (narrow(onehot, middle) + narrow(onehot, low))


def run(kernel, outs, *args, scratch=(), flops=4_000_000_000):
    vmem = pl.BlockSpec(memory_space=pltpu.VMEM)
    shapes = tuple(
        o if isinstance(o, jax.ShapeDtypeStruct) else jax.ShapeDtypeStruct(o, jnp.float32)
        for o in outs
    )
    moved = sum(4 * a.size for a in args) + sum(4 * s.size for s in shapes)
    return pl.pallas_call(
        kernel,
        out_shape=shapes,
        in_specs=[vmem] * len(args),
        out_specs=(vmem,) * len(shapes),
        scratch_shapes=list(scratch),
        compiler_params=pltpu.CompilerParams(vmem_limit_bytes=VMEM_BYTES),
        cost_estimate=pl.CostEstimate(flops=flops, bytes_accessed=moved, transcendentals=0),
    )(*args)


def iota(shape, axis):
    return lax.broadcasted_iota(jnp.int32, shape, axis)


def to_column(row):
    count = row.shape[1]
    square = jnp.broadcast_to(row, (count, count))
    keep = iota((count, count), 0) == iota((count, count), 1)
    return jnp.sum(jnp.where(keep, square, 0.0), axis=1, keepdims=True)


def slot_column(table):
    sources, slots = table.shape
    spread = jnp.concatenate(
        [jnp.broadcast_to(table[s : s + 1], (slots, slots)) for s in range(sources)], axis=0
    )
    keep = iota(spread.shape, 0) % slots == iota(spread.shape, 1)
    return jnp.sum(jnp.where(keep, spread, 0.0), axis=1, keepdims=True)


def source_column(row, slots):
    sources = row.shape[1]
    spread = jnp.broadcast_to(row, (sources * slots, sources))
    keep = iota(spread.shape, 0) // slots == iota(spread.shape, 1)
    return jnp.sum(jnp.where(keep, spread, 0.0), axis=1, keepdims=True)


def pair_kernel(nets, edge, volt_ref, picked_ref, mate_ref, mate_driver_ref, mate_gain_ref, out_ref):
    tiles, nodes, patterns = volt_ref.shape
    odd = lax.axis_index("col") % 2 == 1
    mate_picked = to_column(mate_driver_ref[...].astype(jnp.float32))
    for i, (field, picked) in enumerate(((volt_ref, picked_ref[...]), (mate_ref, mate_picked))):
        rows = jnp.zeros((nets, patterns), jnp.float32)
        for t in range(tiles):
            block = jnp.concatenate([field[t]] * (-(-nets // nodes)), axis=0)[:nets]
            rows = jnp.where(picked == t, block, rows)
        out_ref[i * nets : (i + 1) * nets] = rows
    base = 2 * nets
    out_ref[base : base + edge] = jnp.where(odd, mate_ref[0, :edge], mate_ref[tiles - 1, :edge])
    out_ref[base + edge :] = jnp.zeros((8, patterns), jnp.float32)
    out_ref[base + edge : base + edge + 1, :edge] = mate_gain_ref[tiles - 1, 0:1]


def eye_kernel(out_ref):
    out_ref[...] = jnp.where(iota(out_ref.shape, 0) == iota(out_ref.shape, 1), 1.0, 0.0)


def sink_kernel(
    nets,
    edge,
    conduct_ref,
    volt_ref,
    inject_ref,
    gain_ref,
    net_ref,
    count_ref,
    tile_ref,
    node_ref,
    weight_ref,
    driver_ref,
    rest_ref,
    gains_ref,
    take_ref,
    put_ref,
    scale_ref,
    picked_ref,
):
    picked_ref[...] = jnp.broadcast_to(
        to_column(driver_ref[...].astype(jnp.float32)), picked_ref.shape
    )
    tiles, nodes = conduct_ref.shape[0], conduct_ref.shape[1]
    for t in range(tiles):
        rest_ref[t] = inject_ref[t] - dot(conduct_ref[t], volt_ref[t])
    lane = iota((edge, nodes), 1)
    table = jnp.zeros((edge, nodes), jnp.float32)
    gains_ref[edge:] = jnp.zeros((8, nodes), jnp.float32)
    for side in range(2):
        for t in range(tiles):
            i = side * tiles + t
            gain = gain_ref[t, side : side + 1]
            table = jnp.where(lane == i, to_column(gain), table)
            gains_ref[edge : edge + 1, i * edge : (i + 1) * edge] = gain
    gains_ref[:edge] = table

    sources, slots = net_ref.shape
    mine = lax.axis_index("col")
    block = iota((sources, slots), 0) ^ mine
    place = slot_column((block * nets + net_ref[...]).astype(jnp.float32))
    target = slot_column((tile_ref[...] * nodes + node_ref[...]).astype(jnp.float32))
    live = source_column(count_ref[...].astype(jnp.float32), slots)
    slot = (iota(live.shape, 0) % slots).astype(jnp.float32)
    weight = jnp.where(slot < live, slot_column(weight_ref[...]), 0.0)
    take = jnp.where(place == iota(take_ref.shape, 1).astype(jnp.float32), 1.0, 0.0)
    put = jnp.where(target == iota(put_ref.shape, 1).astype(jnp.float32), 1.0, 0.0)
    take_ref[...] = take.astype(jnp.bfloat16)
    put_ref[...] = put.astype(jnp.bfloat16)
    scale_ref[...] = jnp.broadcast_to(weight, scale_ref.shape)


def tile_kernel(edge, eye_ref, conduct_ref, cap_ref, after_ref, inverse_ref, fold_ref, sum_ref, power_ref):
    tiles, nodes = conduct_ref.shape[0], conduct_ref.shape[1]
    eye = eye_ref[...]
    sums, powers, scales = [], [], []
    for t in range(tiles):
        conduct = conduct_ref[t]
        diagonal = (conduct + cap_ref[t : t + 1, :]) * eye
        down = jnp.sum(diagonal, axis=1, keepdims=True)
        across = jnp.sum(diagonal, axis=0, keepdims=True)
        power = (conduct * eye - conduct) / down
        sums.append(eye + power)
        powers.append(dot(power, power))
        scales.append(1.0 / across)

    def step(sums, powers):
        out_sums, out_powers, largest = [], [], jnp.float32(0.0)
        for total, power in zip(sums, powers):
            both = dot(jnp.concatenate([total, power], axis=0), power)
            out_sums.append(total + both[:nodes])
            out_powers.append(both[nodes:])
            largest = jnp.maximum(largest, jnp.max(jnp.sum(power, axis=1)))
        return out_sums, out_powers, largest

    for _ in range(DOUBLINGS):
        sums, powers, largest = step(sums, powers)
    for t in range(tiles):
        sum_ref[t], power_ref[t] = sums[t], powers[t]

    def again(carry):
        sums, powers, largest = step(
            [sum_ref[t] for t in range(tiles)], [power_ref[t] for t in range(tiles)]
        )
        for t in range(tiles):
            sum_ref[t], power_ref[t] = sums[t], powers[t]
        return largest, carry[1] + 1

    lax.while_loop(
        lambda carry: (carry[0] > SMALL) & (carry[1] < 40), again, (largest, jnp.int32(0))
    )
    parts = nodes // edge
    depth = edge // parts
    lane = iota((depth, nodes), 1)
    for t in range(tiles):
        inverse = sum_ref[t] * scales[t]
        inverse_ref[t] = inverse
        fold = jnp.zeros((depth, nodes), jnp.float32)
        for j in range(parts):
            piece = jnp.where(lane < edge, inverse[j * depth : (j + 1) * depth], 0.0)
            fold = fold + (pltpu.roll(piece, j * edge, 1) if j else piece)
        fold_ref[t * depth : (t + 1) * depth] = fold


def residual_kernel(
    nets,
    edge,
    cols,
    volt_ref,
    mate_ref,
    mate_gain_ref,
    inverse_ref,
    fold_ref,
    rest_ref,
    gains_ref,
    take_ref,
    put_ref,
    scale_ref,
    *refs,
):
    *group_refs, message_ref, precond_ref = refs
    tiles, nodes, patterns = volt_ref.shape
    mine = lax.axis_index("col")
    odd = mine % 2 == 1
    stride = 2 * nets + edge + 8
    blocks = [(ref, base) for ref in group_refs for base in range(0, ref.shape[0], stride)]
    values = sum(
        select(take_ref[:, j * 2 * nets : (j + 1) * 2 * nets], ref[base : base + 2 * nets])
        for j, (ref, base) in enumerate(blocks)
    )
    values = values * scale_ref[...]
    beyond = lax.rem(jnp.where(odd, mine + 1, mine + cols - 1), cols) ^ 1
    which = (mine ^ beyond) // 2
    outer = jnp.zeros((edge + 8, patterns), jnp.float32)
    for j, (ref, base) in enumerate(blocks):
        outer = jnp.where(which == j, ref[base + 2 * nets : base + stride], outer)
    inner = jnp.where(odd, mate_ref[tiles - 1, :edge], mate_ref[0, :edge])
    inner_gain = to_column(mate_gain_ref[tiles - 1, 0:1])
    has_west = jnp.where(mine > 0, 1.0, 0.0)
    has_east = jnp.where(mine < cols - 1, 1.0, 0.0)
    west = jnp.where(odd, inner, outer[:edge]) * has_west
    east = jnp.where(odd, outer[:edge], inner) * has_east
    west_gain = jnp.where(odd, inner_gain, to_column(outer[edge : edge + 1, :edge])) * has_west
    gains = [west_gain] + [gains_ref[:edge, t : t + 1] for t in range(tiles)]
    rims = [west] + [volt_ref[t, :edge] for t in range(tiles)] + [east]
    flows = [gains[t] * (rims[t] - rims[t + 1]) for t in range(tiles + 1)]
    first = jnp.zeros((1, patterns), jnp.float32)
    high, low = split(values)
    for t in range(tiles):
        put = put_ref[:, t * nodes : (t + 1) * nodes]
        injected = sum(
            lax.dot_general(
                put, part, (((0,), (0,)), ((), ())), preferred_element_type=jnp.float32
            )
            for part in (high, low)
        )
        residual = rest_ref[t] + injected
        residual = jnp.concatenate(
            [residual[:edge] - (flows[t + 1] - flows[t]), residual[edge:]], axis=0
        )
        precond = dot3(inverse_ref[t], residual)
        precond_ref[t] = precond
        first = first + jnp.sum(residual * precond, axis=0, keepdims=True)
        message_ref[t * edge : (t + 1) * edge] = precond[:edge]
        message_ref[(tiles + t) * edge : (tiles + t + 1) * edge] = volt_ref[t, :edge]
    base = 2 * tiles * edge
    depth = fold_ref.shape[0]
    message_ref[base : base + depth] = fold_ref[...]
    message_ref[base + depth : base + depth + 8] = gains_ref[edge:]
    message_ref[base + depth + 1 : base + depth + 2] = first


def corners(fold, tiles, edge):
    depth, lanes = fold.shape[0] // tiles, fold.shape[1]
    lane = iota((depth, lanes), 1)
    rows = []
    for t in range(tiles):
        piece = fold[t * depth : (t + 1) * depth]
        for j in range(lanes // edge):
            turn = (t - j) * edge % lanes
            turned = pltpu.roll(piece, turn, 1) if turn else piece
            rows.append(jnp.where((lane >= t * edge) & (lane < (t + 1) * edge), turned, 0.0))
    return jnp.concatenate(rows, axis=0)[:, : tiles * edge]


def turned(rows):
    count, lanes = rows.shape
    full = jnp.concatenate([rows, jnp.zeros((lanes - count, lanes), jnp.float32)], axis=0)
    return jnp.transpose(full)


def row_masks(rows):
    place = lax.axis_index("row")
    index = [lax.rem(place + k, rows) for k in range(rows)]
    not_first = [jnp.where(i > 0, 1.0, 0.0) for i in index]
    not_last = [jnp.where(i < rows - 1, 1.0, 0.0) for i in index]
    return not_first, not_last


def rim_kernel(rows, tiles, edge, depth, *refs):
    column_refs, (message_ref, far_ref, flow_ref, first_ref) = refs[:rows], refs[rows:]
    patterns = message_ref.shape[1]
    span = tiles * edge
    not_first, not_last = row_masks(rows)
    start = [ref[span : 2 * span] for ref in column_refs]
    folds = [ref[2 * span : 2 * span + depth] for ref in column_refs]
    base = 2 * span + depth
    gains = jnp.concatenate([ref[base : base + 1] for ref in column_refs], axis=0)
    columns = turned(gains)
    first = sum(ref[base + 1 : base + 2] for ref in column_refs)
    south = [
        columns[span : 2 * span, k : k + 1] * (start[k] - start[(k + 1) % rows] * not_last[k])
        for k in range(rows)
    ]
    dropped = jnp.zeros((span, patterns), jnp.float32)
    stride = span + depth
    for k in range(rows):
        flow = south[k] - south[k - 1] * not_first[k]
        raw = column_refs[k][:span]
        rim = raw - dot3(corners(folds[k], tiles, edge), flow)
        dropped = dropped + flow * (raw + rim)
        message_ref[k * stride : k * stride + span] = rim
        message_ref[k * stride + span : (k + 1) * stride] = folds[k]
        far_ref[k * edge : (k + 1) * edge] = rim[:edge]
        if k == 0:
            flow_ref[...] = flow
    message_ref[rows * stride : rows * stride + rows] = gains
    if message_ref.shape[0] > rows * stride + rows:
        rest_rows = message_ref.shape[0] - rows * stride - rows
        message_ref[rows * stride + rows :] = jnp.zeros((rest_rows, patterns), jnp.float32)
    first = first - jnp.sum(dropped, axis=0, keepdims=True)
    first_ref[...] = jnp.broadcast_to(first, first_ref.shape)


def moment_kernel(
    rows,
    cols,
    tiles,
    edge,
    depth,
    own_ref,
    inner_ref,
    outer_ref,
    far_ref,
    first_ref,
    moment_ref,
    t0_ref,
    t1_ref,
):
    patterns = own_ref.shape[1]
    mine = lax.axis_index("col")
    odd = mine % 2 == 1
    has_west = jnp.where(mine > 0, 1.0, 0.0)
    has_east = jnp.where(mine < cols - 1, 1.0, 0.0)
    has_far = jnp.where(mine < cols - 2, 1.0, 0.0)
    not_first, not_last = row_masks(rows)
    span = tiles * edge
    stride = span + depth

    def sides(piece):
        west = jnp.where(odd, inner_ref[piece], outer_ref[piece]) * has_west
        east = jnp.where(odd, outer_ref[piece], inner_ref[piece]) * has_east
        return west, own_ref[piece], east

    gains = [turned(block) for block in sides(slice(rows * stride, None))]
    easts, souths, u0, mats = [], [], [], []
    for k in range(rows):
        blocks = sides(slice(k * stride, (k + 1) * stride))
        far = far_ref[k * edge : (k + 1) * edge] * has_far
        u0.append(
            [block[t * edge : (t + 1) * edge] for block in blocks for t in range(tiles)] + [far]
        )

        def gain(columns, base):
            return jnp.broadcast_to(columns[base : base + edge, k : k + 1], (edge, patterns))

        easts.append([gain(g, t * edge) for g in gains for t in range(tiles)])
        souths.append([gain(g, span + t * edge) for g in gains for t in range(tiles)])
        mats.append([corners(block[span:], tiles, edge) for block in blocks])

    def net_flow(rims, low, high):
        flows = []
        for k in range(rows):
            below, above = (k + 1) % rows, k - 1
            row = []
            for c in range(low, high):
                flow = easts[k][c] * (rims[k][c] - rims[k][c + 1])
                flow = flow - easts[k][c - 1] * (rims[k][c - 1] - rims[k][c])
                flow = flow + souths[k][c] * (rims[k][c] - rims[below][c] * not_last[k])
                back = souths[above][c] * (rims[k][c] - rims[above][c])
                row.append(flow + back * not_first[k])
            flows.append([None] * low + row)
        return flows

    def spread(flows, devices, low, high):
        out = []
        for k in range(rows):
            row = []
            for d in devices:
                block = [
                    flows[k][c] if low <= c < high else jnp.zeros((edge, patterns), jnp.float32)
                    for c in range(d * tiles, (d + 1) * tiles)
                ]
                block = dot3(mats[k][d], jnp.concatenate(block, axis=0))
                row += [block[t * edge : (t + 1) * edge] for t in range(tiles)]
            out.append([None] * (devices[0] * tiles) + row)
        return out

    t0 = net_flow(u0, tiles - 1, 3 * tiles)
    u1 = spread(t0, [0, 1, 2], tiles - 1, 3 * tiles)
    t1 = net_flow(u1, tiles, 2 * tiles + 1)
    u2 = spread(t1, [1, 2], tiles, 2 * tiles + 1)
    zero = jnp.zeros((edge, patterns), jnp.float32)
    sums = [zero] * 5
    for k in range(rows):
        for c in range(tiles, 2 * tiles):
            ahead = u2[k][c] - u2[k][c + 1]
            drop = u2[k][c] - u2[(k + 1) % rows][c] * not_last[k]
            parts = (
                u0[k][c] * t0[k][c],
                u1[k][c] * t0[k][c],
                u1[k][c] * t1[k][c],
                u2[k][c] * t1[k][c],
                easts[k][c] * ahead * ahead + souths[k][c] * drop * drop,
            )
            sums = [total + part for total, part in zip(sums, parts)]
    moment_ref[0:1] = first_ref[0:1]
    for i, total in enumerate(sums):
        moment_ref[i + 1 : i + 2] = jnp.sum(total, axis=0, keepdims=True)
    moment_ref[6:8] = jnp.zeros((2, patterns), jnp.float32)
    t0_ref[...] = jnp.concatenate(t0[0][tiles : 2 * tiles], axis=0)
    t1_ref[...] = jnp.concatenate(t1[0][tiles : 2 * tiles], axis=0)


def direction_kernel(edge, precond_ref, inverse_ref, flow_ref, t0_ref, t1_ref, *out_refs):
    for t in range(precond_ref.shape[0]):
        rim = slice(t * edge, (t + 1) * edge)
        flows = jnp.concatenate([flow_ref[rim], t0_ref[rim], t1_ref[rim]], axis=1)
        spread = dot3(inverse_ref[t, :, :edge], flows)
        width = spread.shape[1] // 3
        out_refs[0][t] = precond_ref[t] - spread[:, :width]
        out_refs[1][t] = spread[:, width : 2 * width]
        out_refs[2][t] = spread[:, 2 * width :]


def final_kernel(volt_ref, z0_ref, z1_ref, z2_ref, *refs):
    *sum_refs, out_ref = refs
    tiles = volt_ref.shape[0]
    sums = sum(ref[...] for ref in sum_refs)
    m = [sums[i : i + 1] for i in range(6)]
    a00, a01, a02 = m[0] + m[1], m[1] + m[2], m[2] + m[3]
    a12, a22 = m[3] + m[4], m[4] + m[5]
    l1, l2 = a01 / a00, a02 / a00
    d1 = a02 - l1 * a01
    e12 = a12 - l2 * a01
    l12 = e12 / d1
    d2 = a22 - l2 * a02 - l12 * e12
    y1 = m[1] - l1 * m[0]
    y2 = m[2] - l2 * m[0] - l12 * y1
    c2 = y2 / d2
    c1 = y1 / d1 - l12 * c2
    c0 = m[0] / a00 - l1 * c1 - l2 * c2
    for t in range(tiles):
        out_ref[t] = volt_ref[t] + c0 * z0_ref[t] + c1 * z1_ref[t] + c2 * z2_ref[t]


def other(block, axis, count, distance):
    return lax.ppermute(block, axis, [(i, i ^ distance) for i in range(count)])


def stages(count, held):
    while held < count:
        reach = 2 if (count // held).bit_length() % 2 == 0 else 4
        yield [held * k for k in range(1, reach)]
        held *= reach


def outer_swap(block, axis, count):
    pairs = [(i, (i + 1) % count if i % 2 else (i - 1) % count) for i in range(count)]
    return lax.ppermute(block, axis, pairs)


def local(
    initial_voltage,
    inject,
    conduct,
    capacitance,
    track_gain,
    driver_tile,
    sink_net,
    sink_count,
    sink_tile,
    sink_node,
    sink_gain,
):
    rows, cols = lax.axis_size("row"), lax.axis_size("col")
    tiles, nodes, patterns = initial_voltage.shape[1:]
    edge, nets = track_gain.shape[-1], driver_tile.shape[-1]
    slots = cols * sink_net.shape[-1]
    voltage = initial_voltage[0]
    field = (tiles, nodes, patterns)
    span = tiles * edge

    mate = other(initial_voltage, "col", cols, 1)[0]
    mate_driver = other(driver_tile, "col", cols, 1)[0]
    mate_gain = other(track_gain, "col", cols, 1)[0]
    eye = run(eye_kernel, [(nodes, nodes)])[0]
    narrow_type = functools.partial(jax.ShapeDtypeStruct, dtype=jnp.bfloat16)
    rest, gains, take, put, scale, picked = run(
        functools.partial(sink_kernel, nets, edge),
        [
            field,
            (edge + 8, patterns),
            narrow_type((slots, cols * nets)),
            narrow_type((slots, tiles * nodes)),
            (slots, patterns),
            (nets, patterns),
        ],
        conduct[0],
        voltage,
        inject[0],
        track_gain[0],
        sink_net[0, 0],
        sink_count[0],
        sink_tile[0, 0],
        sink_node[0, 0],
        sink_gain[0, 0],
        driver_tile[0],
    )
    pair = run(
        functools.partial(pair_kernel, nets, edge),
        [(2 * nets + edge + 8, patterns)],
        voltage,
        picked,
        mate,
        mate_driver,
        mate_gain,
    )[0]
    groups = [pair]
    for distances in stages(cols, 2):
        whole = groups[0] if len(groups) == 1 else jnp.concatenate(groups)
        groups = [whole] + [other(whole, "col", cols, d) for d in distances]
    depth = tiles * edge * edge // nodes
    inverse, fold = run(
        functools.partial(tile_kernel, edge),
        [field, (depth, nodes)],
        eye,
        conduct[0],
        capacitance[0],
        pair,
        scratch=[pltpu.VMEM(field, jnp.float32)] * 2,
    )

    message, precond = run(
        functools.partial(residual_kernel, nets, edge, cols),
        [(2 * span + depth + 8, patterns), field],
        voltage,
        mate,
        mate_gain,
        inverse,
        fold,
        rest,
        gains,
        take,
        put,
        scale,
        *groups,
    )

    column = [message] + [
        lax.ppermute(message, "row", [((i + k) % rows, i) for i in range(rows)])
        for k in range(1, rows)
    ]
    height = rows * (span + depth) + -(-rows // 8) * 8
    message, far, flow, first = run(
        functools.partial(rim_kernel, rows, tiles, edge, depth),
        [(height, patterns), (rows * edge, patterns), (span, patterns), (8, patterns)],
        *column,
    )

    inner = other(message, "col", cols, 1)
    beyond = outer_swap(message, "col", cols)
    far = lax.ppermute(far, "col", [((i + 2) % cols, i) for i in range(cols)])
    moments, t0, t1 = run(
        functools.partial(moment_kernel, rows, cols, tiles, edge, depth),
        [(8, patterns), (span, patterns), (span, patterns)],
        message,
        inner,
        beyond,
        far,
        first,
    )

    sums = [moments]
    for distances in stages(cols, 1):
        moments = sum(sums[1:], sums[0])
        sums = [moments] + [other(moments, "col", cols, d) for d in distances]
    directions = run(
        functools.partial(direction_kernel, edge), [field] * 3, precond, inverse, flow, t0, t1
    )
    return run(final_kernel, [field], voltage, *directions, *sums)[0][None]


def solution(mesh):
    whole = P("row", "col", None, None)
    third = P("row", "col", None)
    placed = (whole, whole, whole, third, whole, third, whole, third, whole, whole, whole)
    return jax.shard_map(local, mesh=mesh, in_specs=placed, out_specs=whole, check_vma=False)
```

```python
import functools

import jax
import jax.numpy as jnp
from jax import lax
from jax.experimental import pallas as pl
from jax.experimental.pallas import tpu as pltpu
from jax.sharding import PartitionSpec as P

DOUBLINGS = 5
SMALL = 2.0**-13
VMEM_BYTES = 16 * 1024 * 1024

dot = functools.partial(
    jnp.dot, precision=lax.Precision.HIGHEST, preferred_element_type=jnp.float32
)


def split(block):
    high = block.astype(jnp.bfloat16)
    return high, (block - high.astype(jnp.float32)).astype(jnp.bfloat16)


def narrow(left, right):
    return jnp.dot(left, right, preferred_element_type=jnp.float32)


def dot3(left, right):
    (left_high, left_low), (right_high, right_low) = split(left), split(right)
    return narrow(left_high, right_high) + (
        narrow(left_high, right_low) + narrow(left_low, right_high)
    )


def select(onehot, block):
    high = block.astype(jnp.bfloat16)
    rest = block - high.astype(jnp.float32)
    middle, low = split(rest)
    return narrow(onehot, high) + (narrow(onehot, middle) + narrow(onehot, low))


def run(kernel, outs, *args, scratch=(), flops=4_000_000_000):
    vmem = pl.BlockSpec(memory_space=pltpu.VMEM)
    shapes = tuple(
        o if isinstance(o, jax.ShapeDtypeStruct) else jax.ShapeDtypeStruct(o, jnp.float32)
        for o in outs
    )
    moved = sum(4 * a.size for a in args) + sum(4 * s.size for s in shapes)
    return pl.pallas_call(
        kernel,
        out_shape=shapes,
        in_specs=[vmem] * len(args),
        out_specs=(vmem,) * len(shapes),
        scratch_shapes=list(scratch),
        compiler_params=pltpu.CompilerParams(vmem_limit_bytes=VMEM_BYTES),
        cost_estimate=pl.CostEstimate(flops=flops, bytes_accessed=moved, transcendentals=0),
    )(*args)


def iota(shape, axis):
    return lax.broadcasted_iota(jnp.int32, shape, axis)


def to_column(row):
    count = row.shape[1]
    square = jnp.broadcast_to(row, (count, count))
    keep = iota((count, count), 0) == iota((count, count), 1)
    return jnp.sum(jnp.where(keep, square, 0.0), axis=1, keepdims=True)


def slot_column(table):
    sources, slots = table.shape
    spread = jnp.concatenate(
        [jnp.broadcast_to(table[s : s + 1], (slots, slots)) for s in range(sources)], axis=0
    )
    keep = iota(spread.shape, 0) % slots == iota(spread.shape, 1)
    return jnp.sum(jnp.where(keep, spread, 0.0), axis=1, keepdims=True)


def source_column(row, slots):
    sources = row.shape[1]
    spread = jnp.broadcast_to(row, (sources * slots, sources))
    keep = iota(spread.shape, 0) // slots == iota(spread.shape, 1)
    return jnp.sum(jnp.where(keep, spread, 0.0), axis=1, keepdims=True)


def pair_kernel(nets, edge, volt_ref, picked_ref, mate_ref, mate_driver_ref, mate_gain_ref, out_ref):
    tiles, nodes, patterns = volt_ref.shape
    odd = lax.axis_index("col") % 2 == 1
    mate_picked = to_column(mate_driver_ref[...].astype(jnp.float32))
    for i, (field, picked) in enumerate(((volt_ref, picked_ref[...]), (mate_ref, mate_picked))):
        rows = jnp.zeros((nets, patterns), jnp.float32)
        for t in range(tiles):
            block = jnp.concatenate([field[t]] * (-(-nets // nodes)), axis=0)[:nets]
            rows = jnp.where(picked == t, block, rows)
        out_ref[i * nets : (i + 1) * nets] = rows
    base = 2 * nets
    out_ref[base : base + edge] = jnp.where(odd, mate_ref[0, :edge], mate_ref[tiles - 1, :edge])
    out_ref[base + edge :] = jnp.zeros((8, patterns), jnp.float32)
    out_ref[base + edge : base + edge + 1, :edge] = mate_gain_ref[tiles - 1, 0:1]


def eye_kernel(out_ref):
    out_ref[...] = jnp.where(iota(out_ref.shape, 0) == iota(out_ref.shape, 1), 1.0, 0.0)


def sink_kernel(
    nets,
    edge,
    eye_ref,
    conduct_ref,
    volt_ref,
    inject_ref,
    gain_ref,
    net_ref,
    count_ref,
    tile_ref,
    node_ref,
    weight_ref,
    driver_ref,
    rest_ref,
    gains_ref,
    take_ref,
    put_ref,
    scale_ref,
    picked_ref,
):
    picked_ref[...] = jnp.broadcast_to(
        to_column(driver_ref[...].astype(jnp.float32)), picked_ref.shape
    )
    tiles, nodes = conduct_ref.shape[0], conduct_ref.shape[1]
    for t in range(tiles):
        rest_ref[t] = inject_ref[t] - dot(conduct_ref[t], volt_ref[t])
    lane = iota((edge, nodes), 1)
    table = jnp.zeros((edge, nodes), jnp.float32)
    gains_ref[edge:] = jnp.zeros((8, nodes), jnp.float32)
    for side in range(2):
        for t in range(tiles):
            i = side * tiles + t
            gain = gain_ref[t, side : side + 1]
            table = jnp.where(lane == i, to_column(gain), table)
            gains_ref[edge : edge + 1, i * edge : (i + 1) * edge] = gain
    gains_ref[:edge] = table

    sources, slots = net_ref.shape
    mine = lax.axis_index("col")
    block = iota((sources, slots), 0) ^ mine
    place = slot_column((block * nets + net_ref[...]).astype(jnp.float32))
    target = slot_column((tile_ref[...] * nodes + node_ref[...]).astype(jnp.float32))
    live = source_column(count_ref[...].astype(jnp.float32), slots)
    slot = (iota(live.shape, 0) % slots).astype(jnp.float32)
    weight = jnp.where(slot < live, slot_column(weight_ref[...]), 0.0)
    take = jnp.where(place == iota(take_ref.shape, 1).astype(jnp.float32), 1.0, 0.0)
    put = jnp.where(target == iota(put_ref.shape, 1).astype(jnp.float32), 1.0, 0.0)
    take_ref[...] = take.astype(jnp.bfloat16)
    put_ref[...] = put.astype(jnp.bfloat16)
    scale_ref[...] = jnp.broadcast_to(weight, scale_ref.shape)


def tile_kernel(edge, eye_ref, conduct_ref, cap_ref, after_ref, inverse_ref, fold_ref, sum_ref, power_ref):
    tiles, nodes = conduct_ref.shape[0], conduct_ref.shape[1]
    eye = eye_ref[...]
    sums, powers, scales = [], [], []
    for t in range(tiles):
        conduct = conduct_ref[t]
        diagonal = (conduct + cap_ref[t : t + 1, :]) * eye
        down = jnp.sum(diagonal, axis=1, keepdims=True)
        across = jnp.sum(diagonal, axis=0, keepdims=True)
        power = (conduct * eye - conduct) / down
        sums.append(eye + power)
        powers.append(dot(power, power))
        scales.append(1.0 / across)

    def step(sums, powers):
        out_sums, out_powers, largest = [], [], jnp.float32(0.0)
        for total, power in zip(sums, powers):
            both = dot(jnp.concatenate([total, power], axis=0), power)
            out_sums.append(total + both[:nodes])
            out_powers.append(both[nodes:])
            largest = jnp.maximum(largest, jnp.max(jnp.sum(power, axis=1)))
        return out_sums, out_powers, largest

    for _ in range(DOUBLINGS):
        sums, powers, largest = step(sums, powers)
    for t in range(tiles):
        sum_ref[t], power_ref[t] = sums[t], powers[t]

    def again(carry):
        sums, powers, largest = step(
            [sum_ref[t] for t in range(tiles)], [power_ref[t] for t in range(tiles)]
        )
        for t in range(tiles):
            sum_ref[t], power_ref[t] = sums[t], powers[t]
        return largest, carry[1] + 1

    lax.while_loop(
        lambda carry: (carry[0] > SMALL) & (carry[1] < 40), again, (largest, jnp.int32(0))
    )
    parts = nodes // edge
    depth = edge // parts
    lane = iota((depth, nodes), 1)
    for t in range(tiles):
        inverse = sum_ref[t] * scales[t]
        inverse_ref[t] = inverse
        fold = jnp.zeros((depth, nodes), jnp.float32)
        for j in range(parts):
            piece = jnp.where(lane < edge, inverse[j * depth : (j + 1) * depth], 0.0)
            fold = fold + (pltpu.roll(piece, j * edge, 1) if j else piece)
        fold_ref[t * depth : (t + 1) * depth] = fold


def residual_kernel(
    nets,
    edge,
    cols,
    volt_ref,
    mate_ref,
    mate_gain_ref,
    inverse_ref,
    fold_ref,
    rest_ref,
    gains_ref,
    take_ref,
    put_ref,
    scale_ref,
    *refs,
):
    *group_refs, message_ref, precond_ref = refs
    tiles, nodes, patterns = volt_ref.shape
    mine = lax.axis_index("col")
    odd = mine % 2 == 1
    stride = 2 * nets + edge + 8
    blocks = [(ref, base) for ref in group_refs for base in range(0, ref.shape[0], stride)]
    values = sum(
        select(take_ref[:, j * 2 * nets : (j + 1) * 2 * nets], ref[base : base + 2 * nets])
        for j, (ref, base) in enumerate(blocks)
    )
    values = values * scale_ref[...]
    beyond = lax.rem(jnp.where(odd, mine + 1, mine + cols - 1), cols) ^ 1
    which = (mine ^ beyond) // 2
    outer = jnp.zeros((edge + 8, patterns), jnp.float32)
    for j, (ref, base) in enumerate(blocks):
        outer = jnp.where(which == j, ref[base + 2 * nets : base + stride], outer)
    inner = jnp.where(odd, mate_ref[tiles - 1, :edge], mate_ref[0, :edge])
    inner_gain = to_column(mate_gain_ref[tiles - 1, 0:1])
    has_west = jnp.where(mine > 0, 1.0, 0.0)
    has_east = jnp.where(mine < cols - 1, 1.0, 0.0)
    west = jnp.where(odd, inner, outer[:edge]) * has_west
    east = jnp.where(odd, outer[:edge], inner) * has_east
    west_gain = jnp.where(odd, inner_gain, to_column(outer[edge : edge + 1, :edge])) * has_west
    gains = [west_gain] + [gains_ref[:edge, t : t + 1] for t in range(tiles)]
    rims = [west] + [volt_ref[t, :edge] for t in range(tiles)] + [east]
    flows = [gains[t] * (rims[t] - rims[t + 1]) for t in range(tiles + 1)]
    first = jnp.zeros((1, patterns), jnp.float32)
    high, low = split(values)
    for t in range(tiles):
        put = put_ref[:, t * nodes : (t + 1) * nodes]
        injected = sum(
            lax.dot_general(
                put, part, (((0,), (0,)), ((), ())), preferred_element_type=jnp.float32
            )
            for part in (high, low)
        )
        residual = rest_ref[t] + injected
        residual = jnp.concatenate(
            [residual[:edge] - (flows[t + 1] - flows[t]), residual[edge:]], axis=0
        )
        precond = dot3(inverse_ref[t], residual)
        precond_ref[t] = precond
        first = first + jnp.sum(residual * precond, axis=0, keepdims=True)
        message_ref[t * edge : (t + 1) * edge] = precond[:edge]
        message_ref[(tiles + t) * edge : (tiles + t + 1) * edge] = volt_ref[t, :edge]
    base = 2 * tiles * edge
    depth = fold_ref.shape[0]
    message_ref[base : base + depth] = fold_ref[...]
    message_ref[base + depth : base + depth + 8] = gains_ref[edge:]
    message_ref[base + depth + 1 : base + depth + 2] = first


def corners(fold, tiles, edge):
    depth, lanes = fold.shape[0] // tiles, fold.shape[1]
    lane = iota((depth, lanes), 1)
    rows = []
    for t in range(tiles):
        piece = fold[t * depth : (t + 1) * depth]
        for j in range(lanes // edge):
            turn = (t - j) * edge % lanes
            turned = pltpu.roll(piece, turn, 1) if turn else piece
            rows.append(jnp.where((lane >= t * edge) & (lane < (t + 1) * edge), turned, 0.0))
    return jnp.concatenate(rows, axis=0)[:, : tiles * edge]


def turned(rows):
    count, lanes = rows.shape
    full = jnp.concatenate([rows, jnp.zeros((lanes - count, lanes), jnp.float32)], axis=0)
    return jnp.transpose(full)


def row_masks(rows):
    place = lax.axis_index("row")
    index = [lax.rem(place + k, rows) for k in range(rows)]
    not_first = [jnp.where(i > 0, 1.0, 0.0) for i in index]
    not_last = [jnp.where(i < rows - 1, 1.0, 0.0) for i in index]
    return not_first, not_last


def rim_kernel(rows, tiles, edge, depth, *refs):
    column_refs, (message_ref, far_ref, flow_ref, first_ref) = refs[:rows], refs[rows:]
    patterns = message_ref.shape[1]
    span = tiles * edge
    not_first, not_last = row_masks(rows)
    start = [ref[span : 2 * span] for ref in column_refs]
    folds = [ref[2 * span : 2 * span + depth] for ref in column_refs]
    base = 2 * span + depth
    gains = jnp.concatenate([ref[base : base + 1] for ref in column_refs], axis=0)
    columns = turned(gains)
    first = sum(ref[base + 1 : base + 2] for ref in column_refs)
    south = [
        columns[span : 2 * span, k : k + 1] * (start[k] - start[(k + 1) % rows] * not_last[k])
        for k in range(rows)
    ]
    dropped = jnp.zeros((span, patterns), jnp.float32)
    stride = span + depth
    for k in range(rows):
        flow = south[k] - south[k - 1] * not_first[k]
        raw = column_refs[k][:span]
        rim = raw - dot3(corners(folds[k], tiles, edge), flow)
        dropped = dropped + flow * (raw + rim)
        message_ref[k * stride : k * stride + span] = rim
        message_ref[k * stride + span : (k + 1) * stride] = folds[k]
        far_ref[k * edge : (k + 1) * edge] = rim[:edge]
        if k == 0:
            flow_ref[...] = flow
    message_ref[rows * stride : rows * stride + rows] = gains
    if message_ref.shape[0] > rows * stride + rows:
        rest_rows = message_ref.shape[0] - rows * stride - rows
        message_ref[rows * stride + rows :] = jnp.zeros((rest_rows, patterns), jnp.float32)
    first = first - jnp.sum(dropped, axis=0, keepdims=True)
    first_ref[...] = jnp.broadcast_to(first, first_ref.shape)


def moment_kernel(
    rows,
    cols,
    tiles,
    edge,
    depth,
    own_ref,
    inner_ref,
    outer_ref,
    far_ref,
    first_ref,
    moment_ref,
    t0_ref,
    t1_ref,
):
    patterns = own_ref.shape[1]
    mine = lax.axis_index("col")
    odd = mine % 2 == 1
    has_west = jnp.where(mine > 0, 1.0, 0.0)
    has_east = jnp.where(mine < cols - 1, 1.0, 0.0)
    has_far = jnp.where(mine < cols - 2, 1.0, 0.0)
    not_first, not_last = row_masks(rows)
    span = tiles * edge
    stride = span + depth

    def sides(piece):
        west = jnp.where(odd, inner_ref[piece], outer_ref[piece]) * has_west
        east = jnp.where(odd, outer_ref[piece], inner_ref[piece]) * has_east
        return west, own_ref[piece], east

    gains = [turned(block) for block in sides(slice(rows * stride, None))]
    easts, souths, u0, mats = [], [], [], []
    for k in range(rows):
        blocks = sides(slice(k * stride, (k + 1) * stride))
        far = far_ref[k * edge : (k + 1) * edge] * has_far
        u0.append(
            [block[t * edge : (t + 1) * edge] for block in blocks for t in range(tiles)] + [far]
        )

        def gain(columns, base):
            return jnp.broadcast_to(columns[base : base + edge, k : k + 1], (edge, patterns))

        easts.append([gain(g, t * edge) for g in gains for t in range(tiles)])
        souths.append([gain(g, span + t * edge) for g in gains for t in range(tiles)])
        mats.append([corners(block[span:], tiles, edge) for block in blocks])

    def net_flow(rims, low, high):
        flows = []
        for k in range(rows):
            below, above = (k + 1) % rows, k - 1
            row = []
            for c in range(low, high):
                flow = easts[k][c] * (rims[k][c] - rims[k][c + 1])
                flow = flow - easts[k][c - 1] * (rims[k][c - 1] - rims[k][c])
                flow = flow + souths[k][c] * (rims[k][c] - rims[below][c] * not_last[k])
                back = souths[above][c] * (rims[k][c] - rims[above][c])
                row.append(flow + back * not_first[k])
            flows.append([None] * low + row)
        return flows

    def spread(flows, devices, low, high):
        out = []
        for k in range(rows):
            row = []
            for d in devices:
                block = [
                    flows[k][c] if low <= c < high else jnp.zeros((edge, patterns), jnp.float32)
                    for c in range(d * tiles, (d + 1) * tiles)
                ]
                block = dot3(mats[k][d], jnp.concatenate(block, axis=0))
                row += [block[t * edge : (t + 1) * edge] for t in range(tiles)]
            out.append([None] * (devices[0] * tiles) + row)
        return out

    t0 = net_flow(u0, tiles - 1, 3 * tiles)
    u1 = spread(t0, [0, 1, 2], tiles - 1, 3 * tiles)
    t1 = net_flow(u1, tiles, 2 * tiles + 1)
    u2 = spread(t1, [1, 2], tiles, 2 * tiles + 1)
    zero = jnp.zeros((edge, patterns), jnp.float32)
    sums = [zero] * 5
    for k in range(rows):
        for c in range(tiles, 2 * tiles):
            ahead = u2[k][c] - u2[k][c + 1]
            drop = u2[k][c] - u2[(k + 1) % rows][c] * not_last[k]
            parts = (
                u0[k][c] * t0[k][c],
                u1[k][c] * t0[k][c],
                u1[k][c] * t1[k][c],
                u2[k][c] * t1[k][c],
                easts[k][c] * ahead * ahead + souths[k][c] * drop * drop,
            )
            sums = [total + part for total, part in zip(sums, parts)]
    moment_ref[0:1] = first_ref[0:1]
    for i, total in enumerate(sums):
        moment_ref[i + 1 : i + 2] = jnp.sum(total, axis=0, keepdims=True)
    moment_ref[6:8] = jnp.zeros((2, patterns), jnp.float32)
    t0_ref[...] = jnp.concatenate(t0[0][tiles : 2 * tiles], axis=0)
    t1_ref[...] = jnp.concatenate(t1[0][tiles : 2 * tiles], axis=0)


def direction_kernel(edge, precond_ref, inverse_ref, flow_ref, t0_ref, t1_ref, *out_refs):
    for t in range(precond_ref.shape[0]):
        rim = slice(t * edge, (t + 1) * edge)
        flows = jnp.concatenate([flow_ref[rim], t0_ref[rim], t1_ref[rim]], axis=1)
        spread = dot3(inverse_ref[t, :, :edge], flows)
        width = spread.shape[1] // 3
        out_refs[0][t] = precond_ref[t] - spread[:, :width]
        out_refs[1][t] = spread[:, width : 2 * width]
        out_refs[2][t] = spread[:, 2 * width :]


def final_kernel(volt_ref, z0_ref, z1_ref, z2_ref, *refs):
    *sum_refs, out_ref = refs
    tiles = volt_ref.shape[0]
    sums = sum(ref[...] for ref in sum_refs)
    m = [sums[i : i + 1] for i in range(6)]
    a00, a01, a02 = m[0] + m[1], m[1] + m[2], m[2] + m[3]
    a12, a22 = m[3] + m[4], m[4] + m[5]
    l1, l2 = a01 / a00, a02 / a00
    d1 = a02 - l1 * a01
    e12 = a12 - l2 * a01
    l12 = e12 / d1
    d2 = a22 - l2 * a02 - l12 * e12
    y1 = m[1] - l1 * m[0]
    y2 = m[2] - l2 * m[0] - l12 * y1
    c2 = y2 / d2
    c1 = y1 / d1 - l12 * c2
    c0 = m[0] / a00 - l1 * c1 - l2 * c2
    for t in range(tiles):
        out_ref[t] = volt_ref[t] + c0 * z0_ref[t] + c1 * z1_ref[t] + c2 * z2_ref[t]


def other(block, axis, count, distance):
    return lax.ppermute(block, axis, [(i, i ^ distance) for i in range(count)])


def stages(count, held):
    while held < count:
        reach = 2 if (count // held).bit_length() % 2 == 0 else 4
        yield [held * k for k in range(1, reach)]
        held *= reach


def sum_stages(block, axis, count):
    held, terms = 2, [block]
    while held < count:
        block = sum(terms[1:], terms[0])
        if (count // held).bit_length() % 2 == 0:
            terms = [block, other(block, axis, count, held)]
            held *= 2
            continue
        route = [(i, i ^ (2 * held if i % 2 else held)) for i in range(count)]
        brought = lax.ppermute(block, axis, route)
        third = other(block, axis, count, 3 * held)
        brought, third = lax.optimization_barrier((brought, third))
        terms = [block, brought, third, other(brought, axis, count, 1)]
        held *= 4
    return terms


def outer_swap(block, axis, count):
    pairs = [(i, (i + 1) % count if i % 2 else (i - 1) % count) for i in range(count)]
    return lax.ppermute(block, axis, pairs)


def local(
    initial_voltage,
    inject,
    conduct,
    capacitance,
    track_gain,
    driver_tile,
    sink_net,
    sink_count,
    sink_tile,
    sink_node,
    sink_gain,
):
    rows, cols = lax.axis_size("row"), lax.axis_size("col")
    tiles, nodes, patterns = initial_voltage.shape[1:]
    edge, nets = track_gain.shape[-1], driver_tile.shape[-1]
    slots = cols * sink_net.shape[-1]
    voltage = initial_voltage[0]
    field = (tiles, nodes, patterns)
    span = tiles * edge

    mate = other(initial_voltage, "col", cols, 1)[0]
    mate_driver = other(driver_tile, "col", cols, 1)[0]
    mate_gain = other(track_gain, "col", cols, 1)[0]
    eye = run(eye_kernel, [(nodes, nodes)])[0]
    narrow_type = functools.partial(jax.ShapeDtypeStruct, dtype=jnp.bfloat16)
    rest, gains, take, put, scale, picked = run(
        functools.partial(sink_kernel, nets, edge),
        [
            field,
            (edge + 8, patterns),
            narrow_type((slots, cols * nets)),
            narrow_type((slots, tiles * nodes)),
            (slots, patterns),
            (nets, patterns),
        ],
        eye,
        conduct[0],
        voltage,
        inject[0],
        track_gain[0],
        sink_net[0, 0],
        sink_count[0],
        sink_tile[0, 0],
        sink_node[0, 0],
        sink_gain[0, 0],
        driver_tile[0],
    )
    pair = run(
        functools.partial(pair_kernel, nets, edge),
        [(2 * nets + edge + 8, patterns)],
        voltage,
        picked,
        mate,
        mate_driver,
        mate_gain,
    )[0]
    groups = [pair]
    for distances in stages(cols, 2):
        whole = groups[0] if len(groups) == 1 else jnp.concatenate(groups)
        groups = [whole] + [other(whole, "col", cols, d) for d in distances]
    depth = tiles * edge * edge // nodes
    inverse, fold = run(
        functools.partial(tile_kernel, edge),
        [field, (depth, nodes)],
        eye,
        conduct[0],
        capacitance[0],
        pair,
        scratch=[pltpu.VMEM(field, jnp.float32)] * 2,
    )

    message, precond = run(
        functools.partial(residual_kernel, nets, edge, cols),
        [(2 * span + depth + 8, patterns), field],
        voltage,
        mate,
        mate_gain,
        inverse,
        fold,
        rest,
        gains,
        take,
        put,
        scale,
        *groups,
    )

    column = [message] + [
        lax.ppermute(message, "row", [((i + k) % rows, i) for i in range(rows)])
        for k in range(1, rows)
    ]
    height = rows * (span + depth) + -(-rows // 8) * 8
    message, far, flow, first = run(
        functools.partial(rim_kernel, rows, tiles, edge, depth),
        [(height, patterns), (rows * edge, patterns), (span, patterns), (8, patterns)],
        *column,
    )

    inner = other(message, "col", cols, 1)
    beyond = outer_swap(message, "col", cols)
    far = lax.ppermute(far, "col", [((i + 2) % cols, i) for i in range(cols)])
    moments, t0, t1 = run(
        functools.partial(moment_kernel, rows, cols, tiles, edge, depth),
        [(8, patterns), (span, patterns), (span, patterns)],
        message,
        inner,
        beyond,
        far,
        first,
    )

    sums = sum_stages(moments + other(moments, "col", cols, 1), "col", cols)
    directions = run(
        functools.partial(direction_kernel, edge), [field] * 3, precond, inverse, flow, t0, t1
    )
    return run(final_kernel, [field], voltage, *directions, *sums)[0][None]


def solution(mesh):
    whole = P("row", "col", None, None)
    third = P("row", "col", None)
    placed = (whole, whole, whole, third, whole, third, whole, third, whole, whole, whole)
    return jax.shard_map(local, mesh=mesh, in_specs=placed, out_specs=whole, check_vma=False)
```

```python
import functools

import jax
import jax.numpy as jnp
from jax import lax
from jax.experimental import pallas as pl
from jax.experimental.pallas import tpu as pltpu
from jax.sharding import PartitionSpec as P

DOUBLINGS = 5
SMALL = 2.0**-13
VMEM_BYTES = 16 * 1024 * 1024

dot = functools.partial(
    jnp.dot, precision=lax.Precision.HIGHEST, preferred_element_type=jnp.float32
)


def split(block):
    high = block.astype(jnp.bfloat16)
    return high, (block - high.astype(jnp.float32)).astype(jnp.bfloat16)


def narrow(left, right):
    return jnp.dot(left, right, preferred_element_type=jnp.float32)


def dot3(left, right):
    (left_high, left_low), (right_high, right_low) = split(left), split(right)
    return narrow(left_high, right_high) + (
        narrow(left_high, right_low) + narrow(left_low, right_high)
    )


def select(onehot, block):
    high = block.astype(jnp.bfloat16)
    rest = block - high.astype(jnp.float32)
    middle, low = split(rest)
    return narrow(onehot, high) + (narrow(onehot, middle) + narrow(onehot, low))


def run(kernel, outs, *args, scratch=(), flops=4_000_000_000):
    vmem = pl.BlockSpec(memory_space=pltpu.VMEM)
    shapes = tuple(
        o if isinstance(o, jax.ShapeDtypeStruct) else jax.ShapeDtypeStruct(o, jnp.float32)
        for o in outs
    )
    moved = sum(4 * a.size for a in args) + sum(4 * s.size for s in shapes)
    return pl.pallas_call(
        kernel,
        out_shape=shapes,
        in_specs=[vmem] * len(args),
        out_specs=(vmem,) * len(shapes),
        scratch_shapes=list(scratch),
        compiler_params=pltpu.CompilerParams(vmem_limit_bytes=VMEM_BYTES),
        cost_estimate=pl.CostEstimate(flops=flops, bytes_accessed=moved, transcendentals=0),
    )(*args)


def iota(shape, axis):
    return lax.broadcasted_iota(jnp.int32, shape, axis)


def to_column(row):
    count = row.shape[1]
    square = jnp.broadcast_to(row, (count, count))
    keep = iota((count, count), 0) == iota((count, count), 1)
    return jnp.sum(jnp.where(keep, square, 0.0), axis=1, keepdims=True)


def slot_column(table):
    sources, slots = table.shape
    spread = jnp.concatenate(
        [jnp.broadcast_to(table[s : s + 1], (slots, slots)) for s in range(sources)], axis=0
    )
    keep = iota(spread.shape, 0) % slots == iota(spread.shape, 1)
    return jnp.sum(jnp.where(keep, spread, 0.0), axis=1, keepdims=True)


def source_column(row, slots):
    sources = row.shape[1]
    spread = jnp.broadcast_to(row, (sources * slots, sources))
    keep = iota(spread.shape, 0) // slots == iota(spread.shape, 1)
    return jnp.sum(jnp.where(keep, spread, 0.0), axis=1, keepdims=True)


def pair_kernel(nets, edge, volt_ref, picked_ref, mate_ref, mate_driver_ref, mate_gain_ref, out_ref):
    tiles, nodes, patterns = volt_ref.shape
    odd = lax.axis_index("col") % 2 == 1
    mate_picked = to_column(mate_driver_ref[...].astype(jnp.float32))
    for i, (field, picked) in enumerate(((volt_ref, picked_ref[...]), (mate_ref, mate_picked))):
        rows = jnp.zeros((nets, patterns), jnp.float32)
        for t in range(tiles):
            block = jnp.concatenate([field[t]] * (-(-nets // nodes)), axis=0)[:nets]
            rows = jnp.where(picked == t, block, rows)
        out_ref[i * nets : (i + 1) * nets] = rows
    base = 2 * nets
    out_ref[base : base + edge] = jnp.where(odd, mate_ref[0, :edge], mate_ref[tiles - 1, :edge])
    out_ref[base + edge :] = jnp.zeros((8, patterns), jnp.float32)
    out_ref[base + edge : base + edge + 1, :edge] = mate_gain_ref[tiles - 1, 0:1]


def eye_kernel(out_ref):
    out_ref[...] = jnp.where(iota(out_ref.shape, 0) == iota(out_ref.shape, 1), 1.0, 0.0)


def sink_kernel(
    nets,
    edge,
    eye_ref,
    conduct_ref,
    volt_ref,
    inject_ref,
    gain_ref,
    net_ref,
    count_ref,
    tile_ref,
    node_ref,
    weight_ref,
    driver_ref,
    rest_ref,
    gains_ref,
    take_ref,
    put_ref,
    scale_ref,
    picked_ref,
):
    picked_ref[...] = jnp.broadcast_to(
        to_column(driver_ref[...].astype(jnp.float32)), picked_ref.shape
    )
    tiles, nodes = conduct_ref.shape[0], conduct_ref.shape[1]
    for t in range(tiles):
        rest_ref[t] = inject_ref[t] - dot(conduct_ref[t], volt_ref[t])
    lane = iota((edge, nodes), 1)
    table = jnp.zeros((edge, nodes), jnp.float32)
    gains_ref[edge:] = jnp.zeros((8, nodes), jnp.float32)
    for side in range(2):
        for t in range(tiles):
            i = side * tiles + t
            gain = gain_ref[t, side : side + 1]
            table = jnp.where(lane == i, to_column(gain), table)
            gains_ref[edge : edge + 1, i * edge : (i + 1) * edge] = gain
    gains_ref[:edge] = table

    sources, slots = net_ref.shape
    mine = lax.axis_index("col")
    block = iota((sources, slots), 0) ^ mine
    place = slot_column((block * nets + net_ref[...]).astype(jnp.float32))
    target = slot_column((tile_ref[...] * nodes + node_ref[...]).astype(jnp.float32))
    live = source_column(count_ref[...].astype(jnp.float32), slots)
    slot = (iota(live.shape, 0) % slots).astype(jnp.float32)
    weight = jnp.where(slot < live, slot_column(weight_ref[...]), 0.0)
    take = jnp.where(place == iota(take_ref.shape, 1).astype(jnp.float32), 1.0, 0.0)
    put = jnp.where(target == iota(put_ref.shape, 1).astype(jnp.float32), 1.0, 0.0)
    take_ref[...] = take.astype(jnp.bfloat16)
    put_ref[...] = put.astype(jnp.bfloat16)
    scale_ref[...] = jnp.broadcast_to(weight, scale_ref.shape)


def tile_kernel(
    edge,
    eye_ref,
    conduct_ref,
    cap_ref,
    rest_ref,
    put_ref,
    after_ref,
    inverse_ref,
    fold_ref,
    part_ref,
    reach_ref,
    sum_ref,
    power_ref,
):
    tiles, nodes = conduct_ref.shape[0], conduct_ref.shape[1]
    eye = eye_ref[...]
    sums, powers, scales = [], [], []
    for t in range(tiles):
        conduct = conduct_ref[t]
        diagonal = (conduct + cap_ref[t : t + 1, :]) * eye
        down = jnp.sum(diagonal, axis=1, keepdims=True)
        across = jnp.sum(diagonal, axis=0, keepdims=True)
        power = (conduct * eye - conduct) / down
        sums.append(eye + power)
        powers.append(dot(power, power))
        scales.append(1.0 / across)

    def step(sums, powers):
        out_sums, out_powers, largest = [], [], jnp.float32(0.0)
        for total, power in zip(sums, powers):
            both = dot(jnp.concatenate([total, power], axis=0), power)
            out_sums.append(total + both[:nodes])
            out_powers.append(both[nodes:])
            largest = jnp.maximum(largest, jnp.max(jnp.sum(power, axis=1)))
        return out_sums, out_powers, largest

    for _ in range(DOUBLINGS):
        sums, powers, largest = step(sums, powers)
    for t in range(tiles):
        sum_ref[t], power_ref[t] = sums[t], powers[t]

    def again(carry):
        sums, powers, largest = step(
            [sum_ref[t] for t in range(tiles)], [power_ref[t] for t in range(tiles)]
        )
        for t in range(tiles):
            sum_ref[t], power_ref[t] = sums[t], powers[t]
        return largest, carry[1] + 1

    lax.while_loop(
        lambda carry: (carry[0] > SMALL) & (carry[1] < 40), again, (largest, jnp.int32(0))
    )
    parts = nodes // edge
    depth = edge // parts
    lane = iota((depth, nodes), 1)
    for t in range(tiles):
        inverse = sum_ref[t] * scales[t]
        inverse_ref[t] = inverse
        fold = jnp.zeros((depth, nodes), jnp.float32)
        for j in range(parts):
            piece = jnp.where(lane < edge, inverse[j * depth : (j + 1) * depth], 0.0)
            fold = fold + (pltpu.roll(piece, j * edge, 1) if j else piece)
        fold_ref[t * depth : (t + 1) * depth] = fold
        part_ref[t] = dot3(inverse, rest_ref[t])
        put = put_ref[:, t * nodes : (t + 1) * nodes]
        reach_ref[t] = sum(
            lax.dot_general(
                piece, put, (((1,), (1,)), ((), ())), preferred_element_type=jnp.float32
            )
            for piece in split(inverse)
        )


def residual_kernel(
    nets,
    edge,
    cols,
    volt_ref,
    mate_ref,
    mate_gain_ref,
    inverse_ref,
    fold_ref,
    part_ref,
    reach_ref,
    rest_ref,
    gains_ref,
    take_ref,
    put_ref,
    scale_ref,
    *refs,
):
    *group_refs, message_ref, precond_ref = refs
    tiles, nodes, patterns = volt_ref.shape
    mine = lax.axis_index("col")
    odd = mine % 2 == 1
    stride = 2 * nets + edge + 8
    blocks = [(ref, base) for ref in group_refs for base in range(0, ref.shape[0], stride)]
    values = sum(
        select(take_ref[:, j * 2 * nets : (j + 1) * 2 * nets], ref[base : base + 2 * nets])
        for j, (ref, base) in enumerate(blocks)
    )
    values = values * scale_ref[...]
    beyond = lax.rem(jnp.where(odd, mine + 1, mine + cols - 1), cols) ^ 1
    which = (mine ^ beyond) // 2
    outer = jnp.zeros((edge + 8, patterns), jnp.float32)
    for j, (ref, base) in enumerate(blocks):
        outer = jnp.where(which == j, ref[base + 2 * nets : base + stride], outer)
    inner = jnp.where(odd, mate_ref[tiles - 1, :edge], mate_ref[0, :edge])
    inner_gain = to_column(mate_gain_ref[tiles - 1, 0:1])
    has_west = jnp.where(mine > 0, 1.0, 0.0)
    has_east = jnp.where(mine < cols - 1, 1.0, 0.0)
    west = jnp.where(odd, inner, outer[:edge]) * has_west
    east = jnp.where(odd, outer[:edge], inner) * has_east
    west_gain = jnp.where(odd, inner_gain, to_column(outer[edge : edge + 1, :edge])) * has_west
    gains = [west_gain] + [gains_ref[:edge, t : t + 1] for t in range(tiles)]
    rims = [west] + [volt_ref[t, :edge] for t in range(tiles)] + [east]
    flows = [gains[t] * (rims[t] - rims[t + 1]) for t in range(tiles + 1)]
    first = jnp.zeros((1, patterns), jnp.float32)
    high, low = split(values)
    for t in range(tiles):
        out = flows[t + 1] - flows[t]
        precond = part_ref[t] + (
            dot3(reach_ref[t], values) - dot3(inverse_ref[t, :, :edge], out)
        )
        put = put_ref[:, t * nodes : (t + 1) * nodes]
        injected = sum(
            lax.dot_general(
                put, part, (((0,), (0,)), ((), ())), preferred_element_type=jnp.float32
            )
            for part in (high, low)
        )
        residual = rest_ref[t] + injected
        residual = jnp.concatenate([residual[:edge] - out, residual[edge:]], axis=0)
        precond_ref[t] = precond
        first = first + jnp.sum(residual * precond, axis=0, keepdims=True)
        message_ref[t * edge : (t + 1) * edge] = precond[:edge]
        message_ref[(tiles + t) * edge : (tiles + t + 1) * edge] = volt_ref[t, :edge]
    base = 2 * tiles * edge
    depth = fold_ref.shape[0]
    message_ref[base : base + depth] = fold_ref[...]
    message_ref[base + depth : base + depth + 8] = gains_ref[edge:]
    message_ref[base + depth + 1 : base + depth + 2] = first


def corners(fold, tiles, edge):
    depth, lanes = fold.shape[0] // tiles, fold.shape[1]
    lane = iota((depth, lanes), 1)
    rows = []
    for t in range(tiles):
        piece = fold[t * depth : (t + 1) * depth]
        for j in range(lanes // edge):
            turn = (t - j) * edge % lanes
            turned = pltpu.roll(piece, turn, 1) if turn else piece
            rows.append(jnp.where((lane >= t * edge) & (lane < (t + 1) * edge), turned, 0.0))
    return jnp.concatenate(rows, axis=0)[:, : tiles * edge]


def turned(rows):
    count, lanes = rows.shape
    full = jnp.concatenate([rows, jnp.zeros((lanes - count, lanes), jnp.float32)], axis=0)
    return jnp.transpose(full)


def row_masks(rows):
    place = lax.axis_index("row")
    index = [lax.rem(place + k, rows) for k in range(rows)]
    not_first = [jnp.where(i > 0, 1.0, 0.0) for i in index]
    not_last = [jnp.where(i < rows - 1, 1.0, 0.0) for i in index]
    return not_first, not_last


def rim_kernel(rows, tiles, edge, depth, *refs):
    column_refs, (message_ref, far_ref, flow_ref, first_ref) = refs[:rows], refs[rows:]
    patterns = message_ref.shape[1]
    span = tiles * edge
    not_first, not_last = row_masks(rows)
    start = [ref[span : 2 * span] for ref in column_refs]
    folds = [ref[2 * span : 2 * span + depth] for ref in column_refs]
    base = 2 * span + depth
    gains = jnp.concatenate([ref[base : base + 1] for ref in column_refs], axis=0)
    columns = turned(gains)
    first = sum(ref[base + 1 : base + 2] for ref in column_refs)
    south = [
        columns[span : 2 * span, k : k + 1] * (start[k] - start[(k + 1) % rows] * not_last[k])
        for k in range(rows)
    ]
    dropped = jnp.zeros((span, patterns), jnp.float32)
    stride = span + depth
    for k in range(rows):
        flow = south[k] - south[k - 1] * not_first[k]
        raw = column_refs[k][:span]
        rim = raw - dot3(corners(folds[k], tiles, edge), flow)
        dropped = dropped + flow * (raw + rim)
        message_ref[k * stride : k * stride + span] = rim
        message_ref[k * stride + span : (k + 1) * stride] = folds[k]
        far_ref[k * edge : (k + 1) * edge] = rim[:edge]
        if k == 0:
            flow_ref[...] = flow
    message_ref[rows * stride : rows * stride + rows] = gains
    if message_ref.shape[0] > rows * stride + rows:
        rest_rows = message_ref.shape[0] - rows * stride - rows
        message_ref[rows * stride + rows :] = jnp.zeros((rest_rows, patterns), jnp.float32)
    first = first - jnp.sum(dropped, axis=0, keepdims=True)
    first_ref[...] = jnp.broadcast_to(first, first_ref.shape)


def moment_kernel(
    rows,
    cols,
    tiles,
    edge,
    depth,
    own_ref,
    inner_ref,
    outer_ref,
    far_ref,
    first_ref,
    moment_ref,
    t0_ref,
    t1_ref,
):
    patterns = own_ref.shape[1]
    mine = lax.axis_index("col")
    odd = mine % 2 == 1
    has_west = jnp.where(mine > 0, 1.0, 0.0)
    has_east = jnp.where(mine < cols - 1, 1.0, 0.0)
    has_far = jnp.where(mine < cols - 2, 1.0, 0.0)
    not_first, not_last = row_masks(rows)
    span = tiles * edge
    stride = span + depth

    def sides(piece):
        west = jnp.where(odd, inner_ref[piece], outer_ref[piece]) * has_west
        east = jnp.where(odd, outer_ref[piece], inner_ref[piece]) * has_east
        return west, own_ref[piece], east

    gains = [turned(block) for block in sides(slice(rows * stride, None))]
    easts, souths, u0, mats = [], [], [], []
    for k in range(rows):
        blocks = sides(slice(k * stride, (k + 1) * stride))
        far = far_ref[k * edge : (k + 1) * edge] * has_far
        u0.append(
            [block[t * edge : (t + 1) * edge] for block in blocks for t in range(tiles)] + [far]
        )

        def gain(columns, base):
            return jnp.broadcast_to(columns[base : base + edge, k : k + 1], (edge, patterns))

        easts.append([gain(g, t * edge) for g in gains for t in range(tiles)])
        souths.append([gain(g, span + t * edge) for g in gains for t in range(tiles)])
        mats.append([corners(block[span:], tiles, edge) for block in blocks])

    def net_flow(rims, low, high):
        flows = []
        for k in range(rows):
            below, above = (k + 1) % rows, k - 1
            row = []
            for c in range(low, high):
                flow = easts[k][c] * (rims[k][c] - rims[k][c + 1])
                flow = flow - easts[k][c - 1] * (rims[k][c - 1] - rims[k][c])
                flow = flow + souths[k][c] * (rims[k][c] - rims[below][c] * not_last[k])
                back = souths[above][c] * (rims[k][c] - rims[above][c])
                row.append(flow + back * not_first[k])
            flows.append([None] * low + row)
        return flows

    def spread(flows, devices, low, high):
        out = []
        for k in range(rows):
            row = []
            for d in devices:
                block = [
                    flows[k][c] if low <= c < high else jnp.zeros((edge, patterns), jnp.float32)
                    for c in range(d * tiles, (d + 1) * tiles)
                ]
                block = dot3(mats[k][d], jnp.concatenate(block, axis=0))
                row += [block[t * edge : (t + 1) * edge] for t in range(tiles)]
            out.append([None] * (devices[0] * tiles) + row)
        return out

    t0 = net_flow(u0, tiles - 1, 3 * tiles)
    u1 = spread(t0, [0, 1, 2], tiles - 1, 3 * tiles)
    t1 = net_flow(u1, tiles, 2 * tiles + 1)
    u2 = spread(t1, [1, 2], tiles, 2 * tiles + 1)
    zero = jnp.zeros((edge, patterns), jnp.float32)
    sums = [zero] * 5
    for k in range(rows):
        for c in range(tiles, 2 * tiles):
            ahead = u2[k][c] - u2[k][c + 1]
            drop = u2[k][c] - u2[(k + 1) % rows][c] * not_last[k]
            parts = (
                u0[k][c] * t0[k][c],
                u1[k][c] * t0[k][c],
                u1[k][c] * t1[k][c],
                u2[k][c] * t1[k][c],
                easts[k][c] * ahead * ahead + souths[k][c] * drop * drop,
            )
            sums = [total + part for total, part in zip(sums, parts)]
    moment_ref[0:1] = first_ref[0:1]
    for i, total in enumerate(sums):
        moment_ref[i + 1 : i + 2] = jnp.sum(total, axis=0, keepdims=True)
    moment_ref[6:8] = jnp.zeros((2, patterns), jnp.float32)
    t0_ref[...] = jnp.concatenate(t0[0][tiles : 2 * tiles], axis=0)
    t1_ref[...] = jnp.concatenate(t1[0][tiles : 2 * tiles], axis=0)


def direction_kernel(edge, precond_ref, inverse_ref, flow_ref, t0_ref, t1_ref, *out_refs):
    for t in range(precond_ref.shape[0]):
        rim = slice(t * edge, (t + 1) * edge)
        flows = jnp.concatenate([flow_ref[rim], t0_ref[rim], t1_ref[rim]], axis=1)
        spread = dot3(inverse_ref[t, :, :edge], flows)
        width = spread.shape[1] // 3
        out_refs[0][t] = precond_ref[t] - spread[:, :width]
        out_refs[1][t] = spread[:, width : 2 * width]
        out_refs[2][t] = spread[:, 2 * width :]


def final_kernel(volt_ref, z0_ref, z1_ref, z2_ref, *refs):
    *sum_refs, out_ref = refs
    tiles = volt_ref.shape[0]
    sums = sum(ref[...] for ref in sum_refs)
    m = [sums[i : i + 1] for i in range(6)]
    a00, a01, a02 = m[0] + m[1], m[1] + m[2], m[2] + m[3]
    a12, a22 = m[3] + m[4], m[4] + m[5]
    l1, l2 = a01 / a00, a02 / a00
    d1 = a02 - l1 * a01
    e12 = a12 - l2 * a01
    l12 = e12 / d1
    d2 = a22 - l2 * a02 - l12 * e12
    y1 = m[1] - l1 * m[0]
    y2 = m[2] - l2 * m[0] - l12 * y1
    c2 = y2 / d2
    c1 = y1 / d1 - l12 * c2
    c0 = m[0] / a00 - l1 * c1 - l2 * c2
    for t in range(tiles):
        out_ref[t] = volt_ref[t] + c0 * z0_ref[t] + c1 * z1_ref[t] + c2 * z2_ref[t]


def other(block, axis, count, distance):
    return lax.ppermute(block, axis, [(i, i ^ distance) for i in range(count)])


def stages(count, held):
    while held < count:
        reach = 2 if (count // held).bit_length() % 2 == 0 else 4
        yield [held * k for k in range(1, reach)]
        held *= reach


def sum_stages(block, axis, count):
    held, terms = 2, [block]
    while held < count:
        block = sum(terms[1:], terms[0])
        if (count // held).bit_length() % 2 == 0:
            terms = [block, other(block, axis, count, held)]
            held *= 2
            continue
        route = [(i, i ^ (2 * held if i % 2 else held)) for i in range(count)]
        brought = lax.ppermute(block, axis, route)
        third = other(block, axis, count, 3 * held)
        brought, third = lax.optimization_barrier((brought, third))
        terms = [block, brought, third, other(brought, axis, count, 1)]
        held *= 4
    return terms


def outer_swap(block, axis, count):
    pairs = [(i, (i + 1) % count if i % 2 else (i - 1) % count) for i in range(count)]
    return lax.ppermute(block, axis, pairs)


def local(
    initial_voltage,
    inject,
    conduct,
    capacitance,
    track_gain,
    driver_tile,
    sink_net,
    sink_count,
    sink_tile,
    sink_node,
    sink_gain,
):
    rows, cols = lax.axis_size("row"), lax.axis_size("col")
    tiles, nodes, patterns = initial_voltage.shape[1:]
    edge, nets = track_gain.shape[-1], driver_tile.shape[-1]
    slots = cols * sink_net.shape[-1]
    voltage = initial_voltage[0]
    field = (tiles, nodes, patterns)
    span = tiles * edge

    mate = other(initial_voltage, "col", cols, 1)[0]
    mate_driver = other(driver_tile, "col", cols, 1)[0]
    mate_gain = other(track_gain, "col", cols, 1)[0]
    eye = run(eye_kernel, [(nodes, nodes)])[0]
    narrow_type = functools.partial(jax.ShapeDtypeStruct, dtype=jnp.bfloat16)
    rest, gains, take, put, scale, picked = run(
        functools.partial(sink_kernel, nets, edge),
        [
            field,
            (edge + 8, patterns),
            narrow_type((slots, cols * nets)),
            narrow_type((slots, tiles * nodes)),
            (slots, patterns),
            (nets, patterns),
        ],
        eye,
        conduct[0],
        voltage,
        inject[0],
        track_gain[0],
        sink_net[0, 0],
        sink_count[0],
        sink_tile[0, 0],
        sink_node[0, 0],
        sink_gain[0, 0],
        driver_tile[0],
    )
    pair = run(
        functools.partial(pair_kernel, nets, edge),
        [(2 * nets + edge + 8, patterns)],
        voltage,
        picked,
        mate,
        mate_driver,
        mate_gain,
    )[0]
    groups = [pair]
    for distances in stages(cols, 2):
        whole = groups[0] if len(groups) == 1 else jnp.concatenate(groups)
        groups = [whole] + [other(whole, "col", cols, d) for d in distances]
    depth = tiles * edge * edge // nodes
    inverse, fold, part, reach = run(
        functools.partial(tile_kernel, edge),
        [field, (depth, nodes), field, (tiles, nodes, slots)],
        eye,
        conduct[0],
        capacitance[0],
        rest,
        put,
        pair,
        scratch=[pltpu.VMEM(field, jnp.float32)] * 2,
    )

    message, precond = run(
        functools.partial(residual_kernel, nets, edge, cols),
        [(2 * span + depth + 8, patterns), field],
        voltage,
        mate,
        mate_gain,
        inverse,
        fold,
        part,
        reach,
        rest,
        gains,
        take,
        put,
        scale,
        *groups,
    )

    column = [message] + [
        lax.ppermute(message, "row", [((i + k) % rows, i) for i in range(rows)])
        for k in range(1, rows)
    ]
    height = rows * (span + depth) + -(-rows // 8) * 8
    message, far, flow, first = run(
        functools.partial(rim_kernel, rows, tiles, edge, depth),
        [(height, patterns), (rows * edge, patterns), (span, patterns), (8, patterns)],
        *column,
    )

    inner = other(message, "col", cols, 1)
    beyond = outer_swap(message, "col", cols)
    far = lax.ppermute(far, "col", [((i + 2) % cols, i) for i in range(cols)])
    moments, t0, t1 = run(
        functools.partial(moment_kernel, rows, cols, tiles, edge, depth),
        [(8, patterns), (span, patterns), (span, patterns)],
        message,
        inner,
        beyond,
        far,
        first,
    )

    sums = sum_stages(moments + other(moments, "col", cols, 1), "col", cols)
    directions = run(
        functools.partial(direction_kernel, edge), [field] * 3, precond, inverse, flow, t0, t1
    )
    return run(final_kernel, [field], voltage, *directions, *sums)[0][None]


def solution(mesh):
    whole = P("row", "col", None, None)
    third = P("row", "col", None)
    placed = (whole, whole, whole, third, whole, third, whole, third, whole, whole, whole)
    return jax.shard_map(local, mesh=mesh, in_specs=placed, out_specs=whole, check_vma=False)
```

```python
import functools

import jax
import jax.numpy as jnp
from jax import lax
from jax.experimental import pallas as pl
from jax.experimental.pallas import tpu as pltpu
from jax.sharding import PartitionSpec as P

DOUBLINGS = 5
SMALL = 2.0**-13
VMEM_BYTES = 16 * 1024 * 1024

dot = functools.partial(
    jnp.dot, precision=lax.Precision.HIGHEST, preferred_element_type=jnp.float32
)


def split(block):
    high = block.astype(jnp.bfloat16)
    return high, (block - high.astype(jnp.float32)).astype(jnp.bfloat16)


def thirds(block):
    high = block.astype(jnp.bfloat16)
    middle, low = split(block - high.astype(jnp.float32))
    return low, middle, high


def narrow(left, right):
    return jnp.dot(left, right, preferred_element_type=jnp.float32)


def dot3(left, right):
    (left_high, left_low), (right_high, right_low) = split(left), split(right)
    return narrow(left_high, right_high) + (
        narrow(left_high, right_low) + narrow(left_low, right_high)
    )


def select(onehot, block):
    high = block.astype(jnp.bfloat16)
    rest = block - high.astype(jnp.float32)
    middle, low = split(rest)
    return narrow(onehot, high) + (narrow(onehot, middle) + narrow(onehot, low))


def run(kernel, outs, *args, scratch=(), flops=4_000_000_000):
    vmem = pl.BlockSpec(memory_space=pltpu.VMEM)
    shapes = tuple(
        o if isinstance(o, jax.ShapeDtypeStruct) else jax.ShapeDtypeStruct(o, jnp.float32)
        for o in outs
    )
    moved = sum(4 * a.size for a in args) + sum(4 * s.size for s in shapes)
    return pl.pallas_call(
        kernel,
        out_shape=shapes,
        in_specs=[vmem] * len(args),
        out_specs=(vmem,) * len(shapes),
        scratch_shapes=list(scratch),
        compiler_params=pltpu.CompilerParams(vmem_limit_bytes=VMEM_BYTES),
        cost_estimate=pl.CostEstimate(flops=flops, bytes_accessed=moved, transcendentals=0),
    )(*args)


def iota(shape, axis):
    return lax.broadcasted_iota(jnp.int32, shape, axis)


def to_column(row):
    count = row.shape[1]
    square = jnp.broadcast_to(row, (count, count))
    keep = iota((count, count), 0) == iota((count, count), 1)
    return jnp.sum(jnp.where(keep, square, 0.0), axis=1, keepdims=True)


def slot_column(table):
    sources, slots = table.shape
    spread = jnp.concatenate(
        [jnp.broadcast_to(table[s : s + 1], (slots, slots)) for s in range(sources)], axis=0
    )
    keep = iota(spread.shape, 0) % slots == iota(spread.shape, 1)
    return jnp.sum(jnp.where(keep, spread, 0.0), axis=1, keepdims=True)


def source_column(row, slots):
    sources = row.shape[1]
    spread = jnp.broadcast_to(row, (sources * slots, sources))
    keep = iota(spread.shape, 0) // slots == iota(spread.shape, 1)
    return jnp.sum(jnp.where(keep, spread, 0.0), axis=1, keepdims=True)


def pair_kernel(nets, edge, volt_ref, picked_ref, mate_ref, mate_driver_ref, mate_gain_ref, out_ref):
    tiles, nodes, patterns = volt_ref.shape
    odd = lax.axis_index("col") % 2 == 1
    mate_picked = to_column(mate_driver_ref[...].astype(jnp.float32))
    for i, (field, picked) in enumerate(((volt_ref, picked_ref[...]), (mate_ref, mate_picked))):
        rows = jnp.zeros((nets, patterns), jnp.float32)
        for t in range(tiles):
            block = jnp.concatenate([field[t]] * (-(-nets // nodes)), axis=0)[:nets]
            rows = jnp.where(picked == t, block, rows)
        out_ref[i * nets : (i + 1) * nets] = rows
    base = 2 * nets
    out_ref[base : base + edge] = jnp.where(odd, mate_ref[0, :edge], mate_ref[tiles - 1, :edge])
    out_ref[base + edge :] = jnp.zeros((8, patterns), jnp.float32)
    out_ref[base + edge : base + edge + 1, :edge] = mate_gain_ref[tiles - 1, 0:1]


def eye_kernel(out_ref):
    out_ref[...] = jnp.where(iota(out_ref.shape, 0) == iota(out_ref.shape, 1), 1.0, 0.0)


def sink_kernel(
    nets,
    edge,
    eye_ref,
    conduct_ref,
    volt_ref,
    inject_ref,
    gain_ref,
    net_ref,
    count_ref,
    tile_ref,
    node_ref,
    weight_ref,
    driver_ref,
    rest_ref,
    gains_ref,
    take_ref,
    put_ref,
    scale_ref,
    picked_ref,
):
    picked_ref[...] = jnp.broadcast_to(
        to_column(driver_ref[...].astype(jnp.float32)), picked_ref.shape
    )
    tiles, nodes = conduct_ref.shape[0], conduct_ref.shape[1]
    for t in range(tiles):
        rest_ref[t] = inject_ref[t] - dot(conduct_ref[t], volt_ref[t])
    lane = iota((edge, nodes), 1)
    table = jnp.zeros((edge, nodes), jnp.float32)
    gains_ref[edge:] = jnp.zeros((8, nodes), jnp.float32)
    for side in range(2):
        for t in range(tiles):
            i = side * tiles + t
            gain = gain_ref[t, side : side + 1]
            table = jnp.where(lane == i, to_column(gain), table)
            gains_ref[edge : edge + 1, i * edge : (i + 1) * edge] = gain
    gains_ref[:edge] = table

    sources, slots = net_ref.shape
    mine = lax.axis_index("col")
    block = iota((sources, slots), 0) ^ mine
    place = slot_column((block * nets + net_ref[...]).astype(jnp.float32))
    target = slot_column((tile_ref[...] * nodes + node_ref[...]).astype(jnp.float32))
    live = source_column(count_ref[...].astype(jnp.float32), slots)
    slot = (iota(live.shape, 0) % slots).astype(jnp.float32)
    weight = jnp.where(slot < live, slot_column(weight_ref[...]), 0.0)
    take = jnp.where(place == iota(take_ref.shape, 1).astype(jnp.float32), 1.0, 0.0)
    put = jnp.where(target == iota(put_ref.shape, 1).astype(jnp.float32), 1.0, 0.0)
    take_ref[...] = take.astype(jnp.bfloat16)
    put_ref[...] = put.astype(jnp.bfloat16)
    scale_ref[...] = jnp.broadcast_to(weight, scale_ref.shape)


def tile_kernel(
    edge,
    eye_ref,
    conduct_ref,
    cap_ref,
    rest_ref,
    put_ref,
    after_ref,
    inverse_ref,
    fold_ref,
    part_ref,
    reach_ref,
    sum_ref,
    power_ref,
):
    tiles, nodes = conduct_ref.shape[0], conduct_ref.shape[1]
    eye = eye_ref[...]
    sums, powers, scales = [], [], []
    for t in range(tiles):
        conduct = conduct_ref[t]
        diagonal = (conduct + cap_ref[t : t + 1, :]) * eye
        down = jnp.sum(diagonal, axis=1, keepdims=True)
        across = jnp.sum(diagonal, axis=0, keepdims=True)
        power = (conduct * eye - conduct) / down
        sums.append(eye + power)
        powers.append(dot(power, power))
        scales.append(1.0 / across)

    def step(sums, powers):
        out_sums, out_powers, largest = [], [], jnp.float32(0.0)
        for total, power in zip(sums, powers):
            both = dot(jnp.concatenate([total, power], axis=0), power)
            out_sums.append(total + both[:nodes])
            out_powers.append(both[nodes:])
            largest = jnp.maximum(largest, jnp.max(jnp.sum(power, axis=1)))
        return out_sums, out_powers, largest

    for _ in range(DOUBLINGS):
        sums, powers, largest = step(sums, powers)
    for t in range(tiles):
        sum_ref[t], power_ref[t] = sums[t], powers[t]

    def again(carry):
        sums, powers, largest = step(
            [sum_ref[t] for t in range(tiles)], [power_ref[t] for t in range(tiles)]
        )
        for t in range(tiles):
            sum_ref[t], power_ref[t] = sums[t], powers[t]
        return largest, carry[1] + 1

    lax.while_loop(
        lambda carry: (carry[0] > SMALL) & (carry[1] < 40), again, (largest, jnp.int32(0))
    )
    parts = nodes // edge
    depth = edge // parts
    lane = iota((depth, nodes), 1)
    for t in range(tiles):
        inverse = sum_ref[t] * scales[t]
        inverse_ref[t] = inverse
        fold = jnp.zeros((depth, nodes), jnp.float32)
        for j in range(parts):
            piece = jnp.where(lane < edge, inverse[j * depth : (j + 1) * depth], 0.0)
            fold = fold + (pltpu.roll(piece, j * edge, 1) if j else piece)
        fold_ref[t * depth : (t + 1) * depth] = fold
        part_ref[t] = dot(inverse, rest_ref[t])
        put = put_ref[:, t * nodes : (t + 1) * nodes]
        reach_ref[t] = sum(
            lax.dot_general(
                piece, put, (((1,), (1,)), ((), ())), preferred_element_type=jnp.float32
            )
            for piece in thirds(inverse)
        )


def residual_kernel(
    nets,
    edge,
    cols,
    volt_ref,
    mate_ref,
    mate_gain_ref,
    inverse_ref,
    fold_ref,
    part_ref,
    reach_ref,
    rest_ref,
    gains_ref,
    take_ref,
    put_ref,
    scale_ref,
    *refs,
):
    *group_refs, message_ref, precond_ref = refs
    tiles, nodes, patterns = volt_ref.shape
    mine = lax.axis_index("col")
    odd = mine % 2 == 1
    stride = 2 * nets + edge + 8
    blocks = [(ref, base) for ref in group_refs for base in range(0, ref.shape[0], stride)]
    values = sum(
        select(take_ref[:, j * 2 * nets : (j + 1) * 2 * nets], ref[base : base + 2 * nets])
        for j, (ref, base) in enumerate(blocks)
    )
    values = values * scale_ref[...]
    beyond = lax.rem(jnp.where(odd, mine + 1, mine + cols - 1), cols) ^ 1
    which = (mine ^ beyond) // 2
    outer = jnp.zeros((edge + 8, patterns), jnp.float32)
    for j, (ref, base) in enumerate(blocks):
        outer = jnp.where(which == j, ref[base + 2 * nets : base + stride], outer)
    inner = jnp.where(odd, mate_ref[tiles - 1, :edge], mate_ref[0, :edge])
    inner_gain = to_column(mate_gain_ref[tiles - 1, 0:1])
    has_west = jnp.where(mine > 0, 1.0, 0.0)
    has_east = jnp.where(mine < cols - 1, 1.0, 0.0)
    west = jnp.where(odd, inner, outer[:edge]) * has_west
    east = jnp.where(odd, outer[:edge], inner) * has_east
    west_gain = jnp.where(odd, inner_gain, to_column(outer[edge : edge + 1, :edge])) * has_west
    gains = [west_gain] + [gains_ref[:edge, t : t + 1] for t in range(tiles)]
    rims = [west] + [volt_ref[t, :edge] for t in range(tiles)] + [east]
    flows = [gains[t] * (rims[t] - rims[t + 1]) for t in range(tiles + 1)]
    first = jnp.zeros((1, patterns), jnp.float32)
    high, low = split(values)
    for t in range(tiles):
        out = flows[t + 1] - flows[t]
        precond = part_ref[t] + (
            dot3(reach_ref[t], values) - dot3(inverse_ref[t, :, :edge], out)
        )
        put = put_ref[:, t * nodes : (t + 1) * nodes]
        injected = sum(
            lax.dot_general(
                put, part, (((0,), (0,)), ((), ())), preferred_element_type=jnp.float32
            )
            for part in (high, low)
        )
        residual = rest_ref[t] + injected
        residual = jnp.concatenate([residual[:edge] - out, residual[edge:]], axis=0)
        precond_ref[t] = precond
        first = first + jnp.sum(residual * precond, axis=0, keepdims=True)
        message_ref[t * edge : (t + 1) * edge] = precond[:edge]
        message_ref[(tiles + t) * edge : (tiles + t + 1) * edge] = volt_ref[t, :edge]
    base = 2 * tiles * edge
    depth = fold_ref.shape[0]
    message_ref[base : base + depth] = fold_ref[...]
    message_ref[base + depth : base + depth + 8] = gains_ref[edge:]
    message_ref[base + depth + 1 : base + depth + 2] = first


def corners(fold, tiles, edge):
    depth, lanes = fold.shape[0] // tiles, fold.shape[1]
    lane = iota((depth, lanes), 1)
    rows = []
    for t in range(tiles):
        piece = fold[t * depth : (t + 1) * depth]
        for j in range(lanes // edge):
            turn = (t - j) * edge % lanes
            turned = pltpu.roll(piece, turn, 1) if turn else piece
            rows.append(jnp.where((lane >= t * edge) & (lane < (t + 1) * edge), turned, 0.0))
    return jnp.concatenate(rows, axis=0)[:, : tiles * edge]


def turned(rows):
    count, lanes = rows.shape
    full = jnp.concatenate([rows, jnp.zeros((lanes - count, lanes), jnp.float32)], axis=0)
    return jnp.transpose(full)


def row_masks(rows):
    place = lax.axis_index("row")
    index = [lax.rem(place + k, rows) for k in range(rows)]
    not_first = [jnp.where(i > 0, 1.0, 0.0) for i in index]
    not_last = [jnp.where(i < rows - 1, 1.0, 0.0) for i in index]
    return not_first, not_last


def rim_kernel(rows, tiles, edge, depth, *refs):
    column_refs, (message_ref, far_ref, flow_ref, first_ref) = refs[:rows], refs[rows:]
    patterns = message_ref.shape[1]
    span = tiles * edge
    not_first, not_last = row_masks(rows)
    start = [ref[span : 2 * span] for ref in column_refs]
    folds = [ref[2 * span : 2 * span + depth] for ref in column_refs]
    base = 2 * span + depth
    gains = jnp.concatenate([ref[base : base + 1] for ref in column_refs], axis=0)
    columns = turned(gains)
    first = sum(ref[base + 1 : base + 2] for ref in column_refs)
    south = [
        columns[span : 2 * span, k : k + 1] * (start[k] - start[(k + 1) % rows] * not_last[k])
        for k in range(rows)
    ]
    dropped = jnp.zeros((span, patterns), jnp.float32)
    stride = span + depth
    for k in range(rows):
        flow = south[k] - south[k - 1] * not_first[k]
        raw = column_refs[k][:span]
        rim = raw - dot3(corners(folds[k], tiles, edge), flow)
        dropped = dropped + flow * (raw + rim)
        message_ref[k * stride : k * stride + span] = rim
        message_ref[k * stride + span : (k + 1) * stride] = folds[k]
        far_ref[k * edge : (k + 1) * edge] = rim[:edge]
        if k == 0:
            flow_ref[...] = flow
    message_ref[rows * stride : rows * stride + rows] = gains
    if message_ref.shape[0] > rows * stride + rows:
        rest_rows = message_ref.shape[0] - rows * stride - rows
        message_ref[rows * stride + rows :] = jnp.zeros((rest_rows, patterns), jnp.float32)
    first = first - jnp.sum(dropped, axis=0, keepdims=True)
    first_ref[...] = jnp.broadcast_to(first, first_ref.shape)


def moment_kernel(
    rows,
    cols,
    tiles,
    edge,
    depth,
    own_ref,
    inner_ref,
    outer_ref,
    far_ref,
    first_ref,
    moment_ref,
    t0_ref,
    t1_ref,
):
    patterns = own_ref.shape[1]
    mine = lax.axis_index("col")
    odd = mine % 2 == 1
    has_west = jnp.where(mine > 0, 1.0, 0.0)
    has_east = jnp.where(mine < cols - 1, 1.0, 0.0)
    has_far = jnp.where(mine < cols - 2, 1.0, 0.0)
    not_first, not_last = row_masks(rows)
    span = tiles * edge
    stride = span + depth

    def sides(piece):
        west = jnp.where(odd, inner_ref[piece], outer_ref[piece]) * has_west
        east = jnp.where(odd, outer_ref[piece], inner_ref[piece]) * has_east
        return west, own_ref[piece], east

    gains = [turned(block) for block in sides(slice(rows * stride, None))]
    easts, souths, u0, mats = [], [], [], []
    for k in range(rows):
        blocks = sides(slice(k * stride, (k + 1) * stride))
        far = far_ref[k * edge : (k + 1) * edge] * has_far
        u0.append(
            [block[t * edge : (t + 1) * edge] for block in blocks for t in range(tiles)] + [far]
        )

        def gain(columns, base):
            return jnp.broadcast_to(columns[base : base + edge, k : k + 1], (edge, patterns))

        easts.append([gain(g, t * edge) for g in gains for t in range(tiles)])
        souths.append([gain(g, span + t * edge) for g in gains for t in range(tiles)])
        mats.append([corners(block[span:], tiles, edge) for block in blocks])

    def net_flow(rims, low, high):
        flows = []
        for k in range(rows):
            below, above = (k + 1) % rows, k - 1
            row = []
            for c in range(low, high):
                flow = easts[k][c] * (rims[k][c] - rims[k][c + 1])
                flow = flow - easts[k][c - 1] * (rims[k][c - 1] - rims[k][c])
                flow = flow + souths[k][c] * (rims[k][c] - rims[below][c] * not_last[k])
                back = souths[above][c] * (rims[k][c] - rims[above][c])
                row.append(flow + back * not_first[k])
            flows.append([None] * low + row)
        return flows

    def spread(flows, devices, low, high):
        out = []
        for k in range(rows):
            row = []
            for d in devices:
                block = [
                    flows[k][c] if low <= c < high else jnp.zeros((edge, patterns), jnp.float32)
                    for c in range(d * tiles, (d + 1) * tiles)
                ]
                block = dot3(mats[k][d], jnp.concatenate(block, axis=0))
                row += [block[t * edge : (t + 1) * edge] for t in range(tiles)]
            out.append([None] * (devices[0] * tiles) + row)
        return out

    t0 = net_flow(u0, tiles - 1, 3 * tiles)
    u1 = spread(t0, [0, 1, 2], tiles - 1, 3 * tiles)
    t1 = net_flow(u1, tiles, 2 * tiles + 1)
    u2 = spread(t1, [1, 2], tiles, 2 * tiles + 1)
    zero = jnp.zeros((edge, patterns), jnp.float32)
    sums = [zero] * 5
    for k in range(rows):
        for c in range(tiles, 2 * tiles):
            ahead = u2[k][c] - u2[k][c + 1]
            drop = u2[k][c] - u2[(k + 1) % rows][c] * not_last[k]
            parts = (
                u0[k][c] * t0[k][c],
                u1[k][c] * t0[k][c],
                u1[k][c] * t1[k][c],
                u2[k][c] * t1[k][c],
                easts[k][c] * ahead * ahead + souths[k][c] * drop * drop,
            )
            sums = [total + part for total, part in zip(sums, parts)]
    moment_ref[0:1] = first_ref[0:1]
    for i, total in enumerate(sums):
        moment_ref[i + 1 : i + 2] = jnp.sum(total, axis=0, keepdims=True)
    moment_ref[6:8] = jnp.zeros((2, patterns), jnp.float32)
    t0_ref[...] = jnp.concatenate(t0[0][tiles : 2 * tiles], axis=0)
    t1_ref[...] = jnp.concatenate(t1[0][tiles : 2 * tiles], axis=0)


def direction_kernel(edge, precond_ref, inverse_ref, flow_ref, t0_ref, t1_ref, *out_refs):
    for t in range(precond_ref.shape[0]):
        rim = slice(t * edge, (t + 1) * edge)
        flows = jnp.concatenate([flow_ref[rim], t0_ref[rim], t1_ref[rim]], axis=1)
        spread = dot(inverse_ref[t, :, :edge], flows)
        width = spread.shape[1] // 3
        out_refs[0][t] = precond_ref[t] - spread[:, :width]
        out_refs[1][t] = spread[:, width : 2 * width]
        out_refs[2][t] = spread[:, 2 * width :]


def final_kernel(volt_ref, z0_ref, z1_ref, z2_ref, *refs):
    *sum_refs, out_ref = refs
    tiles = volt_ref.shape[0]
    sums = sum(ref[...] for ref in sum_refs)
    m = [sums[i : i + 1] for i in range(6)]
    a00, a01, a02 = m[0] + m[1], m[1] + m[2], m[2] + m[3]
    a12, a22 = m[3] + m[4], m[4] + m[5]
    l1, l2 = a01 / a00, a02 / a00
    d1 = a02 - l1 * a01
    e12 = a12 - l2 * a01
    l12 = jnp.where(d1 > 0.0, e12 / d1, 0.0)
    d2 = a22 - l2 * a02 - l12 * e12
    y1 = m[1] - l1 * m[0]
    y2 = m[2] - l2 * m[0] - l12 * y1
    c2 = jnp.where(d2 > 0.0, y2 / d2, 0.0)
    c1 = jnp.where(d1 > 0.0, y1 / d1 - l12 * c2, 0.0)
    c0 = m[0] / a00 - l1 * c1 - l2 * c2
    for t in range(tiles):
        out_ref[t] = volt_ref[t] + c0 * z0_ref[t] + c1 * z1_ref[t] + c2 * z2_ref[t]


def other(block, axis, count, distance):
    return lax.ppermute(block, axis, [(i, i ^ distance) for i in range(count)])


def stages(count, held):
    while held < count:
        reach = 2 if (count // held).bit_length() % 2 == 0 else 4
        yield [held * k for k in range(1, reach)]
        held *= reach


def sum_stages(block, axis, count):
    held, terms = 2, [block]
    while held < count:
        block = sum(terms[1:], terms[0])
        if (count // held).bit_length() % 2 == 0:
            terms = [block, other(block, axis, count, held)]
            held *= 2
            continue
        route = [(i, i ^ (2 * held if i % 2 else held)) for i in range(count)]
        brought = lax.ppermute(block, axis, route)
        third = other(block, axis, count, 3 * held)
        brought, third = lax.optimization_barrier((brought, third))
        terms = [block, brought, third, other(brought, axis, count, 1)]
        held *= 4
    return terms


def outer_swap(block, axis, count):
    pairs = [(i, (i + 1) % count if i % 2 else (i - 1) % count) for i in range(count)]
    return lax.ppermute(block, axis, pairs)


def local(
    initial_voltage,
    inject,
    conduct,
    capacitance,
    track_gain,
    driver_tile,
    sink_net,
    sink_count,
    sink_tile,
    sink_node,
    sink_gain,
):
    rows, cols = lax.axis_size("row"), lax.axis_size("col")
    tiles, nodes, patterns = initial_voltage.shape[1:]
    edge, nets = track_gain.shape[-1], driver_tile.shape[-1]
    slots = cols * sink_net.shape[-1]
    voltage = initial_voltage[0]
    field = (tiles, nodes, patterns)
    span = tiles * edge

    mate = other(initial_voltage, "col", cols, 1)[0]
    mate_driver = other(driver_tile, "col", cols, 1)[0]
    mate_gain = other(track_gain, "col", cols, 1)[0]
    eye = run(eye_kernel, [(nodes, nodes)])[0]
    narrow_type = functools.partial(jax.ShapeDtypeStruct, dtype=jnp.bfloat16)
    rest, gains, take, put, scale, picked = run(
        functools.partial(sink_kernel, nets, edge),
        [
            field,
            (edge + 8, patterns),
            narrow_type((slots, cols * nets)),
            narrow_type((slots, tiles * nodes)),
            (slots, patterns),
            (nets, patterns),
        ],
        eye,
        conduct[0],
        voltage,
        inject[0],
        track_gain[0],
        sink_net[0, 0],
        sink_count[0],
        sink_tile[0, 0],
        sink_node[0, 0],
        sink_gain[0, 0],
        driver_tile[0],
    )
    pair = run(
        functools.partial(pair_kernel, nets, edge),
        [(2 * nets + edge + 8, patterns)],
        voltage,
        picked,
        mate,
        mate_driver,
        mate_gain,
    )[0]
    groups = [pair]
    for distances in stages(cols, 2):
        whole = groups[0] if len(groups) == 1 else jnp.concatenate(groups)
        groups = [whole] + [other(whole, "col", cols, d) for d in distances]
    depth = tiles * edge * edge // nodes
    inverse, fold, part, reach = run(
        functools.partial(tile_kernel, edge),
        [field, (depth, nodes), field, (tiles, nodes, slots)],
        eye,
        conduct[0],
        capacitance[0],
        rest,
        put,
        pair,
        scratch=[pltpu.VMEM(field, jnp.float32)] * 2,
    )

    message, precond = run(
        functools.partial(residual_kernel, nets, edge, cols),
        [(2 * span + depth + 8, patterns), field],
        voltage,
        mate,
        mate_gain,
        inverse,
        fold,
        part,
        reach,
        rest,
        gains,
        take,
        put,
        scale,
        *groups,
    )

    column = [message] + [
        lax.ppermute(message, "row", [((i + k) % rows, i) for i in range(rows)])
        for k in range(1, rows)
    ]
    height = rows * (span + depth) + -(-rows // 8) * 8
    message, far, flow, first = run(
        functools.partial(rim_kernel, rows, tiles, edge, depth),
        [(height, patterns), (rows * edge, patterns), (span, patterns), (8, patterns)],
        *column,
    )

    inner = other(message, "col", cols, 1)
    beyond = outer_swap(message, "col", cols)
    far = lax.ppermute(far, "col", [((i + 2) % cols, i) for i in range(cols)])
    moments, t0, t1 = run(
        functools.partial(moment_kernel, rows, cols, tiles, edge, depth),
        [(8, patterns), (span, patterns), (span, patterns)],
        message,
        inner,
        beyond,
        far,
        first,
    )

    sums = sum_stages(moments + other(moments, "col", cols, 1), "col", cols)
    directions = run(
        functools.partial(direction_kernel, edge), [field] * 3, precond, inverse, flow, t0, t1
    )
    return run(final_kernel, [field], voltage, *directions, *sums)[0][None]


def solution(mesh):
    whole = P("row", "col", None, None)
    third = P("row", "col", None)
    placed = (whole, whole, whole, third, whole, third, whole, third, whole, whole, whole)
    return jax.shard_map(local, mesh=mesh, in_specs=placed, out_specs=whole, check_vma=False)
```

```python
import functools

import jax
import jax.numpy as jnp
from jax import lax
from jax.experimental import pallas as pl
from jax.experimental.pallas import tpu as pltpu
from jax.sharding import PartitionSpec as P

DOUBLINGS = 5
SMALL = 2.0**-13
VMEM_BYTES = 16 * 1024 * 1024

dot = functools.partial(
    jnp.dot, precision=lax.Precision.HIGHEST, preferred_element_type=jnp.float32
)


def split(block):
    high = block.astype(jnp.bfloat16)
    return high, (block - high.astype(jnp.float32)).astype(jnp.bfloat16)


def thirds(block):
    high = block.astype(jnp.bfloat16)
    middle, low = split(block - high.astype(jnp.float32))
    return low, middle, high


def narrow(left, right):
    return jnp.dot(left, right, preferred_element_type=jnp.float32)


def dot3(left, right):
    (left_high, left_low), (right_high, right_low) = split(left), split(right)
    return narrow(left_high, right_high) + (
        narrow(left_high, right_low) + narrow(left_low, right_high)
    )


def select(onehot, block):
    high = block.astype(jnp.bfloat16)
    rest = block - high.astype(jnp.float32)
    middle, low = split(rest)
    return narrow(onehot, high) + (narrow(onehot, middle) + narrow(onehot, low))


def run(kernel, outs, *args, scratch=(), flops=4_000_000_000):
    vmem = pl.BlockSpec(memory_space=pltpu.VMEM)
    shapes = tuple(
        o if isinstance(o, jax.ShapeDtypeStruct) else jax.ShapeDtypeStruct(o, jnp.float32)
        for o in outs
    )
    moved = sum(4 * a.size for a in args) + sum(4 * s.size for s in shapes)
    return pl.pallas_call(
        kernel,
        out_shape=shapes,
        in_specs=[vmem] * len(args),
        out_specs=(vmem,) * len(shapes),
        scratch_shapes=list(scratch),
        compiler_params=pltpu.CompilerParams(vmem_limit_bytes=VMEM_BYTES),
        cost_estimate=pl.CostEstimate(flops=flops, bytes_accessed=moved, transcendentals=0),
    )(*args)


def iota(shape, axis):
    return lax.broadcasted_iota(jnp.int32, shape, axis)


def to_column(row):
    count = row.shape[1]
    square = jnp.broadcast_to(row, (count, count))
    keep = iota((count, count), 0) == iota((count, count), 1)
    return jnp.sum(jnp.where(keep, square, 0.0), axis=1, keepdims=True)


def slot_column(table):
    sources, slots = table.shape
    spread = jnp.concatenate(
        [jnp.broadcast_to(table[s : s + 1], (slots, slots)) for s in range(sources)], axis=0
    )
    keep = iota(spread.shape, 0) % slots == iota(spread.shape, 1)
    return jnp.sum(jnp.where(keep, spread, 0.0), axis=1, keepdims=True)


def source_column(row, slots):
    sources = row.shape[1]
    spread = jnp.broadcast_to(row, (sources * slots, sources))
    keep = iota(spread.shape, 0) // slots == iota(spread.shape, 1)
    return jnp.sum(jnp.where(keep, spread, 0.0), axis=1, keepdims=True)


def pair_kernel(nets, edge, volt_ref, picked_ref, mate_ref, mate_driver_ref, mate_gain_ref, out_ref):
    tiles, nodes, patterns = volt_ref.shape
    odd = lax.axis_index("col") % 2 == 1
    mate_picked = to_column(mate_driver_ref[...].astype(jnp.float32))
    for i, (field, picked) in enumerate(((volt_ref, picked_ref[...]), (mate_ref, mate_picked))):
        rows = jnp.zeros((nets, patterns), jnp.float32)
        for t in range(tiles):
            block = jnp.concatenate([field[t]] * (-(-nets // nodes)), axis=0)[:nets]
            rows = jnp.where(picked == t, block, rows)
        out_ref[i * nets : (i + 1) * nets] = rows
    base = 2 * nets
    out_ref[base : base + edge] = jnp.where(odd, mate_ref[0, :edge], mate_ref[tiles - 1, :edge])
    out_ref[base + edge :] = jnp.zeros((8, patterns), jnp.float32)
    out_ref[base + edge : base + edge + 1, :edge] = mate_gain_ref[tiles - 1, 0:1]


def eye_kernel(out_ref):
    out_ref[...] = jnp.where(iota(out_ref.shape, 0) == iota(out_ref.shape, 1), 1.0, 0.0)


def sink_kernel(
    nets,
    edge,
    eye_ref,
    conduct_ref,
    volt_ref,
    inject_ref,
    gain_ref,
    net_ref,
    count_ref,
    tile_ref,
    node_ref,
    weight_ref,
    driver_ref,
    cap_ref,
    rest_ref,
    gains_ref,
    take_ref,
    put_ref,
    scale_ref,
    picked_ref,
    held_ref,
):
    held_ref[...] = cap_ref[...]
    picked_ref[...] = jnp.broadcast_to(
        to_column(driver_ref[...].astype(jnp.float32)), picked_ref.shape
    )
    tiles, nodes = conduct_ref.shape[0], conduct_ref.shape[1]
    for t in range(tiles):
        rest_ref[t] = inject_ref[t] - dot(conduct_ref[t], volt_ref[t])
    lane = iota((edge, nodes), 1)
    table = jnp.zeros((edge, nodes), jnp.float32)
    gains_ref[edge:] = jnp.zeros((8, nodes), jnp.float32)
    for side in range(2):
        for t in range(tiles):
            i = side * tiles + t
            gain = gain_ref[t, side : side + 1]
            table = jnp.where(lane == i, to_column(gain), table)
            gains_ref[edge : edge + 1, i * edge : (i + 1) * edge] = gain
    gains_ref[:edge] = table

    sources, slots = net_ref.shape
    mine = lax.axis_index("col")
    block = iota((sources, slots), 0) ^ mine
    place = slot_column((block * nets + net_ref[...]).astype(jnp.float32))
    target = slot_column((tile_ref[...] * nodes + node_ref[...]).astype(jnp.float32))
    live = source_column(count_ref[...].astype(jnp.float32), slots)
    slot = (iota(live.shape, 0) % slots).astype(jnp.float32)
    weight = jnp.where(slot < live, slot_column(weight_ref[...]), 0.0)
    take = jnp.where(place == iota(take_ref.shape, 1).astype(jnp.float32), 1.0, 0.0)
    put = jnp.where(target == iota(put_ref.shape, 1).astype(jnp.float32), 1.0, 0.0)
    take_ref[...] = take.astype(jnp.bfloat16)
    put_ref[...] = put.astype(jnp.bfloat16)
    scale_ref[...] = jnp.broadcast_to(weight, scale_ref.shape)


def tile_kernel(
    edge,
    eye_ref,
    conduct_ref,
    cap_ref,
    rest_ref,
    put_ref,
    after_ref,
    inverse_ref,
    fold_ref,
    part_ref,
    reach_ref,
    sum_ref,
    power_ref,
):
    tiles, nodes = conduct_ref.shape[0], conduct_ref.shape[1]
    eye = eye_ref[...]
    sums, powers, scales = [], [], []
    for t in range(tiles):
        conduct = conduct_ref[t]
        diagonal = (conduct + cap_ref[t : t + 1, :]) * eye
        down = jnp.sum(diagonal, axis=1, keepdims=True)
        across = jnp.sum(diagonal, axis=0, keepdims=True)
        power = (conduct * eye - conduct) / down
        sums.append(eye + power)
        powers.append(dot(power, power))
        scales.append(1.0 / across)

    def step(sums, powers):
        out_sums, out_powers, largest = [], [], jnp.float32(0.0)
        for total, power in zip(sums, powers):
            both = dot(jnp.concatenate([total, power], axis=0), power)
            out_sums.append(total + both[:nodes])
            out_powers.append(both[nodes:])
            largest = jnp.maximum(largest, jnp.max(jnp.sum(power, axis=1)))
        return out_sums, out_powers, largest

    for _ in range(DOUBLINGS):
        sums, powers, largest = step(sums, powers)
    for t in range(tiles):
        sum_ref[t], power_ref[t] = sums[t], powers[t]

    def again(carry):
        sums, powers, largest = step(
            [sum_ref[t] for t in range(tiles)], [power_ref[t] for t in range(tiles)]
        )
        for t in range(tiles):
            sum_ref[t], power_ref[t] = sums[t], powers[t]
        return largest, carry[1] + 1

    lax.while_loop(
        lambda carry: (carry[0] > SMALL) & (carry[1] < 40), again, (largest, jnp.int32(0))
    )
    parts = nodes // edge
    depth = edge // parts
    lane = iota((depth, nodes), 1)
    for t in range(tiles):
        inverse = sum_ref[t] * scales[t]
        inverse_ref[t] = inverse
        fold = jnp.zeros((depth, nodes), jnp.float32)
        for j in range(parts):
            piece = jnp.where(lane < edge, inverse[j * depth : (j + 1) * depth], 0.0)
            fold = fold + (pltpu.roll(piece, j * edge, 1) if j else piece)
        fold_ref[t * depth : (t + 1) * depth] = fold
        part_ref[t] = dot(inverse, rest_ref[t])
        put = put_ref[:, t * nodes : (t + 1) * nodes]
        reach_ref[t] = sum(
            lax.dot_general(
                piece, put, (((1,), (1,)), ((), ())), preferred_element_type=jnp.float32
            )
            for piece in thirds(inverse)
        )


def residual_kernel(
    nets,
    edge,
    cols,
    volt_ref,
    mate_ref,
    mate_gain_ref,
    inverse_ref,
    fold_ref,
    part_ref,
    reach_ref,
    rest_ref,
    gains_ref,
    take_ref,
    put_ref,
    scale_ref,
    *refs,
):
    *group_refs, message_ref, precond_ref = refs
    tiles, nodes, patterns = volt_ref.shape
    mine = lax.axis_index("col")
    odd = mine % 2 == 1
    stride = 2 * nets + edge + 8
    blocks = [(ref, base) for ref in group_refs for base in range(0, ref.shape[0], stride)]
    values = sum(
        select(take_ref[:, j * 2 * nets : (j + 1) * 2 * nets], ref[base : base + 2 * nets])
        for j, (ref, base) in enumerate(blocks)
    )
    values = values * scale_ref[...]
    beyond = lax.rem(jnp.where(odd, mine + 1, mine + cols - 1), cols) ^ 1
    which = (mine ^ beyond) // 2
    outer = jnp.zeros((edge + 8, patterns), jnp.float32)
    for j, (ref, base) in enumerate(blocks):
        outer = jnp.where(which == j, ref[base + 2 * nets : base + stride], outer)
    inner = jnp.where(odd, mate_ref[tiles - 1, :edge], mate_ref[0, :edge])
    inner_gain = to_column(mate_gain_ref[tiles - 1, 0:1])
    has_west = jnp.where(mine > 0, 1.0, 0.0)
    has_east = jnp.where(mine < cols - 1, 1.0, 0.0)
    west = jnp.where(odd, inner, outer[:edge]) * has_west
    east = jnp.where(odd, outer[:edge], inner) * has_east
    west_gain = jnp.where(odd, inner_gain, to_column(outer[edge : edge + 1, :edge])) * has_west
    gains = [west_gain] + [gains_ref[:edge, t : t + 1] for t in range(tiles)]
    rims = [west] + [volt_ref[t, :edge] for t in range(tiles)] + [east]
    flows = [gains[t] * (rims[t] - rims[t + 1]) for t in range(tiles + 1)]
    first = jnp.zeros((1, patterns), jnp.float32)
    high, low = split(values)
    for t in range(tiles):
        out = flows[t + 1] - flows[t]
        precond = part_ref[t] + (
            dot3(reach_ref[t], values) - dot3(inverse_ref[t, :, :edge], out)
        )
        put = put_ref[:, t * nodes : (t + 1) * nodes]
        injected = sum(
            lax.dot_general(
                put, part, (((0,), (0,)), ((), ())), preferred_element_type=jnp.float32
            )
            for part in (high, low)
        )
        residual = rest_ref[t] + injected
        residual = jnp.concatenate([residual[:edge] - out, residual[edge:]], axis=0)
        precond_ref[t] = precond
        first = first + jnp.sum(residual * precond, axis=0, keepdims=True)
        message_ref[t * edge : (t + 1) * edge] = precond[:edge]
        message_ref[(tiles + t) * edge : (tiles + t + 1) * edge] = volt_ref[t, :edge]
    base = 2 * tiles * edge
    depth = fold_ref.shape[0]
    message_ref[base : base + depth] = fold_ref[...]
    message_ref[base + depth : base + depth + 8] = gains_ref[edge:]
    message_ref[base + depth + 1 : base + depth + 2] = first


def corners(fold, tiles, edge):
    depth, lanes = fold.shape[0] // tiles, fold.shape[1]
    lane = iota((depth, lanes), 1)
    rows = []
    for t in range(tiles):
        piece = fold[t * depth : (t + 1) * depth]
        for j in range(lanes // edge):
            turn = (t - j) * edge % lanes
            turned = pltpu.roll(piece, turn, 1) if turn else piece
            rows.append(jnp.where((lane >= t * edge) & (lane < (t + 1) * edge), turned, 0.0))
    return jnp.concatenate(rows, axis=0)[:, : tiles * edge]


def turned(rows):
    count, lanes = rows.shape
    full = jnp.concatenate([rows, jnp.zeros((lanes - count, lanes), jnp.float32)], axis=0)
    return jnp.transpose(full)


def row_masks(rows):
    place = lax.axis_index("row")
    index = [lax.rem(place + k, rows) for k in range(rows)]
    not_first = [jnp.where(i > 0, 1.0, 0.0) for i in index]
    not_last = [jnp.where(i < rows - 1, 1.0, 0.0) for i in index]
    return not_first, not_last


def rim_kernel(rows, tiles, edge, depth, *refs):
    column_refs, (message_ref, far_ref, flow_ref, first_ref) = refs[:rows], refs[rows:]
    patterns = message_ref.shape[1]
    span = tiles * edge
    not_first, not_last = row_masks(rows)
    start = [ref[span : 2 * span] for ref in column_refs]
    folds = [ref[2 * span : 2 * span + depth] for ref in column_refs]
    base = 2 * span + depth
    gains = jnp.concatenate([ref[base : base + 1] for ref in column_refs], axis=0)
    columns = turned(gains)
    first = sum(ref[base + 1 : base + 2] for ref in column_refs)
    south = [
        columns[span : 2 * span, k : k + 1] * (start[k] - start[(k + 1) % rows] * not_last[k])
        for k in range(rows)
    ]
    dropped = jnp.zeros((span, patterns), jnp.float32)
    stride = span + depth
    for k in range(rows):
        flow = south[k] - south[k - 1] * not_first[k]
        raw = column_refs[k][:span]
        rim = raw - dot3(corners(folds[k], tiles, edge), flow)
        dropped = dropped + flow * (raw + rim)
        message_ref[k * stride : k * stride + span] = rim
        message_ref[k * stride + span : (k + 1) * stride] = folds[k]
        far_ref[k * edge : (k + 1) * edge] = rim[:edge]
        if k == 0:
            flow_ref[...] = flow
    message_ref[rows * stride : rows * stride + rows] = gains
    if message_ref.shape[0] > rows * stride + rows:
        rest_rows = message_ref.shape[0] - rows * stride - rows
        message_ref[rows * stride + rows :] = jnp.zeros((rest_rows, patterns), jnp.float32)
    first = first - jnp.sum(dropped, axis=0, keepdims=True)
    first_ref[...] = jnp.broadcast_to(first, first_ref.shape)


def moment_kernel(
    rows,
    cols,
    tiles,
    edge,
    depth,
    own_ref,
    inner_ref,
    outer_ref,
    far_ref,
    first_ref,
    moment_ref,
    t0_ref,
    t1_ref,
):
    patterns = own_ref.shape[1]
    mine = lax.axis_index("col")
    odd = mine % 2 == 1
    has_west = jnp.where(mine > 0, 1.0, 0.0)
    has_east = jnp.where(mine < cols - 1, 1.0, 0.0)
    has_far = jnp.where(mine < cols - 2, 1.0, 0.0)
    not_first, not_last = row_masks(rows)
    span = tiles * edge
    stride = span + depth

    def sides(piece):
        west = jnp.where(odd, inner_ref[piece], outer_ref[piece]) * has_west
        east = jnp.where(odd, outer_ref[piece], inner_ref[piece]) * has_east
        return west, own_ref[piece], east

    gains = [turned(block) for block in sides(slice(rows * stride, None))]
    easts, souths, u0, mats = [], [], [], []
    for k in range(rows):
        blocks = sides(slice(k * stride, (k + 1) * stride))
        far = far_ref[k * edge : (k + 1) * edge] * has_far
        u0.append(
            [block[t * edge : (t + 1) * edge] for block in blocks for t in range(tiles)] + [far]
        )

        def gain(columns, base):
            return jnp.broadcast_to(columns[base : base + edge, k : k + 1], (edge, patterns))

        easts.append([gain(g, t * edge) for g in gains for t in range(tiles)])
        souths.append([gain(g, span + t * edge) for g in gains for t in range(tiles)])
        mats.append([corners(block[span:], tiles, edge) for block in blocks])

    def net_flow(rims, low, high):
        flows = []
        for k in range(rows):
            below, above = (k + 1) % rows, k - 1
            row = []
            for c in range(low, high):
                flow = easts[k][c] * (rims[k][c] - rims[k][c + 1])
                flow = flow - easts[k][c - 1] * (rims[k][c - 1] - rims[k][c])
                flow = flow + souths[k][c] * (rims[k][c] - rims[below][c] * not_last[k])
                back = souths[above][c] * (rims[k][c] - rims[above][c])
                row.append(flow + back * not_first[k])
            flows.append([None] * low + row)
        return flows

    def spread(flows, devices, low, high):
        out = []
        for k in range(rows):
            row = []
            for d in devices:
                block = [
                    flows[k][c] if low <= c < high else jnp.zeros((edge, patterns), jnp.float32)
                    for c in range(d * tiles, (d + 1) * tiles)
                ]
                block = dot3(mats[k][d], jnp.concatenate(block, axis=0))
                row += [block[t * edge : (t + 1) * edge] for t in range(tiles)]
            out.append([None] * (devices[0] * tiles) + row)
        return out

    t0 = net_flow(u0, tiles - 1, 3 * tiles)
    u1 = spread(t0, [0, 1, 2], tiles - 1, 3 * tiles)
    t1 = net_flow(u1, tiles, 2 * tiles + 1)
    u2 = spread(t1, [1, 2], tiles, 2 * tiles + 1)
    zero = jnp.zeros((edge, patterns), jnp.float32)
    sums = [zero] * 5
    for k in range(rows):
        for c in range(tiles, 2 * tiles):
            ahead = u2[k][c] - u2[k][c + 1]
            drop = u2[k][c] - u2[(k + 1) % rows][c] * not_last[k]
            parts = (
                u0[k][c] * t0[k][c],
                u1[k][c] * t0[k][c],
                u1[k][c] * t1[k][c],
                u2[k][c] * t1[k][c],
                easts[k][c] * ahead * ahead + souths[k][c] * drop * drop,
            )
            sums = [total + part for total, part in zip(sums, parts)]
    moment_ref[0:1] = first_ref[0:1]
    for i, total in enumerate(sums):
        moment_ref[i + 1 : i + 2] = jnp.sum(total, axis=0, keepdims=True)
    moment_ref[6:8] = jnp.zeros((2, patterns), jnp.float32)
    t0_ref[...] = jnp.concatenate(t0[0][tiles : 2 * tiles], axis=0)
    t1_ref[...] = jnp.concatenate(t1[0][tiles : 2 * tiles], axis=0)


def direction_kernel(edge, precond_ref, inverse_ref, flow_ref, t0_ref, t1_ref, *out_refs):
    for t in range(precond_ref.shape[0]):
        rim = slice(t * edge, (t + 1) * edge)
        flows = jnp.concatenate([flow_ref[rim], t0_ref[rim], t1_ref[rim]], axis=1)
        spread = dot(inverse_ref[t, :, :edge], flows)
        width = spread.shape[1] // 3
        out_refs[0][t] = precond_ref[t] - spread[:, :width]
        out_refs[1][t] = spread[:, width : 2 * width]
        out_refs[2][t] = spread[:, 2 * width :]


def final_kernel(volt_ref, z0_ref, z1_ref, z2_ref, *refs):
    *sum_refs, out_ref = refs
    tiles = volt_ref.shape[0]
    sums = sum(ref[...] for ref in sum_refs)
    m = [sums[i : i + 1] for i in range(6)]
    a00, a01, a02 = m[0] + m[1], m[1] + m[2], m[2] + m[3]
    a12, a22 = m[3] + m[4], m[4] + m[5]
    l1, l2 = a01 / a00, a02 / a00
    d1 = a02 - l1 * a01
    e12 = a12 - l2 * a01
    l12 = jnp.where(d1 > 0.0, e12 / d1, 0.0)
    d2 = a22 - l2 * a02 - l12 * e12
    y1 = m[1] - l1 * m[0]
    y2 = m[2] - l2 * m[0] - l12 * y1
    c2 = jnp.where(d2 > 0.0, y2 / d2, 0.0)
    c1 = jnp.where(d1 > 0.0, y1 / d1 - l12 * c2, 0.0)
    c0 = m[0] / a00 - l1 * c1 - l2 * c2
    for t in range(tiles):
        out_ref[t] = volt_ref[t] + c0 * z0_ref[t] + c1 * z1_ref[t] + c2 * z2_ref[t]


def other(block, axis, count, distance):
    return lax.ppermute(block, axis, [(i, i ^ distance) for i in range(count)])


def stages(count, held):
    while held < count:
        reach = 2 if (count // held).bit_length() % 2 == 0 else 4
        yield [held * k for k in range(1, reach)]
        held *= reach


def sum_stages(block, axis, count):
    held, terms = 2, [block]
    while held < count:
        block = sum(terms[1:], terms[0])
        if (count // held).bit_length() % 2 == 0:
            terms = [block, other(block, axis, count, held)]
            held *= 2
            continue
        route = [(i, i ^ (2 * held if i % 2 else held)) for i in range(count)]
        brought = lax.ppermute(block, axis, route)
        third = other(block, axis, count, 3 * held)
        brought, third = lax.optimization_barrier((brought, third))
        terms = [block, brought, third, other(brought, axis, count, 1)]
        held *= 4
    return terms


def outer_swap(block, axis, count):
    pairs = [(i, (i + 1) % count if i % 2 else (i - 1) % count) for i in range(count)]
    return lax.ppermute(block, axis, pairs)


def local(
    initial_voltage,
    inject,
    conduct,
    capacitance,
    track_gain,
    driver_tile,
    sink_net,
    sink_count,
    sink_tile,
    sink_node,
    sink_gain,
):
    rows, cols = lax.axis_size("row"), lax.axis_size("col")
    tiles, nodes, patterns = initial_voltage.shape[1:]
    edge, nets = track_gain.shape[-1], driver_tile.shape[-1]
    slots = cols * sink_net.shape[-1]
    voltage = initial_voltage[0]
    field = (tiles, nodes, patterns)
    span = tiles * edge

    mate = other(initial_voltage, "col", cols, 1)[0]
    mate_driver = other(driver_tile, "col", cols, 1)[0]
    mate_gain = other(track_gain, "col", cols, 1)[0]
    eye = run(eye_kernel, [(nodes, nodes)])[0]
    narrow_type = functools.partial(jax.ShapeDtypeStruct, dtype=jnp.bfloat16)
    rest, gains, take, put, scale, picked, held = run(
        functools.partial(sink_kernel, nets, edge),
        [
            field,
            (edge + 8, patterns),
            narrow_type((slots, cols * nets)),
            narrow_type((slots, tiles * nodes)),
            (slots, patterns),
            (nets, patterns),
            (tiles, nodes),
        ],
        eye,
        conduct[0],
        voltage,
        inject[0],
        track_gain[0],
        sink_net[0, 0],
        sink_count[0],
        sink_tile[0, 0],
        sink_node[0, 0],
        sink_gain[0, 0],
        driver_tile[0],
        capacitance[0],
    )
    pair = run(
        functools.partial(pair_kernel, nets, edge),
        [(2 * nets + edge + 8, patterns)],
        voltage,
        picked,
        mate,
        mate_driver,
        mate_gain,
    )[0]
    groups = [pair]
    for distances in stages(cols, 2):
        whole = groups[0] if len(groups) == 1 else jnp.concatenate(groups)
        groups = [whole] + [other(whole, "col", cols, d) for d in distances]
    depth = tiles * edge * edge // nodes
    inverse, fold, part, reach = run(
        functools.partial(tile_kernel, edge),
        [field, (depth, nodes), field, (tiles, nodes, slots)],
        eye,
        conduct[0],
        held,
        rest,
        put,
        pair,
        scratch=[pltpu.VMEM(field, jnp.float32)] * 2,
    )

    message, precond = run(
        functools.partial(residual_kernel, nets, edge, cols),
        [(2 * span + depth + 8, patterns), field],
        voltage,
        mate,
        mate_gain,
        inverse,
        fold,
        part,
        reach,
        rest,
        gains,
        take,
        put,
        scale,
        *groups,
    )

    column = [message] + [
        lax.ppermute(message, "row", [((i + k) % rows, i) for i in range(rows)])
        for k in range(1, rows)
    ]
    height = rows * (span + depth) + -(-rows // 8) * 8
    message, far, flow, first = run(
        functools.partial(rim_kernel, rows, tiles, edge, depth),
        [(height, patterns), (rows * edge, patterns), (span, patterns), (8, patterns)],
        *column,
    )

    inner = other(message, "col", cols, 1)
    beyond = outer_swap(message, "col", cols)
    far = lax.ppermute(far, "col", [((i + 2) % cols, i) for i in range(cols)])
    moments, t0, t1 = run(
        functools.partial(moment_kernel, rows, cols, tiles, edge, depth),
        [(8, patterns), (span, patterns), (span, patterns)],
        message,
        inner,
        beyond,
        far,
        first,
    )

    sums = sum_stages(moments + other(moments, "col", cols, 1), "col", cols)
    directions = run(
        functools.partial(direction_kernel, edge), [field] * 3, precond, inverse, flow, t0, t1
    )
    return run(final_kernel, [field], voltage, *directions, *sums)[0][None]


def solution(mesh):
    whole = P("row", "col", None, None)
    third = P("row", "col", None)
    placed = (whole, whole, whole, third, whole, third, whole, third, whole, whole, whole)
    return jax.shard_map(local, mesh=mesh, in_specs=placed, out_specs=whole, check_vma=False)
```

```python
import functools

import jax
import jax.numpy as jnp
from jax import lax
from jax.experimental import pallas as pl
from jax.experimental.pallas import tpu as pltpu
from jax.sharding import PartitionSpec as P

DOUBLINGS = 5
SMALL = 2.0**-13
VMEM_BYTES = 16 * 1024 * 1024

dot = functools.partial(
    jnp.dot, precision=lax.Precision.HIGHEST, preferred_element_type=jnp.float32
)


def split(block):
    high = block.astype(jnp.bfloat16)
    return high, (block - high.astype(jnp.float32)).astype(jnp.bfloat16)


def thirds(block):
    high = block.astype(jnp.bfloat16)
    middle, low = split(block - high.astype(jnp.float32))
    return low, middle, high


def narrow(left, right):
    return jnp.dot(left, right, preferred_element_type=jnp.float32)


def dot3(left, right):
    (left_high, left_low), (right_high, right_low) = split(left), split(right)
    return narrow(left_high, right_high) + (
        narrow(left_high, right_low) + narrow(left_low, right_high)
    )


def select(onehot, block):
    high = block.astype(jnp.bfloat16)
    rest = block - high.astype(jnp.float32)
    middle, low = split(rest)
    return narrow(onehot, high) + (narrow(onehot, middle) + narrow(onehot, low))


def run(kernel, outs, *args, scratch=(), flops=4_000_000_000):
    vmem = pl.BlockSpec(memory_space=pltpu.VMEM)
    shapes = tuple(
        o if isinstance(o, jax.ShapeDtypeStruct) else jax.ShapeDtypeStruct(o, jnp.float32)
        for o in outs
    )
    moved = sum(4 * a.size for a in args) + sum(4 * s.size for s in shapes)
    return pl.pallas_call(
        kernel,
        out_shape=shapes,
        in_specs=[vmem] * len(args),
        out_specs=(vmem,) * len(shapes),
        scratch_shapes=list(scratch),
        compiler_params=pltpu.CompilerParams(vmem_limit_bytes=VMEM_BYTES),
        cost_estimate=pl.CostEstimate(flops=flops, bytes_accessed=moved, transcendentals=0),
    )(*args)


def iota(shape, axis):
    return lax.broadcasted_iota(jnp.int32, shape, axis)


def to_column(row):
    count = row.shape[1]
    square = jnp.broadcast_to(row, (count, count))
    keep = iota((count, count), 0) == iota((count, count), 1)
    return jnp.sum(jnp.where(keep, square, 0.0), axis=1, keepdims=True)


def slot_column(table):
    sources, slots = table.shape
    spread = jnp.concatenate(
        [jnp.broadcast_to(table[s : s + 1], (slots, slots)) for s in range(sources)], axis=0
    )
    keep = iota(spread.shape, 0) % slots == iota(spread.shape, 1)
    return jnp.sum(jnp.where(keep, spread, 0.0), axis=1, keepdims=True)


def source_column(row, slots):
    sources = row.shape[1]
    spread = jnp.broadcast_to(row, (sources * slots, sources))
    keep = iota(spread.shape, 0) // slots == iota(spread.shape, 1)
    return jnp.sum(jnp.where(keep, spread, 0.0), axis=1, keepdims=True)


def pair_kernel(nets, edge, volt_ref, picked_ref, mate_ref, mate_driver_ref, mate_gain_ref, out_ref):
    tiles, nodes, patterns = volt_ref.shape
    odd = lax.axis_index("col") % 2 == 1
    mate_picked = to_column(mate_driver_ref[...].astype(jnp.float32))
    for i, (field, picked) in enumerate(((volt_ref, picked_ref[...]), (mate_ref, mate_picked))):
        rows = jnp.zeros((nets, patterns), jnp.float32)
        for t in range(tiles):
            block = jnp.concatenate([field[t]] * (-(-nets // nodes)), axis=0)[:nets]
            rows = jnp.where(picked == t, block, rows)
        out_ref[i * nets : (i + 1) * nets] = rows
    base = 2 * nets
    out_ref[base : base + edge] = jnp.where(odd, mate_ref[0, :edge], mate_ref[tiles - 1, :edge])
    out_ref[base + edge :] = jnp.zeros((8, patterns), jnp.float32)
    out_ref[base + edge : base + edge + 1, :edge] = mate_gain_ref[tiles - 1, 0:1]


def eye_kernel(out_ref):
    out_ref[...] = jnp.where(iota(out_ref.shape, 0) == iota(out_ref.shape, 1), 1.0, 0.0)


def sink_kernel(
    nets,
    edge,
    eye_ref,
    conduct_ref,
    volt_ref,
    inject_ref,
    gain_ref,
    net_ref,
    count_ref,
    tile_ref,
    node_ref,
    weight_ref,
    driver_ref,
    rest_ref,
    gains_ref,
    take_ref,
    put_ref,
    scale_ref,
    picked_ref,
):
    picked_ref[...] = jnp.broadcast_to(
        to_column(driver_ref[...].astype(jnp.float32)), picked_ref.shape
    )
    tiles, nodes = conduct_ref.shape[0], conduct_ref.shape[1]
    for t in range(tiles):
        rest_ref[t] = inject_ref[t] - dot(conduct_ref[t], volt_ref[t])
    lane = iota((edge, nodes), 1)
    table = jnp.zeros((edge, nodes), jnp.float32)
    gains_ref[edge:] = jnp.zeros((8, nodes), jnp.float32)
    for side in range(2):
        for t in range(tiles):
            i = side * tiles + t
            gain = gain_ref[t, side : side + 1]
            table = jnp.where(lane == i, to_column(gain), table)
            gains_ref[edge : edge + 1, i * edge : (i + 1) * edge] = gain
    gains_ref[:edge] = table

    sources, slots = net_ref.shape
    mine = lax.axis_index("col")
    block = iota((sources, slots), 0) ^ mine
    place = slot_column((block * nets + net_ref[...]).astype(jnp.float32))
    target = slot_column((tile_ref[...] * nodes + node_ref[...]).astype(jnp.float32))
    live = source_column(count_ref[...].astype(jnp.float32), slots)
    slot = (iota(live.shape, 0) % slots).astype(jnp.float32)
    weight = jnp.where(slot < live, slot_column(weight_ref[...]), 0.0)
    take = jnp.where(place == iota(take_ref.shape, 1).astype(jnp.float32), 1.0, 0.0)
    put = jnp.where(target == iota(put_ref.shape, 1).astype(jnp.float32), 1.0, 0.0)
    take_ref[...] = take.astype(jnp.bfloat16)
    put_ref[...] = put.astype(jnp.bfloat16)
    scale_ref[...] = jnp.broadcast_to(weight, scale_ref.shape)


def tile_kernel(
    edge,
    eye_ref,
    conduct_ref,
    cap_ref,
    rest_ref,
    put_ref,
    after_ref,
    inverse_ref,
    fold_ref,
    part_ref,
    reach_ref,
    sum_ref,
    power_ref,
):
    tiles, nodes = conduct_ref.shape[0], conduct_ref.shape[1]
    eye = eye_ref[...]
    sums, powers, scales = [], [], []
    for t in range(tiles):
        conduct = conduct_ref[t]
        diagonal = (conduct + cap_ref[t : t + 1, :]) * eye
        down = jnp.sum(diagonal, axis=1, keepdims=True)
        across = jnp.sum(diagonal, axis=0, keepdims=True)
        power = (conduct * eye - conduct) / down
        sums.append(eye + power)
        powers.append(dot(power, power))
        scales.append(1.0 / across)

    def step(sums, powers):
        out_sums, out_powers, largest = [], [], jnp.float32(0.0)
        for total, power in zip(sums, powers):
            both = dot(jnp.concatenate([total, power], axis=0), power)
            out_sums.append(total + both[:nodes])
            out_powers.append(both[nodes:])
            largest = jnp.maximum(largest, jnp.max(jnp.sum(power, axis=1)))
        return out_sums, out_powers, largest

    for _ in range(DOUBLINGS):
        sums, powers, largest = step(sums, powers)
    for t in range(tiles):
        sum_ref[t], power_ref[t] = sums[t], powers[t]

    def again(carry):
        sums, powers, largest = step(
            [sum_ref[t] for t in range(tiles)], [power_ref[t] for t in range(tiles)]
        )
        for t in range(tiles):
            sum_ref[t], power_ref[t] = sums[t], powers[t]
        return largest, carry[1] + 1

    lax.while_loop(
        lambda carry: (carry[0] > SMALL) & (carry[1] < 40), again, (largest, jnp.int32(0))
    )
    parts = nodes // edge
    depth = edge // parts
    lane = iota((depth, nodes), 1)
    for t in range(tiles):
        inverse = sum_ref[t] * scales[t]
        inverse_ref[t] = inverse
        fold = jnp.zeros((depth, nodes), jnp.float32)
        for j in range(parts):
            piece = jnp.where(lane < edge, inverse[j * depth : (j + 1) * depth], 0.0)
            fold = fold + (pltpu.roll(piece, j * edge, 1) if j else piece)
        fold_ref[t * depth : (t + 1) * depth] = fold
        part_ref[t] = dot(inverse, rest_ref[t])
        put = put_ref[:, t * nodes : (t + 1) * nodes]
        reach_ref[t] = sum(
            lax.dot_general(
                piece, put, (((1,), (1,)), ((), ())), preferred_element_type=jnp.float32
            )
            for piece in thirds(inverse)
        )


def residual_kernel(
    nets,
    edge,
    cols,
    volt_ref,
    mate_ref,
    mate_gain_ref,
    inverse_ref,
    fold_ref,
    part_ref,
    reach_ref,
    rest_ref,
    gains_ref,
    take_ref,
    put_ref,
    scale_ref,
    *refs,
):
    *group_refs, message_ref, precond_ref = refs
    tiles, nodes, patterns = volt_ref.shape
    mine = lax.axis_index("col")
    odd = mine % 2 == 1
    stride = 2 * nets + edge + 8
    blocks = [(ref, base) for ref in group_refs for base in range(0, ref.shape[0], stride)]
    values = sum(
        select(take_ref[:, j * 2 * nets : (j + 1) * 2 * nets], ref[base : base + 2 * nets])
        for j, (ref, base) in enumerate(blocks)
    )
    values = values * scale_ref[...]
    beyond = lax.rem(jnp.where(odd, mine + 1, mine + cols - 1), cols) ^ 1
    which = (mine ^ beyond) // 2
    outer = jnp.zeros((edge + 8, patterns), jnp.float32)
    for j, (ref, base) in enumerate(blocks):
        outer = jnp.where(which == j, ref[base + 2 * nets : base + stride], outer)
    inner = jnp.where(odd, mate_ref[tiles - 1, :edge], mate_ref[0, :edge])
    inner_gain = to_column(mate_gain_ref[tiles - 1, 0:1])
    has_west = jnp.where(mine > 0, 1.0, 0.0)
    has_east = jnp.where(mine < cols - 1, 1.0, 0.0)
    west = jnp.where(odd, inner, outer[:edge]) * has_west
    east = jnp.where(odd, outer[:edge], inner) * has_east
    west_gain = jnp.where(odd, inner_gain, to_column(outer[edge : edge + 1, :edge])) * has_west
    gains = [west_gain] + [gains_ref[:edge, t : t + 1] for t in range(tiles)]
    rims = [west] + [volt_ref[t, :edge] for t in range(tiles)] + [east]
    flows = [gains[t] * (rims[t] - rims[t + 1]) for t in range(tiles + 1)]
    first = jnp.zeros((1, patterns), jnp.float32)
    high, low = split(values)
    for t in range(tiles):
        out = flows[t + 1] - flows[t]
        precond = part_ref[t] + (
            dot3(reach_ref[t], values) - dot3(inverse_ref[t, :, :edge], out)
        )
        put = put_ref[:, t * nodes : (t + 1) * nodes]
        injected = sum(
            lax.dot_general(
                put, part, (((0,), (0,)), ((), ())), preferred_element_type=jnp.float32
            )
            for part in (high, low)
        )
        residual = rest_ref[t] + injected
        residual = jnp.concatenate([residual[:edge] - out, residual[edge:]], axis=0)
        precond_ref[t] = precond
        first = first + jnp.sum(residual * precond, axis=0, keepdims=True)
        message_ref[t * edge : (t + 1) * edge] = precond[:edge]
        message_ref[(tiles + t) * edge : (tiles + t + 1) * edge] = volt_ref[t, :edge]
    base = 2 * tiles * edge
    depth = fold_ref.shape[0]
    message_ref[base : base + depth] = fold_ref[...]
    message_ref[base + depth : base + depth + 8] = gains_ref[edge:]
    message_ref[base + depth + 1 : base + depth + 2] = first


def corners(fold, tiles, edge):
    depth, lanes = fold.shape[0] // tiles, fold.shape[1]
    lane = iota((depth, lanes), 1)
    rows = []
    for t in range(tiles):
        piece = fold[t * depth : (t + 1) * depth]
        for j in range(lanes // edge):
            turn = (t - j) * edge % lanes
            turned = pltpu.roll(piece, turn, 1) if turn else piece
            rows.append(jnp.where((lane >= t * edge) & (lane < (t + 1) * edge), turned, 0.0))
    return jnp.concatenate(rows, axis=0)[:, : tiles * edge]


def turned(rows):
    count, lanes = rows.shape
    full = jnp.concatenate([rows, jnp.zeros((lanes - count, lanes), jnp.float32)], axis=0)
    return jnp.transpose(full)


def row_masks(rows):
    place = lax.axis_index("row")
    index = [lax.rem(place + k, rows) for k in range(rows)]
    not_first = [jnp.where(i > 0, 1.0, 0.0) for i in index]
    not_last = [jnp.where(i < rows - 1, 1.0, 0.0) for i in index]
    return not_first, not_last


def rim_kernel(rows, tiles, edge, depth, *refs):
    column_refs, (message_ref, far_ref, flow_ref, first_ref) = refs[:rows], refs[rows:]
    patterns = message_ref.shape[1]
    span = tiles * edge
    not_first, not_last = row_masks(rows)
    start = [ref[span : 2 * span] for ref in column_refs]
    folds = [ref[2 * span : 2 * span + depth] for ref in column_refs]
    base = 2 * span + depth
    gains = jnp.concatenate([ref[base : base + 1] for ref in column_refs], axis=0)
    columns = turned(gains)
    first = sum(ref[base + 1 : base + 2] for ref in column_refs)
    south = [
        columns[span : 2 * span, k : k + 1] * (start[k] - start[(k + 1) % rows] * not_last[k])
        for k in range(rows)
    ]
    dropped = jnp.zeros((span, patterns), jnp.float32)
    stride = span + depth
    for k in range(rows):
        flow = south[k] - south[k - 1] * not_first[k]
        raw = column_refs[k][:span]
        rim = raw - dot3(corners(folds[k], tiles, edge), flow)
        dropped = dropped + flow * (raw + rim)
        message_ref[k * stride : k * stride + span] = rim
        message_ref[k * stride + span : (k + 1) * stride] = folds[k]
        far_ref[k * edge : (k + 1) * edge] = rim[:edge]
        if k == 0:
            flow_ref[...] = flow
    message_ref[rows * stride : rows * stride + rows] = gains
    if message_ref.shape[0] > rows * stride + rows:
        rest_rows = message_ref.shape[0] - rows * stride - rows
        message_ref[rows * stride + rows :] = jnp.zeros((rest_rows, patterns), jnp.float32)
    first = first - jnp.sum(dropped, axis=0, keepdims=True)
    first_ref[...] = jnp.broadcast_to(first, first_ref.shape)


def moment_kernel(
    rows,
    cols,
    tiles,
    edge,
    depth,
    own_ref,
    inner_ref,
    outer_ref,
    far_ref,
    first_ref,
    moment_ref,
    t0_ref,
    t1_ref,
):
    patterns = own_ref.shape[1]
    mine = lax.axis_index("col")
    odd = mine % 2 == 1
    has_west = jnp.where(mine > 0, 1.0, 0.0)
    has_east = jnp.where(mine < cols - 1, 1.0, 0.0)
    has_far = jnp.where(mine < cols - 2, 1.0, 0.0)
    not_first, not_last = row_masks(rows)
    span = tiles * edge
    stride = span + depth

    def sides(piece):
        west = jnp.where(odd, inner_ref[piece], outer_ref[piece]) * has_west
        east = jnp.where(odd, outer_ref[piece], inner_ref[piece]) * has_east
        return west, own_ref[piece], east

    gains = [turned(block) for block in sides(slice(rows * stride, None))]
    easts, souths, u0, mats = [], [], [], []
    for k in range(rows):
        blocks = sides(slice(k * stride, (k + 1) * stride))
        far = far_ref[k * edge : (k + 1) * edge] * has_far
        u0.append(
            [block[t * edge : (t + 1) * edge] for block in blocks for t in range(tiles)] + [far]
        )

        def gain(columns, base):
            return jnp.broadcast_to(columns[base : base + edge, k : k + 1], (edge, patterns))

        easts.append([gain(g, t * edge) for g in gains for t in range(tiles)])
        souths.append([gain(g, span + t * edge) for g in gains for t in range(tiles)])
        mats.append([corners(block[span:], tiles, edge) for block in blocks])

    def net_flow(rims, low, high):
        flows = []
        for k in range(rows):
            below, above = (k + 1) % rows, k - 1
            row = []
            for c in range(low, high):
                flow = easts[k][c] * (rims[k][c] - rims[k][c + 1])
                flow = flow - easts[k][c - 1] * (rims[k][c - 1] - rims[k][c])
                flow = flow + souths[k][c] * (rims[k][c] - rims[below][c] * not_last[k])
                back = souths[above][c] * (rims[k][c] - rims[above][c])
                row.append(flow + back * not_first[k])
            flows.append([None] * low + row)
        return flows

    def spread(flows, devices, low, high):
        out = []
        for k in range(rows):
            row = []
            for d in devices:
                inside = range(d * tiles, (d + 1) * tiles)
                block = [
                    flows[k][c] if low <= c < high else jnp.zeros((edge, patterns), jnp.float32)
                    for c in inside
                ]
                used = [c - d * tiles for c in inside if low <= c < high]
                place = slice(used[0] * edge, (used[-1] + 1) * edge)
                block = dot3(mats[k][d][place], jnp.concatenate(block, axis=0))
                found = [block[i * edge : (i + 1) * edge] for i in range(len(used))]
                row += [None] * used[0] + found + [None] * (tiles - 1 - used[-1])
            out.append([None] * (devices[0] * tiles) + row)
        return out

    t0 = net_flow(u0, tiles - 1, 3 * tiles)
    u1 = spread(t0, [0, 1, 2], tiles - 1, 3 * tiles)
    t1 = net_flow(u1, tiles, 2 * tiles + 1)
    u2 = spread(t1, [1, 2], tiles, 2 * tiles + 1)
    zero = jnp.zeros((edge, patterns), jnp.float32)
    sums = [zero] * 5
    for k in range(rows):
        for c in range(tiles, 2 * tiles):
            ahead = u2[k][c] - u2[k][c + 1]
            drop = u2[k][c] - u2[(k + 1) % rows][c] * not_last[k]
            parts = (
                u0[k][c] * t0[k][c],
                u1[k][c] * t0[k][c],
                u1[k][c] * t1[k][c],
                u2[k][c] * t1[k][c],
                easts[k][c] * ahead * ahead + souths[k][c] * drop * drop,
            )
            sums = [total + part for total, part in zip(sums, parts)]
    moment_ref[0:1] = first_ref[0:1]
    for i, total in enumerate(sums):
        moment_ref[i + 1 : i + 2] = jnp.sum(total, axis=0, keepdims=True)
    moment_ref[6:8] = jnp.zeros((2, patterns), jnp.float32)
    t0_ref[...] = jnp.concatenate(t0[0][tiles : 2 * tiles], axis=0)
    t1_ref[...] = jnp.concatenate(t1[0][tiles : 2 * tiles], axis=0)


def direction_kernel(edge, precond_ref, inverse_ref, flow_ref, t0_ref, t1_ref, *out_refs):
    for t in range(precond_ref.shape[0]):
        rim = slice(t * edge, (t + 1) * edge)
        flows = jnp.concatenate([flow_ref[rim], t0_ref[rim], t1_ref[rim]], axis=1)
        spread = dot(inverse_ref[t, :, :edge], flows)
        width = spread.shape[1] // 3
        out_refs[0][t] = precond_ref[t] - spread[:, :width]
        out_refs[1][t] = spread[:, width : 2 * width]
        out_refs[2][t] = spread[:, 2 * width :]


def final_kernel(volt_ref, z0_ref, z1_ref, z2_ref, *refs):
    *sum_refs, out_ref = refs
    tiles = volt_ref.shape[0]
    sums = sum(ref[...] for ref in sum_refs)
    m = [sums[i : i + 1] for i in range(6)]
    a00, a01, a02 = m[0] + m[1], m[1] + m[2], m[2] + m[3]
    a12, a22 = m[3] + m[4], m[4] + m[5]
    l1, l2 = a01 / a00, a02 / a00
    d1 = a02 - l1 * a01
    e12 = a12 - l2 * a01
    l12 = jnp.where(d1 > 0.0, e12 / d1, 0.0)
    d2 = a22 - l2 * a02 - l12 * e12
    y1 = m[1] - l1 * m[0]
    y2 = m[2] - l2 * m[0] - l12 * y1
    c2 = jnp.where(d2 > 0.0, y2 / d2, 0.0)
    c1 = jnp.where(d1 > 0.0, y1 / d1 - l12 * c2, 0.0)
    c0 = m[0] / a00 - l1 * c1 - l2 * c2
    for t in range(tiles):
        out_ref[t] = volt_ref[t] + c0 * z0_ref[t] + c1 * z1_ref[t] + c2 * z2_ref[t]


def other(block, axis, count, distance):
    return lax.ppermute(block, axis, [(i, i ^ distance) for i in range(count)])


def stages(count, held):
    while held < count:
        reach = 2 if (count // held).bit_length() % 2 == 0 else 4
        yield [held * k for k in range(1, reach)]
        held *= reach


def sum_stages(block, axis, count):
    held, terms = 2, [block]
    while held < count:
        block = sum(terms[1:], terms[0])
        if (count // held).bit_length() % 2 == 0:
            terms = [block, other(block, axis, count, held)]
            held *= 2
            continue
        route = [(i, i ^ (2 * held if i % 2 else held)) for i in range(count)]
        brought = lax.ppermute(block, axis, route)
        third = other(block, axis, count, 3 * held)
        brought, third = lax.optimization_barrier((brought, third))
        terms = [block, brought, third, other(brought, axis, count, 1)]
        held *= 4
    return terms


def outer_swap(block, axis, count):
    pairs = [(i, (i + 1) % count if i % 2 else (i - 1) % count) for i in range(count)]
    return lax.ppermute(block, axis, pairs)


def local(
    initial_voltage,
    inject,
    conduct,
    capacitance,
    track_gain,
    driver_tile,
    sink_net,
    sink_count,
    sink_tile,
    sink_node,
    sink_gain,
):
    rows, cols = lax.axis_size("row"), lax.axis_size("col")
    tiles, nodes, patterns = initial_voltage.shape[1:]
    edge, nets = track_gain.shape[-1], driver_tile.shape[-1]
    slots = cols * sink_net.shape[-1]
    voltage = initial_voltage[0]
    field = (tiles, nodes, patterns)
    span = tiles * edge

    mate = other(initial_voltage, "col", cols, 1)[0]
    mate_driver = other(driver_tile, "col", cols, 1)[0]
    mate_gain = other(track_gain, "col", cols, 1)[0]
    eye = run(eye_kernel, [(nodes, nodes)])[0]
    narrow_type = functools.partial(jax.ShapeDtypeStruct, dtype=jnp.bfloat16)
    rest, gains, take, put, scale, picked = run(
        functools.partial(sink_kernel, nets, edge),
        [
            field,
            (edge + 8, patterns),
            narrow_type((slots, cols * nets)),
            narrow_type((slots, tiles * nodes)),
            (slots, patterns),
            (nets, patterns),
        ],
        eye,
        conduct[0],
        voltage,
        inject[0],
        track_gain[0],
        sink_net[0, 0],
        sink_count[0],
        sink_tile[0, 0],
        sink_node[0, 0],
        sink_gain[0, 0],
        driver_tile[0],
    )
    pair = run(
        functools.partial(pair_kernel, nets, edge),
        [(2 * nets + edge + 8, patterns)],
        voltage,
        picked,
        mate,
        mate_driver,
        mate_gain,
    )[0]
    groups = [pair]
    for distances in stages(cols, 2):
        whole = groups[0] if len(groups) == 1 else jnp.concatenate(groups)
        groups = [whole] + [other(whole, "col", cols, d) for d in distances]
    depth = tiles * edge * edge // nodes
    inverse, fold, part, reach = run(
        functools.partial(tile_kernel, edge),
        [field, (depth, nodes), field, (tiles, nodes, slots)],
        eye,
        conduct[0],
        capacitance[0],
        rest,
        put,
        pair,
        scratch=[pltpu.VMEM(field, jnp.float32)] * 2,
    )

    message, precond = run(
        functools.partial(residual_kernel, nets, edge, cols),
        [(2 * span + depth + 8, patterns), field],
        voltage,
        mate,
        mate_gain,
        inverse,
        fold,
        part,
        reach,
        rest,
        gains,
        take,
        put,
        scale,
        *groups,
    )

    column = [message] + [
        lax.ppermute(message, "row", [((i + k) % rows, i) for i in range(rows)])
        for k in range(1, rows)
    ]
    height = rows * (span + depth) + -(-rows // 8) * 8
    message, far, flow, first = run(
        functools.partial(rim_kernel, rows, tiles, edge, depth),
        [(height, patterns), (rows * edge, patterns), (span, patterns), (8, patterns)],
        *column,
    )

    inner = other(message, "col", cols, 1)
    beyond = outer_swap(message, "col", cols)
    far = lax.ppermute(far, "col", [((i + 2) % cols, i) for i in range(cols)])
    moments, t0, t1 = run(
        functools.partial(moment_kernel, rows, cols, tiles, edge, depth),
        [(8, patterns), (span, patterns), (span, patterns)],
        message,
        inner,
        beyond,
        far,
        first,
    )

    sums = sum_stages(moments + other(moments, "col", cols, 1), "col", cols)
    directions = run(
        functools.partial(direction_kernel, edge), [field] * 3, precond, inverse, flow, t0, t1
    )
    return run(final_kernel, [field], voltage, *directions, *sums)[0][None]


def solution(mesh):
    whole = P("row", "col", None, None)
    third = P("row", "col", None)
    placed = (whole, whole, whole, third, whole, third, whole, third, whole, whole, whole)
    return jax.shard_map(local, mesh=mesh, in_specs=placed, out_specs=whole, check_vma=False)
```
